32 devices in a mesh: dp: 4 (over x, core), fsdp: 8 (over z, y).
Axes of the slice: x: 2, y: 2, z: 4, core: 2. Of those that a mesh axis runs over, the one named last changes fastest.
Arguments:
- tokens: bfloat16 [32, 512, 768], P(('dp', 'fsdp'))
- segment_ids: int32 [32, 512], P(('dp', 'fsdp')), may hold values from 0 to 5, never falling along the last dimension, each value on 1 to 256 neighbouring positions
- cotangent: bfloat16 [32, 512, 768], P(('dp', 'fsdp')), may hold values from -6 to 6
- attention_weight: float32 [4, 768, 768], P(None, 'fsdp')
- attention_first: float32 [4, 768, 768], P(None, 'fsdp'), may hold values from -0.00061035156 to 0.00061035156
- attention_second: float32 [4, 768, 768], P(None, 'fsdp'), may hold values from 9.877095e-11 to 8.466082e-10
- inner_weight: float32 [768, 3072], P('fsdp'), may hold values from -0.21875 to 0.21875
- inner_first: float32 [768, 3072], P('fsdp'), may hold values from -0.00061035156 to 0.00061035156
- inner_second: float32 [768, 3072], P('fsdp'), may hold values from 1.2699122e-11 to 5.079649e-11
- outer_weight: float32 [3072, 768], P('fsdp'), may hold values from -0.109375 to 0.109375
- outer_first: float32 [3072, 768], P('fsdp'), may hold values from -0.00061035156 to 0.00061035156
- outer_second: float32 [3072, 768], P('fsdp'), may hold values from 9.877095e-11 to 8.466082e-10
- vectors: float32 [12, 768], P(None, 'fsdp')
- vector_first: float32 [12, 768], P(None, 'fsdp'), may hold values from -0.00061035156 to 0.00061035156
- vector_second: float32 [12, 768], P(None, 'fsdp'), may hold values from 9.877095e-11 to 8.466082e-10
Outputs:
- activations: bfloat16 [32, 512, 768], P(('dp', 'fsdp'))
- input_grad: float32 [32, 512, 768], P(('dp', 'fsdp'))
- grad_norm: float32 [], replicated
- attention_new: float32 [4, 768, 768], P(None, 'fsdp')
- attention_first_new: float32 [4, 768, 768], P(None, 'fsdp')
- attention_second_new: float32 [4, 768, 768], P(None, 'fsdp')
- inner_new: float32 [768, 3072], P('fsdp')
- inner_first_new: float32 [768, 3072], P('fsdp')
- inner_second_new: float32 [768, 3072], P('fsdp')
- outer_new: float32 [3072, 768], P('fsdp')
- outer_first_new: float32 [3072, 768], P('fsdp')
- outer_second_new: float32 [3072, 768], P('fsdp')
- vectors_new: float32 [12, 768], P(None, 'fsdp')
- vector_first_new: float32 [12, 768], P(None, 'fsdp')
- vector_second_new: float32 [12, 768], P(None, 'fsdp')
- vector_grad: float32 [12, 768], P(None, 'fsdp')
The draws below stay inside these ranges and needn't reach their ends.
Inputs may be any that keep to these rules, and one draw needn't show every extreme that they name: `segment_ids`: within a row the ids never fall; a run of one id holds at most 256 positions, and some run of each row holds exactly that many.
All inputs are finite; a program needn't handle non-finite values.
Results may differ from the reference program's by a relative error of at most 0.022.
Values may be sent and summed in bfloat16 or wider, within the bound.
A program may use at most 192 MiB of HBM per device.

```python
import math
import jax
import jax.numpy as jnp
import numpy as np
from jax import lax

D = 768
HEADS = 12
HD = 64
FF = 3072
SEQ = 512
STEP = 10
ROWS = 32


def draw_tokens(key, part):
    key = jax.random.fold_in(key, 11)
    column = jnp.arange(D, dtype=jnp.float32)
    ramp = 1.0 + 2.0 * column / (D - 1)
    base = jax.random.normal(key, (ROWS, SEQ, D), jnp.float32)
    return (base * ramp).astype(jnp.bfloat16)


def draw_attention_weight(key, part):
    key = jax.random.fold_in(key, 23)
    scales = jnp.array([0.7, 0.7, 1.0, 4.0], jnp.float32) * D ** (-0.5)
    base = jax.random.normal(key, (4, D, D), jnp.float32)
    return base * scales[:, None, None]


def draw_vectors(key, part):
    key = jax.random.fold_in(key, 37)
    noise_key, gain_key = jax.random.split(key)
    column = jnp.arange(D, dtype=jnp.float32)
    noise = 0.3 * jax.random.normal(noise_key, (12, D), jnp.float32)
    ramp = 1.0 + 2.0 * column / (D - 1)
    jitter = jnp.exp(jax.random.uniform(gain_key, (12, D), jnp.float32, -0.2, 0.2))
    gains = ramp[None, :] * jitter
    row_index = jnp.arange(12)[:, None]
    is_gain = (row_index == 3) | (row_index == 10)
    return jnp.where(is_gain, gains, noise)


def level_of(rng, shape, cuts, low, largest):
    loudness = 1.0
    for dim, parts in cuts:
        steps = jax.random.uniform(jax.random.fold_in(jax.random.fold_in(rng, 6), dim), (parts,), jnp.float32, low / len(cuts), largest / len(cuts))
        loudness = loudness * jnp.repeat(jnp.exp(steps), shape[dim] // parts).reshape((-1,) + (1,) * (len(shape) - 1 - dim))
    return loudness


def split_up(number_of, total, reach, skew):
    loads = [(1 << 20) // math.isqrt(grade ** skew) + 1 for grade in range(2, number_of + 1)]
    spare, holding = total - reach - (number_of - 1), [1] * (number_of - 1)
    while spare > 0:
        free = [i for i in range(number_of - 1) if holding[i] < reach]
        mass, remaining = sum([loads[i] for i in free]), spare
        for i in free:
            extra = min(reach - holding[i], max(1, remaining * loads[i] // mass), spare)
            holding[i] = holding[i] + extra
            spare = spare - extra
    return np.array([reach] + holding)


def ragged(own_key, number_of, total, limit, skew):
    if number_of == 2:
        one = jax.random.randint(own_key, (), max(1, total - limit), min(limit, total - 1) + 1)
        return jnp.stack([one, total - one])
    tallies = jnp.asarray(split_up(number_of, total, limit, skew), jnp.int32)
    pairs = (number_of - 1) // 2
    source_of, taker = tallies[1:1 + 2 * pairs:2], tallies[2:2 + 2 * pairs:2]
    margin = jnp.minimum(source_of - 1, limit - taker)
    shifted = jax.random.randint(jax.random.fold_in(own_key, 1), (pairs,), 0, 1 << 20) % (margin + 1)
    tallies = tallies.at[1:1 + 2 * pairs:2].set(source_of - shifted).at[2:2 + 2 * pairs:2].set(taker + shifted)
    return tallies[jax.random.permutation(jax.random.fold_in(own_key, 2), number_of)]


def bell_draw(own_key, extent, deviation, bound, cuts=(), kind=jnp.bfloat16):
    values = deviation * jax.random.normal(own_key, extent, jnp.float32)
    if cuts:
        values = values * level_of(own_key, extent, cuts, -0.22, 0.18)
    return jnp.clip(values, -bound, bound).astype(kind)


def setup_inputs(seed: int = 0) -> dict:
    seeds = jax.random.split(jax.random.key(seed), 16)
    return {
        "tokens": draw_tokens(jax.random.fold_in(seeds[15], 71), 0),
        "segment_ids": jax.vmap(lambda own: jnp.searchsorted(jnp.cumsum(ragged(own, 6, SEQ, SEQ // 2, 0)), jnp.arange(SEQ), side="right"))(jax.random.split(seeds[1], ROWS)).reshape((ROWS, SEQ)).astype(jnp.int32),
        "cotangent": bell_draw(seeds[2], (ROWS, SEQ, D), 1.0, 6.0, ((0, 32),)),
        "attention_weight": draw_attention_weight(jax.random.fold_in(seeds[15], 71), 0),
        "attention_first": bell_draw(seeds[4], (4, D, D), (0.11 * (4 * D * D + 2 * D * FF + 12 * D) ** -0.5), 0.00061035156, ((1, 8),), jnp.float32),
        "attention_second": jnp.clip(jnp.exp(math.log(8.466081724556318e-10) - 2.1484345 * jax.random.uniform(seeds[5], (4, D, D), jnp.float32) ** level_of(seeds[5], (4, D, D), ((1, 8),), -0.2, 0.2)), 9.877094975241363e-11, 8.466081724556318e-10),
        "inner_weight": bell_draw(seeds[6], (D, FF), D ** -0.5, 0.21875, ((0, 8),), jnp.float32),
        "inner_first": bell_draw(seeds[7], (D, FF), (0.11 * (4 * D * D + 2 * D * FF + 12 * D) ** -0.5), 0.00061035156, ((0, 8),), jnp.float32),
        "inner_second": jnp.clip(jnp.exp(math.log(5.079648854322549e-11) - 1.3862944 * jax.random.uniform(seeds[8], (D, FF), jnp.float32) ** level_of(seeds[8], (D, FF), ((0, 8),), -0.2, 0.2)), 1.2699122135806373e-11, 5.079648854322549e-11),
        "outer_weight": bell_draw(seeds[9], (FF, D), FF ** -0.5, 0.109375, ((0, 8),), jnp.float32),
        "outer_first": bell_draw(seeds[10], (FF, D), (0.11 * (4 * D * D + 2 * D * FF + 12 * D) ** -0.5), 0.00061035156, ((0, 8),), jnp.float32),
        "outer_second": jnp.clip(jnp.exp(math.log(8.466081724556318e-10) - 2.1484345 * jax.random.uniform(seeds[11], (FF, D), jnp.float32) ** level_of(seeds[11], (FF, D), ((0, 8),), -0.2, 0.2)), 9.877094975241363e-11, 8.466081724556318e-10),
        "vectors": draw_vectors(jax.random.fold_in(seeds[15], 71), 0),
        "vector_first": bell_draw(seeds[13], (12, D), (0.11 * (4 * D * D + 2 * D * FF + 12 * D) ** -0.5), 0.00061035156, ((1, 8),), jnp.float32),
        "vector_second": jnp.clip(jnp.exp(math.log(8.466081724556318e-10) - 2.1484345 * jax.random.uniform(seeds[14], (12, D), jnp.float32) ** level_of(seeds[14], (12, D), ((1, 8),), -0.2, 0.2)), 9.877094975241363e-11, 8.466081724556318e-10),
    }


EPS_NORM = 1e-12
BETA_ONE = 0.9
BETA_TWO = 0.999
ADAM_EPS = 1e-08
DECAY = 0.01
RATE_MATRIX = 0.03
RATE_VECTOR = 0.5
CLIP = 1.0
precise = lax.Precision.HIGHEST

@jax.custom_vjp
def low(v):
    return lax.optimization_barrier(v.astype(jnp.bfloat16)).astype(jnp.float32)

@jax.custom_vjp
def low_back(v):
    return v

def low_keep(v):
    return (low(v), None)

def low_pass(kept, grad):
    return (grad,)

def back_keep(v):
    return (v, None)

def back_low(kept, grad):
    return (low(grad),)
low.defvjp(low_keep, low_pass)
low_back.defvjp(back_keep, back_low)

def product(matrix_left, matrix_right):
    return jnp.dot(matrix_left, matrix_right, precision=precise)

def layer_norm(resid, gain, shift):
    centre = lax.optimization_barrier(jnp.mean(resid, axis=-1, keepdims=True))
    centered = resid - centre
    spread = lax.optimization_barrier(jnp.mean(centered * centered, axis=-1, keepdims=True))
    return centered * lax.rsqrt(spread + EPS_NORM) * gain + shift

def split_heads(matrix):
    return matrix.reshape(matrix.shape[0], HEADS, HD)

def attend(pieces):
    queries, key_rows, value_rows, segment_row = pieces
    scores = low_back(jnp.einsum('qhe,khe->hqk', split_heads(queries), split_heads(key_rows), precision=precise))
    same_segment = segment_row[:, None] == segment_row[None, :]
    scores = jnp.where(same_segment[None], scores, -1000000000.0)
    softmax_rows = low(jax.nn.softmax(scores, axis=-1))
    mixture = jnp.einsum('hqk,khe->qhe', softmax_rows, split_heads(value_rows), precision=precise)
    return mixture.reshape(queries.shape[0], D)

def forward(attention, inner, outer, vector_rows, token_rows, segment_ids):
    attention = low(attention)
    inner = low(inner)
    outer = low(outer)
    vector_rows = low(vector_rows)
    bias_query = vector_rows[0]
    bias_value = vector_rows[1]
    bias_output = vector_rows[2]
    gain_one = vector_rows[3]
    shift_one = vector_rows[4]
    bias_inner = vector_rows[5:9].reshape(FF)
    bias_outer = vector_rows[9]
    gain_two = vector_rows[10]
    shift_two = vector_rows[11]

    def group_layer(pieces):
        token_group, segment_group = pieces
        row_count = token_group.shape[0]
        flat_rows = token_group.reshape(row_count * SEQ, D)
        queries = low_back(low((product(flat_rows, attention[0]) + bias_query) * 0.125))
        key_rows = low_back(low(product(flat_rows, attention[1])))
        value_rows = low_back(low(product(flat_rows, attention[2]) + bias_value))
        context = lax.map(jax.checkpoint(attend), (queries.reshape(row_count, SEQ, D), key_rows.reshape(row_count, SEQ, D), value_rows.reshape(row_count, SEQ, D), segment_group))
        context = low_back(low(context.reshape(row_count * SEQ, D)))
        attention_out = low_back(product(context, attention[3]) + bias_output)
        hidden_one = layer_norm(flat_rows + attention_out, gain_one, shift_one)
        inner_pre = low_back(product(low(hidden_one), inner) + bias_inner)
        activated = low(jax.nn.gelu(inner_pre, approximate=False))
        outer_pre = low_back(product(activated, outer) + bias_outer)
        result = layer_norm(hidden_one + outer_pre, gain_two, shift_two)
        return result.reshape(row_count, SEQ, D)
    groups = token_rows.reshape(ROWS // 8, 8, SEQ, D)
    segment_groups = segment_ids.reshape(ROWS // 8, 8, SEQ)
    result = lax.map(jax.checkpoint(group_layer), (groups, segment_groups))
    return result.reshape(ROWS, SEQ, D)

def adam_update(weight, first, second, gradient, factor, rate):
    clipped = gradient * factor
    first_new = BETA_ONE * first + (1.0 - BETA_ONE) * clipped
    second_new = BETA_TWO * second + (1.0 - BETA_TWO) * clipped * clipped
    first_hat = first_new / (1.0 - BETA_ONE ** STEP)
    second_hat = second_new / (1.0 - BETA_TWO ** STEP)
    weight_new = weight - rate * (first_hat / (jnp.sqrt(second_hat) + ADAM_EPS) + DECAY * weight)
    return (weight_new, first_new, second_new)

def reference(tokens, segment_ids, cotangent, attention_weight, attention_first, attention_second, inner_weight, inner_first, inner_second, outer_weight, outer_first, outer_second, vectors, vector_first, vector_second):
    tokens_f = tokens.astype(jnp.float32)

    def layer(attention, inner, outer, vector_rows, token_rows):
        return forward(attention, inner, outer, vector_rows, token_rows, segment_ids)
    output, pullback = jax.vjp(layer, attention_weight, inner_weight, outer_weight, vectors, tokens_f)
    grad_attention, grad_inner, grad_outer, grad_vectors, input_grad = pullback(cotangent.astype(jnp.float32))
    squares = jnp.sum(grad_attention * grad_attention) + jnp.sum(grad_inner * grad_inner) + jnp.sum(grad_outer * grad_outer) + jnp.sum(grad_vectors * grad_vectors)
    grad_norm = jnp.sqrt(squares)
    factor = CLIP / (grad_norm + 1e-06)
    attention_new, attention_first_new, attention_second_new = adam_update(attention_weight, attention_first, attention_second, grad_attention, factor, RATE_MATRIX)
    inner_new, inner_first_new, inner_second_new = adam_update(inner_weight, inner_first, inner_second, grad_inner, factor, RATE_MATRIX)
    outer_new, outer_first_new, outer_second_new = adam_update(outer_weight, outer_first, outer_second, grad_outer, factor, RATE_MATRIX)
    vectors_new, vector_first_new, vector_second_new = adam_update(vectors, vector_first, vector_second, grad_vectors, factor, RATE_VECTOR)
    vector_grad = grad_vectors * factor
    return (output.astype(jnp.bfloat16), input_grad, grad_norm, attention_new, attention_first_new, attention_second_new, inner_new, inner_first_new, inner_second_new, outer_new, outer_first_new, outer_second_new, vectors_new, vector_first_new, vector_second_new, vector_grad)
```

```python
import functools

import jax
import jax.numpy as jnp
from jax import lax
from jax.sharding import PartitionSpec as P

from jax.experimental import pallas as pl
from jax.experimental.pallas import tpu as pltpu

MESH = pl.DeviceIdType.MESH
NB = 6
ALPHA = (1, 1, 1, 1, 0, 0)

def place():
    dp, f = lax.axis_index("dp"), lax.axis_index("fsdp")
    return dp//2, dp%2, f//2, f%2

class Gather:
    def __init__(self, att, out, inn, sems, alpha):
        self.att,self.out,self.inn=att,out,inn
        self.zs,self.zr,self.ys,self.yr,self.xs,self.xr,self.cs,self.cr=sems
        self.x,self.c,self.z,self.y=place()
        self.alpha=alpha
        self.started=[]
    def dev(self,x=None,c=None,z=None,y=None):
        x=self.x if x is None else x; c=self.c if c is None else c; z=self.z if z is None else z; y=self.y if y is None else y
        return (x*2+c, z*2+y)
    def ref(self,i,shard,cols,c=None):
        c=self.c if c is None else c
        cc=slice(None) if cols is None else pl.ds(pl.multiple_of(cols*384,128),384)
        if i<2: return self.att.at[2*i+c,shard,:,cc]
        if i<4: return self.out.at[shard,2*(i-2)+c,:,cc]
        return self.inn.at[2*(i-4)+c,shard,:,cc]
    def cp(self,r,ss,rs,dev):
        return pltpu.make_async_remote_copy(src_ref=r,dst_ref=r,send_sem=ss,recv_sem=rs,device_id=dev,device_id_type=MESH)
    def ccopy(self, i, recv=False):
        c = 1 - self.c if recv else self.c
        return self.cp(self.ref(i, slice(None), None, c), self.cs.at[i], self.cr.at[i], self.dev(c=1 - self.c))
    def go(self, cp):
        cp.start()
    def zmove(self,i,s,right,shard,):
        k=s if right else 3+s
        d=jnp.minimum(self.z+1,3) if right else jnp.maximum(self.z-1,0)
        return self.cp(self.ref(i,shard*2+self.y,self.x if self.alpha[i] else None),self.zs.at[i,k],self.zr.at[i,k],self.dev(z=d))
    def yown(self,i): self.ymove(i,self.z).start()
    def zown(self,i):
        @pl.when(self.z<3)
        def _(): self.zmove(i,0,True,self.z).start()
        @pl.when(self.z>0)
        def _(): self.zmove(i,0,False,self.z).start()
    def ymove(self,i,sz,recv=False):
        yy=1-self.y if recv else self.y
        return self.cp(self.ref(i,sz*2+yy,self.x if self.alpha[i] else None),self.ys.at[i,sz],self.yr.at[i,sz],self.dev(y=1-self.y))
    def xmove(self,i,sz,own,recv=False):
        yy=self.y if own else 1-self.y
        xx=1-self.x if recv else self.x
        k=sz+(0 if own else 4)
        return self.cp(self.ref(i,sz*2+yy,xx),self.xs.at[i,k],self.xr.at[i,k],self.dev(x=1-self.x))
    def arrive(self,i,s):
        z=self.z
        @pl.when(z>=1+s)
        def _():
            sh=jnp.maximum(z-1-s,0)
            self.zmove(i,s,True,sh).wait_recv()
            if s<2:
                @pl.when(z<3)
                def _(): self.zmove(i,s+1,True,sh).start()
            self.ymove(i,sh).start()
            if self.alpha[i]: self.xmove(i,sh,True).start()
        @pl.when(z+1+s<=3)
        def _():
            sh=jnp.minimum(z+1+s,3)
            self.zmove(i,s,False,sh).wait_recv()
            if s<2:
                @pl.when(z>0)
                def _(): self.zmove(i,s+1,False,sh).start()
            self.ymove(i,sh).start()
            if self.alpha[i]: self.xmove(i,sh,True).start()
    def a0(self,i): self.arrive(i,0)
    def a1(self,i): self.arrive(i,1)
    def a2(self,i): self.arrive(i,2)
    def third(self,i):
        def one(sh):
            self.ymove(i,sh,True).wait_recv()
            if self.alpha[i]: self.xmove(i,sh,False).start()
        one(self.z)
        for s in range(3):
            @pl.when(self.z>=1+s)
            def _(): one(jnp.maximum(self.z-1-s,0))
            @pl.when(self.z+1+s<=3)
            def _(): one(jnp.minimum(self.z+1+s,3))
    def fourth(self,i):
        if self.alpha[i]:
            for sz in range(4):
                self.xmove(i,sz,False,True).wait_recv()
                @pl.when(sz!=self.z)
                def _(): self.xmove(i,sz,True,True).wait_recv()
        self.go(self.ccopy(i))
    def finish(self):
        z=self.z
        for i in range(NB):
            for s in range(3):
                @pl.when((z<3)&(z-s>=0))
                def _(): self.zmove(i,s,True,jnp.maximum(z-s,0)).wait_send()
                @pl.when((z>0)&(z+s<=3))
                def _(): self.zmove(i,s,False,jnp.minimum(z+s,3)).wait_send()
            for sz in range(4):
                self.ymove(i,sz).wait_send()
                if self.alpha[i]:
                    self.xmove(i,sz,False).wait_send()
                    @pl.when(sz!=z)
                    def _(): self.xmove(i,sz,True).wait_send()
            self.ccopy(i).wait_send()
    def fifth(self,i): self.ccopy(i,True).wait_recv()

def order_d(look,yl,d3,d4,d5,n=NB):
    o=[]
    for i in range(max(look,yl)):
        if i<look: o.append(("zown",i))
        if i<yl: o.append(("yown",i))
    for t in range(n+d5):
        for s in range(3):
            if 0<=t-s<n: o.append((f"a{s}",t-s))
        if t+look<n: o.append(("zown",t+look))
        if t+yl<n: o.append(("yown",t+yl))
        if 0<=t-d3<n: o.append(("third",t-d3))
        if 0<=t-d4<n: o.append(("fourth",t-d4))
        if 0<=t-d5<n: o.append(("fifth",t-d5))
    return o

def line_kernel(alpha,order,a,o,n,att,out,inn,*sems):
    g=Gather(att,out,inn,sems,alpha)
    me=g.z*2+g.y
    for k in range(4):
        att[k,me]=a[k]
        out[me,k]=o[pl.ds(96*k,96),:]
        inn[k,me]=n[:,768*k:768*k+768]
    zr,zl=g.dev(z=jnp.minimum(g.z+1,3)),g.dev(z=jnp.maximum(g.z-1,0))
    bar=pltpu.get_barrier_semaphore()
    for d in (g.dev(y=1-g.y),g.dev(x=1-g.x),g.dev(c=1-g.c)): pl.semaphore_signal(bar,inc=1,device_id=d,device_id_type=MESH)
    @pl.when(g.z<3)
    def _(): pl.semaphore_signal(bar,inc=1,device_id=zr,device_id_type=MESH)
    @pl.when(g.z>0)
    def _(): pl.semaphore_signal(bar,inc=1,device_id=zl,device_id_type=MESH)
    pl.semaphore_wait(bar,jnp.where((g.z==0)|(g.z==3),4,5))
    steps = dict(zown=g.zown, yown=g.yown, a0=g.a0, a1=g.a1, a2=g.a2, third=g.third, fourth=g.fourth, fifth=g.fifth)
    for s,i in order: steps[s](i)
    g.finish()

def gather_weights(a,o,n,alpha,order):
    sems = [pltpu.SemaphoreType.DMA((NB,6)),pltpu.SemaphoreType.DMA((NB,6)),pltpu.SemaphoreType.DMA((NB,4)),pltpu.SemaphoreType.DMA((NB,4)),pltpu.SemaphoreType.DMA((NB,8)),pltpu.SemaphoreType.DMA((NB,8)),pltpu.SemaphoreType.DMA((NB,)),pltpu.SemaphoreType.DMA((NB,))]
    vm=pl.BlockSpec(memory_space=pltpu.VMEM)
    return tuple(pl.pallas_call(functools.partial(line_kernel,alpha,order),
        out_shape=[jax.ShapeDtypeStruct((4,8,96,768),jnp.bfloat16),jax.ShapeDtypeStruct((8,4,96,768),jnp.bfloat16),jax.ShapeDtypeStruct((4,8,96,768),jnp.bfloat16)],
        in_specs=[vm]*3,out_specs=[vm]*3,scratch_shapes=sems,
        compiler_params=pltpu.CompilerParams(collective_id=0,has_side_effects=True,vmem_limit_bytes=60*2**20))(a,o,n))

HEADS = 12
STEP = 10


EPS_NORM = 1e-12
BETA_ONE = 0.9
BETA_TWO = 0.999
ADAM_EPS = 1e-08
DECAY = 0.01
RATE_MATRIX = 0.03
RATE_VECTOR = 0.5
CLIP = 1.0


def layer_norm(resid, gain, shift):
    centre = jnp.mean(resid, axis=-1, keepdims=True)
    centered = resid - centre
    spread = jnp.mean(centered * centered, axis=-1, keepdims=True)
    return centered * lax.rsqrt(spread + EPS_NORM) * gain + shift


def gelu_exact(values):
    return jax.nn.gelu(values, approximate=False)


def split_heads(matrix):
    return matrix.reshape(matrix.shape[0], HEADS, matrix.shape[1] // HEADS)


def row_scores(query_row, key_row, segment_row):
    scores = jnp.einsum(
        "qhe,khe->hqk",
        split_heads(query_row),
        split_heads(key_row),
        preferred_element_type=jnp.float32,
    )
    same_segment = segment_row[:, None] == segment_row[None, :]
    return jnp.where(same_segment[None], scores, -1000000000.0)


def attend_row(pieces):
    query_row, key_row, value_row, segment_row = pieces
    scores = row_scores(query_row, key_row, segment_row)
    row_peak = jnp.max(scores, axis=-1, keepdims=True)
    exponent = jnp.exp(scores - row_peak)
    row_total = jnp.sum(exponent, axis=-1, keepdims=True)
    softmax_rows = exponent / row_total
    mixture = jnp.einsum(
        "hqk,khe->qhe",
        softmax_rows.astype(jnp.bfloat16),
        split_heads(value_row),
        preferred_element_type=jnp.float32,
    )
    return (mixture.reshape(query_row.shape).astype(jnp.bfloat16), row_peak + jnp.log(row_total))


def attend_back(pieces):
    query_row, key_row, value_row, segment_row, log_total, context_grad = pieces
    row_shape = query_row.shape
    scores = row_scores(query_row, key_row, segment_row)
    softmax_rows = jnp.exp(scores - log_total)
    grad_heads = split_heads(context_grad)
    prob_grad = jnp.einsum(
        "qhe,khe->hqk", grad_heads, split_heads(value_row), preferred_element_type=jnp.float32
    )
    value_grad = jnp.einsum(
        "hqk,qhe->khe",
        softmax_rows.astype(jnp.bfloat16),
        grad_heads,
        preferred_element_type=jnp.float32,
    )
    row_delta = jnp.sum(prob_grad * softmax_rows, axis=-1, keepdims=True)
    score_grad = (softmax_rows * (prob_grad - row_delta)).astype(jnp.bfloat16)
    query_grad = jnp.einsum(
        "hqk,khe->qhe", score_grad, split_heads(key_row), preferred_element_type=jnp.float32
    )
    key_grad = jnp.einsum(
        "hqk,qhe->khe", score_grad, split_heads(query_row), preferred_element_type=jnp.float32
    )
    return (
        query_grad.reshape(row_shape).astype(jnp.bfloat16),
        key_grad.reshape(row_shape).astype(jnp.bfloat16),
        value_grad.reshape(row_shape).astype(jnp.bfloat16),
    )


def adam_update(weight, first, second, gradient, factor, rate):
    clipped = gradient * factor
    first_new = BETA_ONE * first + (1.0 - BETA_ONE) * clipped
    second_new = BETA_TWO * second + (1.0 - BETA_TWO) * clipped * clipped
    first_hat = first_new / (1.0 - BETA_ONE**STEP)
    second_hat = second_new / (1.0 - BETA_TWO**STEP)
    weight_new = weight - rate * (first_hat / (jnp.sqrt(second_hat) + ADAM_EPS) + DECAY * weight)
    return (weight_new, first_new, second_new)


def body(
    tokens,
    segment_ids,
    cotangent,
    attention_weight,
    attention_first,
    attention_second,
    inner_weight,
    inner_first,
    inner_second,
    outer_weight,
    outer_first,
    outer_second,
    vectors,
    vector_first,
    vector_second,
):
    row_count, seq_length, model_width = tokens.shape
    token_count = row_count * seq_length
    flat_rows = tokens.reshape(token_count, model_width)
    shards = (
        attention_weight.astype(jnp.bfloat16),
        inner_weight.astype(jnp.bfloat16),
        outer_weight.astype(jnp.bfloat16),
        vectors.astype(jnp.bfloat16),
    )
    vector_full = lax.all_gather(shards[3], "fsdp", axis=1, tiled=True)
    if lax.axis_size("fsdp") == 8 and lax.axis_size("dp") == 4:
        attention_full, outer_full, inner_full = gather_weights(
            shards[0], shards[2], shards[1], ALPHA, order_d(2, 4, 3, 4, 5)
        )
        attention_full = attention_full.reshape(4, model_width, model_width)
        outer_full = outer_full.reshape(-1, model_width)
        inner_full = inner_full.reshape(4, model_width, -1).transpose(1, 0, 2).reshape(model_width, -1)
    else:
        attention_full, inner_full, outer_full = (
            lax.all_gather(shards[0], "fsdp", axis=1, tiled=True),
            lax.all_gather(shards[1], "fsdp", axis=0, tiled=True),
            lax.all_gather(shards[2], "fsdp", axis=0, tiled=True),
        )
    vector_rows = vector_full.astype(jnp.float32)
    bias_query = vector_rows[0]
    bias_value = vector_rows[1]
    bias_output = vector_rows[2]
    gain_one = vector_rows[3]
    shift_one = vector_rows[4]
    bias_inner = vector_rows[5:9].reshape(-1)
    bias_outer = vector_rows[9]
    gain_two = vector_rows[10]
    shift_two = vector_rows[11]
    projected = jnp.einsum(
        "td,kde->kte", flat_rows, attention_full[:3], preferred_element_type=jnp.float32
    )
    queries = ((projected[0] + bias_query) * 0.125).astype(jnp.bfloat16)
    key_rows = projected[1].astype(jnp.bfloat16)
    value_rows = (projected[2] + bias_value).astype(jnp.bfloat16)
    row_view = (row_count, seq_length, model_width)
    query_view = queries.reshape(row_view)
    key_view = key_rows.reshape(row_view)
    value_view = value_rows.reshape(row_view)
    context, log_totals = lax.map(attend_row, (query_view, key_view, value_view, segment_ids))
    context_flat = context.reshape(token_count, model_width)
    attention_out = (
        jnp.dot(context_flat, attention_full[3], preferred_element_type=jnp.float32) + bias_output
    )
    sum_one = flat_rows.astype(jnp.float32) + attention_out
    hidden_one, norm_one_back = jax.vjp(layer_norm, sum_one, gain_one, shift_one)
    hidden_low = hidden_one.astype(jnp.bfloat16)
    inner_pre = jnp.dot(hidden_low, inner_full, preferred_element_type=jnp.float32) + bias_inner
    activated, gelu_back = jax.vjp(gelu_exact, inner_pre)
    activated_low = activated.astype(jnp.bfloat16)
    outer_pre = jnp.dot(activated_low, outer_full, preferred_element_type=jnp.float32) + bias_outer
    sum_two = hidden_one + outer_pre
    output, norm_two_back = jax.vjp(layer_norm, sum_two, gain_two, shift_two)
    activations = output.astype(jnp.bfloat16).reshape(row_view)
    attention_back, inner_back, outer_back = attention_full, inner_full, outer_full
    output_grad = cotangent.reshape(token_count, model_width).astype(jnp.float32)
    sum_two_grad, gain_two_grad, shift_two_grad = norm_two_back(output_grad)
    outer_grad = sum_two_grad.astype(jnp.bfloat16)
    outer_weight_grad = jnp.einsum(
        "tf,td->fd", activated_low, outer_grad, preferred_element_type=jnp.float32
    )
    bias_outer_grad = jnp.sum(outer_grad.astype(jnp.float32), axis=0)
    activated_grad = jnp.einsum(
        "td,fd->tf", outer_grad, outer_back, preferred_element_type=jnp.float32
    )
    (inner_raw_grad,) = gelu_back(activated_grad)
    inner_grad = inner_raw_grad.astype(jnp.bfloat16)
    inner_weight_grad = jnp.einsum(
        "td,tf->df", hidden_low, inner_grad, preferred_element_type=jnp.float32
    )
    bias_inner_grad = jnp.sum(inner_grad.astype(jnp.float32), axis=0)
    hidden_one_grad = sum_two_grad + jnp.einsum(
        "tf,df->td", inner_grad, inner_back, preferred_element_type=jnp.float32
    )
    sum_one_grad, gain_one_grad, shift_one_grad = norm_one_back(hidden_one_grad)
    attention_grad = sum_one_grad.astype(jnp.bfloat16)
    output_weight_grad = jnp.einsum(
        "td,te->de", context_flat, attention_grad, preferred_element_type=jnp.float32
    )
    bias_output_grad = jnp.sum(attention_grad.astype(jnp.float32), axis=0)
    context_grad = jnp.einsum(
        "te,de->td", attention_grad, attention_back[3], preferred_element_type=jnp.float32
    ).astype(jnp.bfloat16)
    query_grad, key_grad, value_grad = lax.map(
        attend_back,
        (query_view, key_view, value_view, segment_ids, log_totals, context_grad.reshape(row_view)),
    )
    query_grad = query_grad.reshape(token_count, model_width)
    key_grad = key_grad.reshape(token_count, model_width)
    value_grad = value_grad.reshape(token_count, model_width)
    grad_stack = jnp.stack([query_grad, key_grad, value_grad])
    projection_grad = jnp.einsum(
        "td,kte->kde", flat_rows, grad_stack, preferred_element_type=jnp.float32
    )
    projection_grad = projection_grad * jnp.array([0.125, 1.0, 1.0], jnp.float32)[:, None, None]
    attention_weight_grad = jnp.concatenate([projection_grad, output_weight_grad[None]], axis=0)
    bias_query_grad = 0.125 * jnp.sum(query_grad.astype(jnp.float32), axis=0)
    bias_value_grad = jnp.sum(value_grad.astype(jnp.float32), axis=0)
    token_grad = sum_one_grad + 0.125 * jnp.einsum(
        "te,de->td", query_grad, attention_back[0], preferred_element_type=jnp.float32
    )
    token_grad = token_grad + jnp.einsum(
        "kte,kde->td", grad_stack[1:], attention_back[1:3], preferred_element_type=jnp.float32
    )
    input_grad = token_grad.reshape(row_view)
    vector_grad = jnp.concatenate(
        [
            jnp.stack(
                [bias_query_grad, bias_value_grad, bias_output_grad, gain_one_grad, shift_one_grad]
            ),
            bias_inner_grad.reshape(4, model_width),
            jnp.stack([bias_outer_grad, gain_two_grad, shift_two_grad]),
        ],
        axis=0,
    )
    shard_grads = (
        lax.psum_scatter(
            attention_weight_grad.astype(jnp.bfloat16), "fsdp", scatter_dimension=1, tiled=True
        ).astype(jnp.float32),
        lax.psum_scatter(
            inner_weight_grad.astype(jnp.bfloat16), "fsdp", scatter_dimension=0, tiled=True
        ).astype(jnp.float32),
        lax.psum_scatter(
            outer_weight_grad.astype(jnp.bfloat16), "fsdp", scatter_dimension=0, tiled=True
        ).astype(jnp.float32),
        lax.psum_scatter(
            vector_grad.astype(jnp.bfloat16), "fsdp", scatter_dimension=1, tiled=True
        ).astype(jnp.float32),
    )
    summed = (
        lax.psum(shard_grads[0].astype(jnp.bfloat16), "dp").astype(jnp.float32),
        lax.psum(shard_grads[1].astype(jnp.bfloat16), "dp").astype(jnp.float32),
        lax.psum(shard_grads[2].astype(jnp.bfloat16), "dp").astype(jnp.float32),
        lax.psum(shard_grads[3].astype(jnp.bfloat16), "dp").astype(jnp.float32),
    )
    local_squares = (
        jnp.sum(summed[0] * summed[0])
        + jnp.sum(summed[1] * summed[1])
        + jnp.sum(summed[2] * summed[2])
        + jnp.sum(summed[3] * summed[3])
    )
    total_squares = lax.psum(local_squares, "fsdp")
    grad_norm = jnp.sqrt(total_squares)
    factor = CLIP / (grad_norm + 1e-06)
    attention_new, attention_first_new, attention_second_new = adam_update(
        attention_weight, attention_first, attention_second, summed[0], factor, RATE_MATRIX
    )
    inner_new, inner_first_new, inner_second_new = adam_update(
        inner_weight, inner_first, inner_second, summed[1], factor, RATE_MATRIX
    )
    outer_new, outer_first_new, outer_second_new = adam_update(
        outer_weight, outer_first, outer_second, summed[2], factor, RATE_MATRIX
    )
    vectors_new, vector_first_new, vector_second_new = adam_update(
        vectors, vector_first, vector_second, summed[3], factor, RATE_VECTOR
    )
    clipped_vectors = summed[3] * factor
    return (
        activations,
        input_grad,
        grad_norm,
        attention_new,
        attention_first_new,
        attention_second_new,
        inner_new,
        inner_first_new,
        inner_second_new,
        outer_new,
        outer_first_new,
        outer_second_new,
        vectors_new,
        vector_first_new,
        vector_second_new,
        clipped_vectors,
    )


def solution(mesh):
    placed = (
        P(("dp", "fsdp"), None, None),
        P(("dp", "fsdp"), None),
        P(("dp", "fsdp"), None, None),
        P(None, "fsdp", None),
        P(None, "fsdp", None),
        P(None, "fsdp", None),
        P("fsdp", None),
        P("fsdp", None),
        P("fsdp", None),
        P("fsdp", None),
        P("fsdp", None),
        P("fsdp", None),
        P(None, "fsdp"),
        P(None, "fsdp"),
        P(None, "fsdp"),
    )
    return jax.shard_map(
        body,
        mesh=mesh,
        in_specs=placed,
        out_specs=(
            P(("dp", "fsdp"), None, None),
            P(("dp", "fsdp"), None, None),
            P(),
            P(None, "fsdp", None),
            P(None, "fsdp", None),
            P(None, "fsdp", None),
            P("fsdp", None),
            P("fsdp", None),
            P("fsdp", None),
            P("fsdp", None),
            P("fsdp", None),
            P("fsdp", None),
            P(None, "fsdp"),
            P(None, "fsdp"),
            P(None, "fsdp"),
            P(None, "fsdp"),
        ),
        check_vma=False,
    )
```

```python
import functools

import jax
import jax.numpy as jnp
from jax import lax
from jax.experimental import pallas as pl
from jax.experimental.pallas import tpu as pltpu
from jax.sharding import PartitionSpec as P

HEADS = 12
STEP = 10


EPS_NORM = 1e-12
BETA_ONE = 0.9
BETA_TWO = 0.999
ADAM_EPS = 1e-08
DECAY = 0.01
RATE_MATRIX = 0.03
RATE_VECTOR = 0.5
CLIP = 1.0


def layer_norm(resid, gain, shift):
    centre = jnp.mean(resid, axis=-1, keepdims=True)
    centered = resid - centre
    spread = jnp.mean(centered * centered, axis=-1, keepdims=True)
    return centered * lax.rsqrt(spread + EPS_NORM) * gain + shift


def gelu_exact(values):
    return jax.nn.gelu(values, approximate=False)


def split_heads(matrix):
    return matrix.reshape(matrix.shape[0], HEADS, matrix.shape[1] // HEADS)


def row_scores(query_row, key_row, segment_row):
    scores = jnp.einsum(
        "qhe,khe->hqk",
        split_heads(query_row),
        split_heads(key_row),
        preferred_element_type=jnp.float32,
    )
    same_segment = segment_row[:, None] == segment_row[None, :]
    return jnp.where(same_segment[None], scores, -1000000000.0)


def attend_row(pieces):
    query_row, key_row, value_row, segment_row = pieces
    scores = row_scores(query_row, key_row, segment_row)
    row_peak = jnp.max(scores, axis=-1, keepdims=True)
    exponent = jnp.exp(scores - row_peak)
    row_total = jnp.sum(exponent, axis=-1, keepdims=True)
    softmax_rows = exponent / row_total
    mixture = jnp.einsum(
        "hqk,khe->qhe",
        softmax_rows.astype(jnp.bfloat16),
        split_heads(value_row),
        preferred_element_type=jnp.float32,
    )
    return (mixture.reshape(query_row.shape).astype(jnp.bfloat16), row_peak + jnp.log(row_total))


def attend_back(pieces):
    query_row, key_row, value_row, segment_row, log_total, context_grad = pieces
    row_shape = query_row.shape
    scores = row_scores(query_row, key_row, segment_row)
    softmax_rows = jnp.exp(scores - log_total)
    grad_heads = split_heads(context_grad)
    prob_grad = jnp.einsum(
        "qhe,khe->hqk", grad_heads, split_heads(value_row), preferred_element_type=jnp.float32
    )
    value_grad = jnp.einsum(
        "hqk,qhe->khe",
        softmax_rows.astype(jnp.bfloat16),
        grad_heads,
        preferred_element_type=jnp.float32,
    )
    row_delta = jnp.sum(prob_grad * softmax_rows, axis=-1, keepdims=True)
    score_grad = (softmax_rows * (prob_grad - row_delta)).astype(jnp.bfloat16)
    query_grad = jnp.einsum(
        "hqk,khe->qhe", score_grad, split_heads(key_row), preferred_element_type=jnp.float32
    )
    key_grad = jnp.einsum(
        "hqk,qhe->khe", score_grad, split_heads(query_row), preferred_element_type=jnp.float32
    )
    return (
        query_grad.reshape(row_shape).astype(jnp.bfloat16),
        key_grad.reshape(row_shape).astype(jnp.bfloat16),
        value_grad.reshape(row_shape).astype(jnp.bfloat16),
    )


def adam_update(weight, first, second, gradient, factor, rate):
    clipped = gradient * factor
    first_new = BETA_ONE * first + (1.0 - BETA_ONE) * clipped
    second_new = BETA_TWO * second + (1.0 - BETA_TWO) * clipped * clipped
    first_hat = first_new / (1.0 - BETA_ONE**STEP)
    second_hat = second_new / (1.0 - BETA_TWO**STEP)
    weight_new = weight - rate * (first_hat / (jnp.sqrt(second_hat) + ADAM_EPS) + DECAY * weight)
    return (weight_new, first_new, second_new)


F32, BF16 = jnp.float32, jnp.bfloat16
MESH = pl.DeviceIdType.MESH
BLOCKS = 6
CHUNKS = 6
INV_SQRT2 = 0.7071067811865476
INV_SQRT2PI = 0.3989422804014327


def dot_nn(a, b):
    return lax.dot_general(a, b, (((1,), (0,)), ((), ())), preferred_element_type=F32)


def dot_nt(a, b):
    return lax.dot_general(a, b, (((1,), (1,)), ((), ())), preferred_element_type=F32)


def dot_tn(a, b):
    return lax.dot_general(a, b, (((0,), (0,)), ((), ())), preferred_element_type=F32)


def wide(value):
    return value.astype(F32)


class Place:
    def __init__(self):
        dp, fsdp = lax.axis_index("dp"), lax.axis_index("fsdp")
        self.x, self.c, self.z, self.y = dp // 2, dp % 2, fsdp // 2, fsdp % 2

    def dev(self, x=None, c=None, z=None, y=None):
        x = self.x if x is None else x
        c = self.c if c is None else c
        z = self.z if z is None else z
        y = self.y if y is None else y
        return (x * 2 + c, z * 2 + y)

    def far(self, dz):
        return lax.rem(self.z + dz, 4)


def half(x):
    return pl.ds(pl.multiple_of(x * 384, 128), 384)


def remote(src, dst, send, recv, dev):
    return pltpu.make_async_remote_copy(
        src_ref=src, dst_ref=dst, send_sem=send, recv_sem=recv, device_id=dev, device_id_type=MESH
    )


class Gather:
    def __init__(self, at, att, inn, out, sems, alpha):
        self.at, self.att, self.inn, self.out, self.alpha = at, att, inn, out, alpha
        self.zs, self.zr, self.ys, self.yr, self.xs, self.xr, self.cs, self.cr = sems

    def ref(self, i, z, y, x, c=None):
        c = self.at.c if c is None else c
        cols = half(x) if self.alpha[i] else slice(None)
        if i < 2:
            return self.att.at[2 * i + c, z, y, :, cols]
        if i < 4:
            return self.inn.at[2 * (i - 2) + c, z, y, :, cols]
        return self.out.at[z, y, 2 * (i - 4) + c, :, cols]

    def whole(self, i, c):
        if i < 2:
            return self.att.at[2 * i + c]
        if i < 4:
            return self.inn.at[2 * (i - 2) + c]
        return self.out.at[:, :, 2 * (i - 4) + c]

    def zmove(self, i, s, right, sz):
        k = s if right else 3 + s
        z = self.at.z
        dest = jnp.minimum(z + 1, 3) if right else jnp.maximum(z - 1, 0)
        r = self.ref(i, sz, self.at.y, self.at.x)
        return remote(r, r, self.zs.at[i, k], self.zr.at[i, k], self.at.dev(z=dest))

    def ymove(self, i, sz, recv=False):
        y = 1 - self.at.y if recv else self.at.y
        r = self.ref(i, sz, y, self.at.x)
        return remote(r, r, self.ys.at[i, sz], self.yr.at[i, sz], self.at.dev(y=1 - self.at.y))

    def xmove(self, i, sz, own, recv=False):
        y = self.at.y if own else 1 - self.at.y
        x = 1 - self.at.x if recv else self.at.x
        k = sz + (0 if own else 4)
        r = self.ref(i, sz, y, x)
        return remote(r, r, self.xs.at[i, k], self.xr.at[i, k], self.at.dev(x=1 - self.at.x))

    def cmove(self, i, recv=False):
        r = self.whole(i, 1 - self.at.c if recv else self.at.c)
        return remote(r, r, self.cs.at[i], self.cr.at[i], self.at.dev(c=1 - self.at.c))

    def zown(self, i):
        z = self.at.z

        @pl.when(z < 3)
        def _():
            self.zmove(i, 0, True, z).start()

        @pl.when(z > 0)
        def _():
            self.zmove(i, 0, False, z).start()

    def yown(self, i):
        self.ymove(i, self.at.z).start()

    def arrive(self, i, s):
        z = self.at.z

        def forward(sz, right, more):
            self.zmove(i, s, right, sz).wait_recv()
            if s < 2:

                @pl.when(more)
                def _():
                    self.zmove(i, s + 1, right, sz).start()

            self.ymove(i, sz).start()
            if self.alpha[i]:
                self.xmove(i, sz, True).start()

        @pl.when(z >= 1 + s)
        def _():
            forward(jnp.maximum(z - 1 - s, 0), True, z < 3)

        @pl.when(z + 1 + s <= 3)
        def _():
            forward(jnp.minimum(z + 1 + s, 3), False, z > 0)

    def across(self, i, s):
        z = self.at.z

        def one(sz):
            self.ymove(i, sz, True).wait_recv()
            if self.alpha[i]:
                self.xmove(i, sz, False).start()

        if s == 0:
            one(z)
            return

        @pl.when(z >= s)
        def _():
            one(jnp.maximum(z - s, 0))

        @pl.when(z + s <= 3)
        def _():
            one(jnp.minimum(z + s, 3))

    def join(self, i):
        if self.alpha[i]:
            for sz in range(4):
                self.xmove(i, sz, False, True).wait_recv()

                @pl.when(sz != self.at.z)
                def _():
                    self.xmove(i, sz, True, True).wait_recv()

        self.cmove(i).start()

    def have(self, i):
        self.cmove(i, True).wait_recv()

    def finish(self):
        z = self.at.z
        for i in range(BLOCKS):
            for s in range(3):

                @pl.when((z < 3) & (z - s >= 0))
                def _():
                    self.zmove(i, s, True, jnp.maximum(z - s, 0)).wait_send()

                @pl.when((z > 0) & (z + s <= 3))
                def _():
                    self.zmove(i, s, False, jnp.minimum(z + s, 3)).wait_send()

            for sz in range(4):
                self.ymove(i, sz).wait_send()
                if self.alpha[i]:
                    self.xmove(i, sz, False).wait_send()

                    @pl.when(sz != z)
                    def _():
                        self.xmove(i, sz, True).wait_send()

            self.cmove(i).wait_send()


class Scatter:
    def __init__(self, at, grad, total, bufs, sems, alpha):
        self.at, self.grad, self.total, self.alpha = at, grad, total, alpha
        self.ra1, self.ra2, self.ra3, self.rb1, self.rb2, self.rb3 = bufs
        self.ss, self.rs = sems
        self.slot = [sum(1 for q in alpha[:j] if q == alpha[j]) for j in range(CHUNKS)]

    def cp(self, j, k, src, dst, dev):
        return remote(src, dst, self.ss.at[j, k], self.rs.at[j, k], dev)

    def block(self, j, c):
        return 4 * (j // 2) + 2 * c + j % 2

    def firsts(self, j, dz, own):
        n, at = self.slot[j], self.at
        z = at.far(dz)
        if self.alpha[j]:
            y = at.y if own else 1 - at.y
            return self.cp(
                j, dz + 4 * own, self.grad(j, z, y).at[:, half(1 - at.x)], self.ra1.at[n, z, y], at.dev(x=1 - at.x)
            )
        return self.cp(j, dz, self.grad(j, z, 1 - at.y), self.rb1.at[n, z], at.dev(y=1 - at.y))

    def second(self, j, dz):
        n, at = self.slot[j], self.at
        z = at.far(dz)
        return self.cp(
            j, 8 + dz, self.grad(j, z, 1 - at.y).at[:, half(at.x)], self.ra2.at[n, z], at.dev(y=1 - at.y)
        )

    def third(self, j, dz):
        n, at = self.slot[j], self.at
        z = at.far(dz)
        src = self.grad(j, z, at.y)
        if self.alpha[j]:
            return self.cp(j, 11 + dz, src.at[:, half(at.x)], self.ra3.at[n, dz - 1], at.dev(z=z))
        return self.cp(j, 11 + dz, src, self.rb2.at[n, dz - 1], at.dev(z=z))

    def fourth(self, j, recv=False):
        n, at = self.slot[j], self.at
        if self.alpha[j]:
            r = self.total.at[self.block(j, at.c), :, half(1 - at.x if recv else at.x)]
            return self.cp(j, 15, r, r, at.dev(x=1 - at.x))
        return self.cp(j, 15, self.grad(j, at.z, at.y), self.rb3.at[n], at.dev(x=1 - at.x))

    def fifth(self, j, recv=False):
        r = self.total.at[self.block(j, 1 - self.at.c if recv else self.at.c)]
        return self.cp(j, 16, r, r, self.at.dev(c=1 - self.at.c))

    def s1(self, j):
        for dz in (2, 1, 3, 0):
            self.firsts(j, dz, 0).start()

    def r1(self, j):
        if self.alpha[j]:
            for dz in (2, 1, 3, 0):
                self.firsts(j, dz, 1).start()

    def p(self, j, dz):
        if not self.alpha[j]:
            return
        n, at = self.slot[j], self.at
        z, y, h = at.far(dz), 1 - at.y, half(at.x)
        self.firsts(j, dz, 0).wait_recv()
        r = self.grad(j, z, y)
        r[:, h] = (wide(r[:, h]) + wide(self.ra1[n, z, y])).astype(BF16)
        self.second(j, dz).start()

    def q(self, j, dz):
        n, at = self.slot[j], self.at
        z, y, h = at.far(dz), at.y, half(at.x)
        r = self.grad(j, z, y)
        if self.alpha[j]:
            self.firsts(j, dz, 1).wait_recv()
            self.second(j, dz).wait_recv()
            r[:, h] = (wide(r[:, h]) + wide(self.ra1[n, z, y]) + wide(self.ra2[n, z])).astype(BF16)
        else:
            self.firsts(j, dz, 0).wait_recv()
            r[...] = (wide(r[...]) + wide(self.rb1[n, z])).astype(BF16)
        if dz:
            self.third(j, dz).start()

    def s4(self, j):
        n, at = self.slot[j], self.at
        for dz in (1, 2, 3):
            self.third(j, dz).wait_recv()
        r = self.grad(j, at.z, at.y)
        if self.alpha[j]:
            h = half(at.x)
            total = wide(r[:, h])
            for dz in range(3):
                total = total + wide(self.ra3[n, dz])
            self.total[self.block(j, at.c), :, h] = total.astype(BF16)
        else:
            total = wide(r[...])
            for dz in range(3):
                total = total + wide(self.rb2[n, dz])
            r[...] = total.astype(BF16)
        self.fourth(j).start()

    def s5(self, j):
        n, at = self.slot[j], self.at
        self.fourth(j, True).wait_recv()
        if not self.alpha[j]:
            r = self.grad(j, at.z, at.y)
            self.total[self.block(j, at.c)] = (wide(r[...]) + wide(self.rb3[n])).astype(BF16)
        self.fifth(j).start()

    def s6(self, j):
        self.fifth(j, True).wait_recv()

    def finish(self):
        for j in range(CHUNKS):
            for dz in range(4):
                self.firsts(j, dz, 0).wait_send()
                if self.alpha[j]:
                    self.firsts(j, dz, 1).wait_send()
                    self.second(j, dz).wait_send()
                if dz:
                    self.third(j, dz).wait_send()
            self.fourth(j).wait_send()
            self.fifth(j).wait_send()


def layer_kernel(
    order, alpha_gather, alpha_scatter,
    tok_h, cot_h, seg_row, watt_h, winn_h, wout_h, vec_in,
    act_h, grad_h, total, vec_grad, norm,
    att, inn, out, norm_one, resid, work, pair_in, stack, hidden, outer_grad, shown, turn, turn_two,
    active, slope, probs, mask, vec, dev_one, dev_two,
    sib_in, sib_hidden, sib_active, sib_outer, sib_slope, sib_stack,
    grad_out, ra1, ra2, ra3, rb1, rb2, rb3,
    vec_parts, vec_sib, vec_x, vec_y, vec_z, norm_parts,
    zs, zr, ys, yr, xs, xr, cs, cr, ss, rs, bs, br, vs, vr, ws, wr, ns, nr, ls,
):
    at = Place()
    me = at.z * 2 + at.y
    ag = Gather(at, att, inn, out, (zs, zr, ys, yr, xs, xr, cs, cr), alpha_gather)

    def grad_ref(j, z, y):
        return grad_out.at[j, z, y] if j < 2 else out.at[z, y, j - 2]

    rd = Scatter(at, grad_ref, total, (ra1, ra2, ra3, rb1, rb2, rb3), (ss, rs), alpha_scatter)

    def square(ref, n=768):
        return ref[...].reshape(n, n)

    other = at.dev(c=1 - at.c)

    def to_sibling(k, src, dst):
        return remote(src, dst, bs.at[k], br.at[k], other)

    sib_tokens = to_sibling(0, pair_in.at[0], sib_in.at[0])
    sib_context = to_sibling(1, pair_in.at[1], sib_in.at[1])
    sib_hid = to_sibling(2, hidden, sib_hidden)
    sib_act = to_sibling(3, active.at[:, :, pl.ds(2 * (1 - at.c), 2)], sib_active)
    sib_og = to_sibling(4, outer_grad, sib_outer)
    sib_sl = to_sibling(5, slope.at[:, pl.ds(pl.multiple_of((1 - at.c) * 1536, 128), 1536)], sib_slope)
    sib_first = to_sibling(6, stack.at[1 - at.c], sib_stack.at[0])
    sib_last = to_sibling(7, stack.at[3 - at.c], sib_stack.at[1])

    peers = [(dz, dy) for dz in range(4) for dy in range(2) if (dz, dy) != (0, 0)]

    def peer(dz, dy):
        return at.dev(z=at.far(dz), y=lax.rem(at.y + dy, 2))

    def vec_move(k, recv=False):
        dz, dy = peers[k]
        s = lax.rem(at.z + 4 - dz, 4) * 2 + lax.rem(at.y + dy, 2) if recv else me
        return remote(vec_parts.at[s], vec_parts.at[s], vs.at[k], vr.at[k], peer(dz, dy))

    def norm_move(k, recv=False):
        dz, dy = peers[k]
        s = lax.rem(at.z + 4 - dz, 4) * 2 + lax.rem(at.y + dy, 2) if recv else me
        return remote(norm_parts.at[s], norm_parts.at[s], ns.at[k], nr.at[k], peer(dz, dy))

    loads = [pltpu.make_async_copy(watt_h.at[k], norm_one.at[pl.ds(96 * k, 96)], ls.at[k]) for k in range(4)]
    loads += [
        pltpu.make_async_copy(winn_h.at[:, pl.ds(768 * k, 768)], work.at[pl.ds(96 * k, 96)], ls.at[4 + k])
        for k in range(4)
    ]
    loads += [pltpu.make_async_copy(wout_h, resid.at[pl.ds(0, 384)], ls.at[8])]
    load_tokens = pltpu.make_async_copy(tok_h, pair_in.at[0], ls.at[9])
    load_cotangent = pltpu.make_async_copy(cot_h, stack.at[3], ls.at[10])
    store_shown = pltpu.make_async_copy(shown, act_h, ls.at[11])
    store_grad = pltpu.make_async_copy(work, grad_h, ls.at[12])

    def init():
        for cp in loads:
            cp.start()
        load_tokens.start()
        load_cotangent.start()
        barrier = pltpu.get_barrier_semaphore()
        greet = [peer(dz, dy) for dz, dy in peers] + [at.dev(x=1 - at.x), other]
        for d in greet:
            pl.semaphore_signal(barrier, inc=1, device_id=d, device_id_type=MESH)
        for cp in loads:
            cp.wait()
        for i in range(2):
            k = 2 * i + at.c
            rows = pl.ds(pl.multiple_of(96 * k, 96), 96)
            att[k, at.z, at.y] = norm_one[rows, :].astype(BF16)
            inn[k, at.z, at.y] = work[rows, :].astype(BF16)
            out[at.z, at.y, k] = resid[rows, :].astype(BF16)
        vec_parts[me] = jnp.zeros((16, 128), F32)
        vec_parts[me, :12, :96] = vec_in[...]
        vec_grad[...] = jnp.zeros_like(vec_grad)
        pl.semaphore_wait(barrier, len(greet))

    def early():
        for k in range(7):
            vec_move(k).start()
        load_tokens.wait()
        sib_tokens.start()
        ids = jnp.broadcast_to(seg_row[...].astype(F32), (512, 512))
        mask[...] = jnp.where(ids.T == ids, 1.0, 0.0)

    def vectors_here():
        for k in range(7):
            vec_move(k, True).wait_recv()
        full = jnp.zeros((16, 768), F32)
        row = lax.broadcasted_iota(jnp.int32, (128, 768), 0)
        col = lax.broadcasted_iota(jnp.int32, (128, 768), 1)
        for s in range(8):
            pick = jnp.where((col == row + 96 * s) & (row < 96), 1.0, 0.0).astype(BF16)
            full = full + dot_nn(vec_parts[s].astype(BF16), pick)
        vec[...] = full

    def vrow(r):
        return vec[pl.ds(r, 1), :]

    def queries_keys():
        tokens = pair_in[0]
        stack[0] = ((dot_nn(tokens, square(att.at[0])) + vrow(0)) * 0.125).astype(BF16)
        stack[2] = dot_nn(tokens, square(att.at[1])).astype(BF16)

    def values():
        stack[1] = (dot_nn(pair_in[0], square(att.at[2])) + vrow(1)).astype(BF16)

    low = lax.broadcasted_iota(jnp.int32, (512, 128), 1) < 64

    def attend(p):
        ls_ = pl.ds(128 * p, 128)
        queries, keys = stack[0, :, ls_], stack[2, :, ls_]
        values_t = stack[1, :, ls_].T
        for h in range(2):
            mine = jnp.where(low if h == 0 else ~low, keys, jnp.zeros_like(keys))
            scores = jnp.where(mask[...] > 0.5, dot_nt(mine, queries), -1000000000.0)
            peak = jnp.max(scores, axis=0, keepdims=True)
            exponent = jnp.exp(scores - peak)
            scale = 1.0 / jnp.sum(exponent, axis=0, keepdims=True)
            weights = (exponent * scale).astype(BF16)
            probs[2 * p + h] = weights
            turn[pl.ds(128 * p + 64 * h, 64), :] = dot_nn(values_t[64 * h : 64 * h + 64], weights).astype(BF16)

    def norm_stats(value):
        centre = jnp.mean(value, axis=1, keepdims=True)
        centered = value - centre
        spread = jnp.mean(centered * centered, axis=1, keepdims=True)
        scale = lax.rsqrt(spread + EPS_NORM)
        return centered * scale, scale

    def project_out():
        pair_in[1] = turn[...].T
        sib_context.start()
        resid[...] = wide(pair_in[0]) + dot_nn(pair_in[1], square(att.at[3])) + vrow(2)
        for r in range(4):
            rows = pl.ds(128 * r, 128)
            normed, scale = norm_stats(resid[rows, :])
            norm_one[rows, :] = normed
            dev_one[rows, :] = scale
            hidden[rows, :] = (normed * vrow(3) + vrow(4)).astype(BF16)
        sib_hid.start()

    def feed_in(q):
        work[...] = dot_nn(hidden[...], square(inn.at[q])) + vrow(5 + q)
        for r in range(4):
            rows = pl.ds(128 * r, 128)
            value = work[rows, :]
            share = 0.5 * (1.0 + lax.erf(value * INV_SQRT2))
            shown[rows, :] = (value * share).astype(BF16)
            density = jnp.exp(-0.5 * value * value) * INV_SQRT2PI
            slope[rows, 768 * q : 768 * q + 768] = (share + value * density).astype(BF16)
        active[q] = shown[...].T.reshape(2, 4, 96, 512)

    def feed_out():
        sib_act.start()
        for n in range(3):
            cols = slice(256 * n, 256 * n + 256)
            value = norm_one[:, cols] * vec[3:4, cols] + vec[4:5, cols] + vec[9:10, cols]
            for q in range(4):
                value = value + dot_tn(
                    active[q].reshape(768, 512), out[q, :, :, :, cols].reshape(768, 256)
                )
            resid[:, cols] = value

    def end_norm():
        load_cotangent.wait()
        sums = [jnp.zeros((1, 768), F32) for _ in range(3)]
        for r in range(4):
            rows = pl.ds(128 * r, 128)
            normed, scale = norm_stats(resid[rows, :])
            shown[rows, :] = (normed * vrow(10) + vrow(11)).astype(BF16)
            given = wide(stack[3, rows, :])
            scaled = given * vrow(10)
            back = scale * (
                scaled
                - jnp.mean(scaled, axis=1, keepdims=True)
                - normed * jnp.mean(scaled * normed, axis=1, keepdims=True)
            )
            work[rows, :] = back
            low_back = back.astype(BF16)
            outer_grad[rows, :] = low_back
            for k, term in enumerate((wide(low_back), given * normed, given)):
                sums[k] = sums[k] + jnp.sum(term, axis=0, keepdims=True)
        for k in range(3):
            vec_grad[9 + k : 10 + k, :] = sums[k]
        sib_og.start()
        store_shown.start()

    def inner_back(q):
        cols = slice(768 * q, 768 * q + 768)
        resid[...] = dot_nt(outer_grad[...], out[q].reshape(768, 768))
        total_row = jnp.zeros((1, 768), F32)
        for r in range(4):
            rows = pl.ds(128 * r, 128)
            value = (resid[rows, :] * wide(slope[rows, cols])).astype(BF16)
            slope[rows, cols] = value
            total_row = total_row + jnp.sum(wide(value), axis=0, keepdims=True)
        vec_grad[5 + q : 6 + q, :] = total_row
        if q == 3:
            sib_sl.start()

    def put_chunk(j, value):
        value = value.astype(BF16).reshape(4, 2, 96, 768)
        if j < 2:
            grad_out[j] = value
        else:
            out[:, :, j - 2] = value

    def chunk_out(j):
        if j == 0:
            sib_act.wait_recv()
            sib_og.wait_recv()
        mine = active[:, :, pl.ds(2 * at.c + j, 1)].reshape(768, 512)
        theirs = sib_active[:, :, j].reshape(768, 512)
        put_chunk(j, dot_nn(mine, outer_grad[...]) + dot_nn(theirs, sib_outer[...]))

    def chunk_in(j):
        if j == 2:
            sib_hid.wait_recv()
            sib_sl.wait_recv()
        cols = pl.ds(pl.multiple_of(at.c * 1536 + 768 * (j - 2), 128), 768)
        put_chunk(
            j,
            dot_tn(hidden[...], slope[:, cols])
            + dot_tn(sib_hidden[...], sib_slope[:, 768 * (j - 2) : 768 * (j - 1)]),
        )

    def chunk_attention(j):
        if j == 4:
            sib_tokens.wait_recv()
            sib_first.wait_recv()
            value = dot_tn(pair_in[0], stack[at.c]) + dot_tn(sib_in[0], sib_stack[0])
            put_chunk(j, value * jnp.where(at.c == 0, 0.125, 1.0))
        else:
            sib_context.wait_recv()
            sib_last.wait_recv()
            put_chunk(j, dot_tn(pair_in[at.c], stack[2 + at.c]) + dot_tn(sib_in[at.c], sib_stack[1]))

    def hidden_back(q):
        work[...] += dot_nt(slope[:, 768 * q : 768 * q + 768], square(inn.at[q]))

    def middle_norm():
        sums = [jnp.zeros((1, 768), F32) for _ in range(3)]
        for r in range(4):
            rows = pl.ds(128 * r, 128)
            given = work[rows, :]
            normed = norm_one[rows, :]
            scaled = given * vrow(3)
            back = dev_one[rows, :] * (
                scaled
                - jnp.mean(scaled, axis=1, keepdims=True)
                - normed * jnp.mean(scaled * normed, axis=1, keepdims=True)
            )
            work[rows, :] = back
            low_back = back.astype(BF16)
            stack[3, rows, :] = low_back
            for k, term in enumerate((wide(low_back), given * normed, given)):
                sums[k] = sums[k] + jnp.sum(term, axis=0, keepdims=True)
        for k in range(3):
            vec_grad[2 + k : 3 + k, :] = sums[k]

    def context_back():
        store_shown.wait()
        shown[...] = dot_nt(stack[3], square(att.at[3])).astype(BF16)

    def attend_back(p):
        ls_ = pl.ds(128 * p, 128)
        queries, keys, vals, given = stack[0, :, ls_], stack[2, :, ls_], stack[1, :, ls_], shown[:, ls_]
        keys_t = keys.T
        value_grads, key_grads = [], []
        for h in range(2):
            mine = jnp.where(low if h == 0 else ~low, vals, jnp.zeros_like(vals))
            prob_grad = dot_nt(mine, given)
            weights = probs[2 * p + h]
            wide_weights = wide(weights)
            delta = jnp.sum(prob_grad * wide_weights, axis=0, keepdims=True)
            score_grad = (wide_weights * (prob_grad - delta)).astype(BF16)
            value_grads.append(dot_nn(weights, given))
            key_grads.append(dot_nn(score_grad, queries))
            turn[pl.ds(128 * p + 64 * h, 64), :] = dot_nn(keys_t[64 * h : 64 * h + 64], score_grad).astype(BF16)
        stack[1, :, ls_] = jnp.where(low, value_grads[0], value_grads[1]).astype(BF16)
        stack[2, :, ls_] = jnp.where(low, key_grads[0], key_grads[1]).astype(BF16)

    def queries_back():
        stack[0] = turn[...].T
        sib_first.start()
        sib_last.start()
        vec_grad[0:1, :] = 0.125 * jnp.sum(wide(stack[0]), axis=0, keepdims=True)
        vec_grad[1:2, :] = jnp.sum(wide(stack[1]), axis=0, keepdims=True)

    def input_back():
        work[...] += (
            0.125 * dot_nt(stack[0], square(att.at[0]))
            + dot_nt(stack[2], square(att.at[1]))
            + dot_nt(stack[1], square(att.at[2]))
        )
        store_grad.start()

    def vec_sum(k):
        if k == 0:
            return remote(vec_grad, vec_sib, ws.at[0], wr.at[0], other)
        if k == 1:
            return remote(vec_grad, vec_x, ws.at[1], wr.at[1], at.dev(x=1 - at.x))
        if k == 2:
            return remote(vec_grad, vec_y, ws.at[2], wr.at[2], at.dev(y=1 - at.y))
        return remote(vec_z.at[at.z], vec_z.at[at.z], ws.at[k], wr.at[k], at.dev(z=at.far(k - 2)))

    def vec_sum_recv(k):
        s = lax.rem(at.z + 4 - (k - 2), 4)
        return remote(vec_z.at[s], vec_z.at[s], ws.at[k], wr.at[k], at.dev(z=at.far(k - 2)))

    def vec_step(k):
        if k == 0:
            vec_sum(0).start()
        elif k <= 2:
            vec_sum(k - 1).wait()
            vec_grad[...] += (vec_sib if k == 1 else vec_x)[...]
            vec_sum(k).start()
        elif k == 3:
            vec_sum(2).wait()
            vec_z[at.z] = vec_grad[...] + vec_y[...]
            for m in (3, 4, 5):
                vec_sum(m).start()
        else:
            for m in (3, 4, 5):
                vec_sum_recv(m).wait_recv()
                vec_sum(m).wait_send()
            vec_grad[...] = (vec_z[0] + vec_z[1]) + (vec_z[2] + vec_z[3])

    def squares():
        part = jnp.zeros((96, 768), F32)
        for b in range(12):
            value = wide(total[b])
            part = part + value * value
        norm_parts[me] = jnp.full((8, 128), jnp.sum(part), F32)
        for k in range(7):
            norm_move(k).start()
        own = jnp.sum(vec_grad[...] * vec_grad[...])
        for k in range(7):
            norm_move(k, True).wait_recv()
        sums = norm_parts[0]
        for s in range(1, 8):
            sums = sums + norm_parts[s]
        norm[...] = sums + own

    def finish():
        for k in range(7):
            vec_move(k).wait_send()
            norm_move(k).wait_send()
        for cp in (sib_tokens, sib_context, sib_hid, sib_act, sib_og, sib_sl, sib_first, sib_last):
            cp.wait_send()
        store_grad.wait()
        rd.finish()

    run = {
        "init": init, "early": early, "vec": vectors_here, "qk": queries_keys, "v": values, "wo": project_out,
        "out": feed_out, "ln2": end_norm, "ln1": middle_norm, "dc": context_back, "dq": queries_back,
        "ig": input_back, "sq": squares, "fin": finish, "agf": ag.finish,
    }
    steps = {
        "at": attend, "ab": attend_back, "F": feed_in, "D": inner_back, "H": hidden_back, "V": vec_step,
        "G": lambda j: (chunk_out, chunk_in, chunk_attention)[j // 2](j),
        "s1": rd.s1, "r1": rd.r1, "s4": rd.s4, "s5": rd.s5, "s6": rd.s6,
        "zown": ag.zown, "yown": ag.yown, "f": ag.join, "g": ag.have,
    }
    for k in range(4):
        steps[f"p{k}"] = functools.partial(rd.p, dz=k)
        steps[f"q{k}"] = functools.partial(rd.q, dz=k)
        steps[f"a{k}"] = functools.partial(ag.arrive, s=k)
        steps[f"t{k}"] = functools.partial(ag.across, s=k)
    for name, index in order:
        if name in run:
            run[name]()
        else:
            steps[name](index)


def whole_layer(tokens, cotangent, segments, watt, winn, wout, vectors_low, order, alpha_gather, alpha_scatter):
    na = max(1, sum(alpha_scatter))
    nb = max(1, CHUNKS - sum(alpha_scatter))
    vmem, dma = pltpu.VMEM, pltpu.SemaphoreType.DMA
    flat = (512, 768)
    scratch = [
        vmem((4, 4, 2, 96, 768), BF16), vmem((4, 4, 2, 96, 768), BF16), vmem((4, 2, 4, 96, 768), BF16),
        vmem(flat, F32), vmem(flat, F32), vmem(flat, F32),
        vmem((2,) + flat, BF16), vmem((4,) + flat, BF16), vmem(flat, BF16), vmem(flat, BF16), vmem(flat, BF16),
        vmem((768, 512), BF16), vmem((8, 128), BF16),
        vmem((4, 2, 4, 96, 512), BF16), vmem((512, 3072), BF16), vmem((12, 512, 512), BF16),
        vmem((512, 512), F32), vmem((16, 768), F32), vmem((512, 1), F32), vmem((8, 128), F32),
        vmem((2,) + flat, BF16), vmem(flat, BF16), vmem((4, 2, 2, 96, 512), BF16), vmem(flat, BF16),
        vmem((512, 1536), BF16), vmem((2,) + flat, BF16),
        vmem((2, 4, 2, 96, 768), BF16),
        vmem((na, 4, 2, 96, 384), BF16), vmem((na, 4, 96, 384), BF16), vmem((na, 3, 96, 384), BF16),
        vmem((nb, 4, 96, 768), BF16), vmem((nb, 3, 96, 768), BF16), vmem((nb, 96, 768), BF16),
        vmem((8, 16, 128), F32), vmem((16, 768), F32), vmem((16, 768), F32), vmem((16, 768), F32),
        vmem((4, 16, 768), F32), vmem((8, 8, 128), F32),
    ]
    for n in ((BLOCKS, 6), (BLOCKS, 4), (BLOCKS, 8), (BLOCKS,), (CHUNKS, 17), (8,), (7,), (6,), (7,)):
        scratch += [dma(n), dma(n)]
    scratch += [dma((13,))]
    local, far = pl.BlockSpec(memory_space=pltpu.VMEM), pl.BlockSpec(memory_space=pl.ANY)
    return pl.pallas_call(
        functools.partial(layer_kernel, order, alpha_gather, alpha_scatter),
        out_shape=[
            jax.ShapeDtypeStruct(flat, BF16), jax.ShapeDtypeStruct(flat, F32),
            jax.ShapeDtypeStruct((12, 96, 768), BF16), jax.ShapeDtypeStruct((16, 768), F32),
            jax.ShapeDtypeStruct((8, 128), F32),
        ],
        in_specs=[far, far, local, far, far, far, local],
        out_specs=[far, far, local, local, local],
        scratch_shapes=scratch,
        compiler_params=pltpu.CompilerParams(
            collective_id=0, has_side_effects=True, vmem_limit_bytes=63 * 2**20
        ),
        name="layer",
    )(
        tokens, cotangent, segments.reshape(1, 512), watt, winn, wout, vectors_low
    )


def adam_kernel(
    act_ref, back_ref, norm_ref, vec_ref, grad_att, grad_inn, grad_out,
    att_w, att_m, att_v, inn_w, inn_m, inn_v, out_w, out_m, out_v, vec_w, vec_m, vec_v,
    act_new, back_new, norm_new, att_wn, att_mn, att_vn, inn_wn, inn_mn, inn_vn, out_wn, out_mn, out_vn,
    vec_wn, vec_mn, vec_vn, vec_gn,
):
    act_new[...] = act_ref[...]
    back_new[...] = back_ref[...]
    length = jnp.sqrt(norm_ref[0:1, 0:1])
    factor = CLIP / (length + 1e-06)
    for grad, old, new in (
        (grad_att, (att_w, att_m, att_v), (att_wn, att_mn, att_vn)),
        (grad_inn, (inn_w, inn_m, inn_v), (inn_wn, inn_mn, inn_vn)),
        (grad_out, (out_w, out_m, out_v), (out_wn, out_mn, out_vn)),
    ):
        shape = old[0].shape
        found = adam_update(
            *(ref[...].reshape(96, 768) for ref in old), grad[...].reshape(96, 768).astype(F32), factor, RATE_MATRIX
        )
        for ref, value in zip(new, found):
            ref[...] = value.reshape(shape)

    @pl.when(pl.program_id(0) == 0)
    def _():
        norm_new[...] = length
        shard = vec_w.shape[1]
        own = lax.axis_index("fsdp")
        grad = jnp.zeros(vec_w.shape, F32)
        for s in range(8):
            grad = grad + jnp.where(own == s, vec_ref[:12, shard * s : shard * s + shard], 0.0)
        found = adam_update(vec_w[...], vec_m[...], vec_v[...], grad, factor, RATE_VECTOR)
        for ref, value in zip((vec_wn, vec_mn, vec_vn), found):
            ref[...] = value
        vec_gn[...] = grad * factor


def adam_step(activations, input_grad, norm, vec_grad, total, att, inn, out, vec):
    def whole(a):
        return pl.BlockSpec(a.shape, lambda k: (0,) * a.ndim)

    def grads(first):
        return pl.BlockSpec((1, 96, 768), lambda k: (first + k, 0, 0))

    att_spec = pl.BlockSpec((1, 96, 768), lambda k: (k, 0, 0))
    inn_spec = pl.BlockSpec((96, 768), lambda k: (0, k))
    out_spec = pl.BlockSpec((96, 768), lambda k: (k, 0))
    vec_spec = whole(vec[0])
    rows = pl.BlockSpec((128, 768), lambda k: (k, 0))
    one = pl.BlockSpec((1, 1), lambda k: (0, 0))
    like = [jax.ShapeDtypeStruct(a.shape, F32) for a in (*att, *inn, *out, *vec, vec[0])]
    return pl.pallas_call(
        adam_kernel,
        grid=(4,),
        out_shape=[
            jax.ShapeDtypeStruct(activations.shape, BF16), jax.ShapeDtypeStruct(input_grad.shape, F32),
            jax.ShapeDtypeStruct((1, 1), F32), *like,
        ],
        in_specs=[
            rows, rows,
            whole(norm), whole(vec_grad), grads(8), grads(4), grads(0),
            *[att_spec] * 3, *[inn_spec] * 3, *[out_spec] * 3, *[vec_spec] * 3,
        ],
        out_specs=[rows, rows, one, *[att_spec] * 3, *[inn_spec] * 3, *[out_spec] * 3, *[vec_spec] * 4],
        compiler_params=pltpu.CompilerParams(vmem_limit_bytes=63 * 2**20),
        name="adam",
    )(activations, input_grad, norm, vec_grad, total, total, total, *att, *inn, *out, *vec)


ALPHA_GATHER = (1, 1, 0, 1, 1, 0)
ALPHA_SCATTER = (0, 1, 0, 1, 0, 1)
ORDER = (
    ("init", 0), ("yown", 0), ("zown", 0), ("yown", 1), ("yown", 2), ("zown", 1), ("early", 0), ("t0", 0),
    ("a0", 0), ("a0", 1), ("zown", 2), ("t0", 1), ("a1", 0), ("zown", 3), ("yown", 3), ("t1", 0), ("a1", 1),
    ("a0", 2), ("t1", 1), ("t2", 0), ("zown", 4), ("t2", 1), ("a2", 0), ("a2", 1), ("yown", 4), ("a0", 3),
    ("t3", 0), ("yown", 5), ("t3", 1), ("t0", 3), ("zown", 5), ("a1", 3), ("a1", 2), ("f", 0), ("f", 1),
    ("g", 0), ("a0", 4), ("a2", 3), ("vec", 0), ("qk", 0), ("t1", 3), ("g", 1), ("t0", 2), ("v", 0),
    ("a1", 4), ("at", 0), ("t1", 2), ("at", 1), ("t2", 3), ("a2", 2), ("a0", 5), ("t2", 2), ("at", 2),
    ("t3", 3), ("a2", 4), ("at", 3), ("t3", 2), ("t0", 4), ("f", 2), ("a1", 5), ("at", 4), ("t1", 4),
    ("f", 3), ("t0", 5), ("at", 5), ("t2", 4), ("wo", 0), ("t3", 4), ("g", 2), ("g", 3), ("a2", 5), ("F", 2),
    ("F", 3), ("f", 4), ("t1", 5), ("F", 0), ("t2", 5), ("t3", 5), ("f", 5), ("g", 4), ("F", 1), ("g", 5),
    ("out", 0), ("ln2", 0), ("D", 0), ("G", 0), ("s1", 0), ("r1", 0), ("p2", 0), ("G", 1), ("D", 1),
    ("p1", 0), ("s1", 1), ("p3", 0), ("D", 2), ("agf", 0), ("q2", 0), ("D", 3), ("r1", 1), ("H", 0), ("H", 1),
    ("G", 2), ("s1", 2), ("q1", 0), ("H", 2), ("p2", 2), ("G", 3), ("q3", 0), ("H", 3), ("p3", 2), ("r1", 2),
    ("p3", 1), ("ln1", 0), ("q2", 2), ("dc", 0), ("ab", 0), ("ab", 1), ("s1", 3), ("ab", 2), ("r1", 3),
    ("p1", 2), ("p1", 1), ("q1", 2), ("p2", 1), ("ab", 3), ("q3", 2), ("p0", 0), ("p0", 2), ("ab", 4),
    ("p2", 3), ("p0", 1), ("q3", 1), ("ab", 5), ("dq", 0), ("p1", 3), ("p0", 3), ("p3", 3), ("V", 0),
    ("q2", 1), ("G", 4), ("q2", 3), ("s1", 4), ("q0", 1), ("p3", 4), ("G", 5), ("q1", 3), ("p0", 4),
    ("s1", 5), ("r1", 5), ("q3", 3), ("p2", 4), ("q1", 1), ("V", 1), ("r1", 4), ("p1", 4), ("p2", 5),
    ("V", 2), ("q0", 2), ("q0", 3), ("q2", 4), ("p3", 5), ("s4", 2), ("s4", 3), ("V", 3), ("q1", 4),
    ("q3", 4), ("p1", 5), ("p0", 5), ("ig", 0), ("q3", 5), ("V", 4), ("q0", 0), ("s4", 0), ("s4", 1),
    ("q0", 4), ("q1", 5), ("q2", 5), ("q0", 5), ("s4", 4), ("s5", 0), ("s6", 0), ("s4", 5), ("s5", 1),
    ("s5", 2), ("s5", 4), ("s5", 3), ("s6", 1), ("s6", 4), ("s5", 5), ("s6", 5), ("s6", 2), ("s6", 3),
    ("sq", 0), ("fin", 0),
)

def plain_body(
    tokens,
    segment_ids,
    cotangent,
    attention_weight,
    attention_first,
    attention_second,
    inner_weight,
    inner_first,
    inner_second,
    outer_weight,
    outer_first,
    outer_second,
    vectors,
    vector_first,
    vector_second,
):
    row_count, seq_length, model_width = tokens.shape
    token_count = row_count * seq_length
    flat_rows = tokens.reshape(token_count, model_width)
    shards = (
        attention_weight.astype(jnp.bfloat16),
        inner_weight.astype(jnp.bfloat16),
        outer_weight.astype(jnp.bfloat16),
        vectors.astype(jnp.bfloat16),
    )
    attention_full, inner_full, outer_full, vector_full = (
        lax.all_gather(shards[0], "fsdp", axis=1, tiled=True),
        lax.all_gather(shards[1], "fsdp", axis=0, tiled=True),
        lax.all_gather(shards[2], "fsdp", axis=0, tiled=True),
        lax.all_gather(shards[3], "fsdp", axis=1, tiled=True),
    )
    vector_rows = vector_full.astype(jnp.float32)
    bias_query = vector_rows[0]
    bias_value = vector_rows[1]
    bias_output = vector_rows[2]
    gain_one = vector_rows[3]
    shift_one = vector_rows[4]
    bias_inner = vector_rows[5:9].reshape(-1)
    bias_outer = vector_rows[9]
    gain_two = vector_rows[10]
    shift_two = vector_rows[11]
    projected = jnp.einsum(
        "td,kde->kte", flat_rows, attention_full[:3], preferred_element_type=jnp.float32
    )
    queries = ((projected[0] + bias_query) * 0.125).astype(jnp.bfloat16)
    key_rows = projected[1].astype(jnp.bfloat16)
    value_rows = (projected[2] + bias_value).astype(jnp.bfloat16)
    row_view = (row_count, seq_length, model_width)
    query_view = queries.reshape(row_view)
    key_view = key_rows.reshape(row_view)
    value_view = value_rows.reshape(row_view)
    context, log_totals = lax.map(attend_row, (query_view, key_view, value_view, segment_ids))
    context_flat = context.reshape(token_count, model_width)
    attention_out = (
        jnp.dot(context_flat, attention_full[3], preferred_element_type=jnp.float32) + bias_output
    )
    sum_one = flat_rows.astype(jnp.float32) + attention_out
    hidden_one, norm_one_back = jax.vjp(layer_norm, sum_one, gain_one, shift_one)
    hidden_low = hidden_one.astype(jnp.bfloat16)
    inner_pre = jnp.dot(hidden_low, inner_full, preferred_element_type=jnp.float32) + bias_inner
    activated, gelu_back = jax.vjp(gelu_exact, inner_pre)
    activated_low = activated.astype(jnp.bfloat16)
    outer_pre = jnp.dot(activated_low, outer_full, preferred_element_type=jnp.float32) + bias_outer
    sum_two = hidden_one + outer_pre
    output, norm_two_back = jax.vjp(layer_norm, sum_two, gain_two, shift_two)
    activations = output.astype(jnp.bfloat16).reshape(row_view)
    attention_back, inner_back, outer_back = (
        lax.all_gather(shards[0], "fsdp", axis=1, tiled=True),
        lax.all_gather(shards[1], "fsdp", axis=0, tiled=True),
        lax.all_gather(shards[2], "fsdp", axis=0, tiled=True),
    )
    output_grad = cotangent.reshape(token_count, model_width).astype(jnp.float32)
    sum_two_grad, gain_two_grad, shift_two_grad = norm_two_back(output_grad)
    outer_grad = sum_two_grad.astype(jnp.bfloat16)
    outer_weight_grad = jnp.einsum(
        "tf,td->fd", activated_low, outer_grad, preferred_element_type=jnp.float32
    )
    bias_outer_grad = jnp.sum(outer_grad.astype(jnp.float32), axis=0)
    activated_grad = jnp.einsum(
        "td,fd->tf", outer_grad, outer_back, preferred_element_type=jnp.float32
    )
    (inner_raw_grad,) = gelu_back(activated_grad)
    inner_grad = inner_raw_grad.astype(jnp.bfloat16)
    inner_weight_grad = jnp.einsum(
        "td,tf->df", hidden_low, inner_grad, preferred_element_type=jnp.float32
    )
    bias_inner_grad = jnp.sum(inner_grad.astype(jnp.float32), axis=0)
    hidden_one_grad = sum_two_grad + jnp.einsum(
        "tf,df->td", inner_grad, inner_back, preferred_element_type=jnp.float32
    )
    sum_one_grad, gain_one_grad, shift_one_grad = norm_one_back(hidden_one_grad)
    attention_grad = sum_one_grad.astype(jnp.bfloat16)
    output_weight_grad = jnp.einsum(
        "td,te->de", context_flat, attention_grad, preferred_element_type=jnp.float32
    )
    bias_output_grad = jnp.sum(attention_grad.astype(jnp.float32), axis=0)
    context_grad = jnp.einsum(
        "te,de->td", attention_grad, attention_back[3], preferred_element_type=jnp.float32
    ).astype(jnp.bfloat16)
    query_grad, key_grad, value_grad = lax.map(
        attend_back,
        (query_view, key_view, value_view, segment_ids, log_totals, context_grad.reshape(row_view)),
    )
    query_grad = query_grad.reshape(token_count, model_width)
    key_grad = key_grad.reshape(token_count, model_width)
    value_grad = value_grad.reshape(token_count, model_width)
    grad_stack = jnp.stack([query_grad, key_grad, value_grad])
    projection_grad = jnp.einsum(
        "td,kte->kde", flat_rows, grad_stack, preferred_element_type=jnp.float32
    )
    projection_grad = projection_grad * jnp.array([0.125, 1.0, 1.0], jnp.float32)[:, None, None]
    attention_weight_grad = jnp.concatenate([projection_grad, output_weight_grad[None]], axis=0)
    bias_query_grad = 0.125 * jnp.sum(query_grad.astype(jnp.float32), axis=0)
    bias_value_grad = jnp.sum(value_grad.astype(jnp.float32), axis=0)
    token_grad = sum_one_grad + 0.125 * jnp.einsum(
        "te,de->td", query_grad, attention_back[0], preferred_element_type=jnp.float32
    )
    token_grad = token_grad + jnp.einsum(
        "kte,kde->td", grad_stack[1:], attention_back[1:3], preferred_element_type=jnp.float32
    )
    input_grad = token_grad.reshape(row_view)
    vector_grad = jnp.concatenate(
        [
            jnp.stack(
                [bias_query_grad, bias_value_grad, bias_output_grad, gain_one_grad, shift_one_grad]
            ),
            bias_inner_grad.reshape(4, model_width),
            jnp.stack([bias_outer_grad, gain_two_grad, shift_two_grad]),
        ],
        axis=0,
    )
    shard_grads = (
        lax.psum_scatter(
            attention_weight_grad.astype(jnp.bfloat16), "fsdp", scatter_dimension=1, tiled=True
        ).astype(jnp.float32),
        lax.psum_scatter(
            inner_weight_grad.astype(jnp.bfloat16), "fsdp", scatter_dimension=0, tiled=True
        ).astype(jnp.float32),
        lax.psum_scatter(
            outer_weight_grad.astype(jnp.bfloat16), "fsdp", scatter_dimension=0, tiled=True
        ).astype(jnp.float32),
        lax.psum_scatter(
            vector_grad.astype(jnp.bfloat16), "fsdp", scatter_dimension=1, tiled=True
        ).astype(jnp.float32),
    )
    summed = (
        lax.psum(shard_grads[0].astype(jnp.bfloat16), "dp").astype(jnp.float32),
        lax.psum(shard_grads[1].astype(jnp.bfloat16), "dp").astype(jnp.float32),
        lax.psum(shard_grads[2].astype(jnp.bfloat16), "dp").astype(jnp.float32),
        lax.psum(shard_grads[3].astype(jnp.bfloat16), "dp").astype(jnp.float32),
    )
    local_squares = (
        jnp.sum(summed[0] * summed[0])
        + jnp.sum(summed[1] * summed[1])
        + jnp.sum(summed[2] * summed[2])
        + jnp.sum(summed[3] * summed[3])
    )
    total_squares = lax.psum(local_squares, "fsdp")
    grad_norm = jnp.sqrt(total_squares)
    factor = CLIP / (grad_norm + 1e-06)
    attention_new, attention_first_new, attention_second_new = adam_update(
        attention_weight, attention_first, attention_second, summed[0], factor, RATE_MATRIX
    )
    inner_new, inner_first_new, inner_second_new = adam_update(
        inner_weight, inner_first, inner_second, summed[1], factor, RATE_MATRIX
    )
    outer_new, outer_first_new, outer_second_new = adam_update(
        outer_weight, outer_first, outer_second, summed[2], factor, RATE_MATRIX
    )
    vectors_new, vector_first_new, vector_second_new = adam_update(
        vectors, vector_first, vector_second, summed[3], factor, RATE_VECTOR
    )
    clipped_vectors = summed[3] * factor
    return (
        activations,
        input_grad,
        grad_norm,
        attention_new,
        attention_first_new,
        attention_second_new,
        inner_new,
        inner_first_new,
        inner_second_new,
        outer_new,
        outer_first_new,
        outer_second_new,
        vectors_new,
        vector_first_new,
        vector_second_new,
        clipped_vectors,
    )


def fused_body(
    tokens,
    segment_ids,
    cotangent,
    attention_weight,
    attention_first,
    attention_second,
    inner_weight,
    inner_first,
    inner_second,
    outer_weight,
    outer_first,
    outer_second,
    vectors,
    vector_first,
    vector_second,
):
    _, seq_length, model_width = tokens.shape
    activations, input_grad, total, vec_grad, norm = whole_layer(
        tokens.reshape(seq_length, model_width),
        cotangent.reshape(seq_length, model_width),
        segment_ids,
        attention_weight,
        inner_weight,
        outer_weight,
        vectors,
        ORDER,
        ALPHA_GATHER,
        ALPHA_SCATTER,
    )
    found = adam_step(
        activations,
        input_grad,
        norm,
        vec_grad,
        total,
        (attention_weight, attention_first, attention_second),
        (inner_weight, inner_first, inner_second),
        (outer_weight, outer_first, outer_second),
        (vectors, vector_first, vector_second),
    )
    return (found[0][None], found[1][None], found[2].reshape(()), *found[3:])


def solution(mesh):
    placed = (
        P(("dp", "fsdp"), None, None),
        P(("dp", "fsdp"), None),
        P(("dp", "fsdp"), None, None),
        P(None, "fsdp", None),
        P(None, "fsdp", None),
        P(None, "fsdp", None),
        P("fsdp", None),
        P("fsdp", None),
        P("fsdp", None),
        P("fsdp", None),
        P("fsdp", None),
        P("fsdp", None),
        P(None, "fsdp"),
        P(None, "fsdp"),
        P(None, "fsdp"),
    )
    fused = mesh.shape["dp"] == 4 and mesh.shape["fsdp"] == 8
    return jax.shard_map(
        fused_body if fused else plain_body,
        mesh=mesh,
        in_specs=placed,
        out_specs=(
            P(("dp", "fsdp"), None, None),
            P(("dp", "fsdp"), None, None),
            P(),
            P(None, "fsdp", None),
            P(None, "fsdp", None),
            P(None, "fsdp", None),
            P("fsdp", None),
            P("fsdp", None),
            P("fsdp", None),
            P("fsdp", None),
            P("fsdp", None),
            P("fsdp", None),
            P(None, "fsdp"),
            P(None, "fsdp"),
            P(None, "fsdp"),
            P(None, "fsdp"),
        ),
        check_vma=False,
    )
```

```python
import functools

import jax
import jax.numpy as jnp
from jax import lax
from jax.experimental import pallas as pl
from jax.experimental.pallas import tpu as pltpu
from jax.sharding import PartitionSpec as P

HEADS = 12
STEP = 10


EPS_NORM = 1e-12
BETA_ONE = 0.9
BETA_TWO = 0.999
ADAM_EPS = 1e-08
DECAY = 0.01
RATE_MATRIX = 0.03
RATE_VECTOR = 0.5
CLIP = 1.0


def layer_norm(resid, gain, shift):
    centre = jnp.mean(resid, axis=-1, keepdims=True)
    centered = resid - centre
    spread = jnp.mean(centered * centered, axis=-1, keepdims=True)
    return centered * lax.rsqrt(spread + EPS_NORM) * gain + shift


def gelu_exact(values):
    return jax.nn.gelu(values, approximate=False)


def split_heads(matrix):
    return matrix.reshape(matrix.shape[0], HEADS, matrix.shape[1] // HEADS)


def row_scores(query_row, key_row, segment_row):
    scores = jnp.einsum(
        "qhe,khe->hqk",
        split_heads(query_row),
        split_heads(key_row),
        preferred_element_type=jnp.float32,
    )
    same_segment = segment_row[:, None] == segment_row[None, :]
    return jnp.where(same_segment[None], scores, -1000000000.0)


def attend_row(pieces):
    query_row, key_row, value_row, segment_row = pieces
    scores = row_scores(query_row, key_row, segment_row)
    row_peak = jnp.max(scores, axis=-1, keepdims=True)
    exponent = jnp.exp(scores - row_peak)
    row_total = jnp.sum(exponent, axis=-1, keepdims=True)
    softmax_rows = exponent / row_total
    mixture = jnp.einsum(
        "hqk,khe->qhe",
        softmax_rows.astype(jnp.bfloat16),
        split_heads(value_row),
        preferred_element_type=jnp.float32,
    )
    return (mixture.reshape(query_row.shape).astype(jnp.bfloat16), row_peak + jnp.log(row_total))


def attend_back(pieces):
    query_row, key_row, value_row, segment_row, log_total, context_grad = pieces
    row_shape = query_row.shape
    scores = row_scores(query_row, key_row, segment_row)
    softmax_rows = jnp.exp(scores - log_total)
    grad_heads = split_heads(context_grad)
    prob_grad = jnp.einsum(
        "qhe,khe->hqk", grad_heads, split_heads(value_row), preferred_element_type=jnp.float32
    )
    value_grad = jnp.einsum(
        "hqk,qhe->khe",
        softmax_rows.astype(jnp.bfloat16),
        grad_heads,
        preferred_element_type=jnp.float32,
    )
    row_delta = jnp.sum(prob_grad * softmax_rows, axis=-1, keepdims=True)
    score_grad = (softmax_rows * (prob_grad - row_delta)).astype(jnp.bfloat16)
    query_grad = jnp.einsum(
        "hqk,khe->qhe", score_grad, split_heads(key_row), preferred_element_type=jnp.float32
    )
    key_grad = jnp.einsum(
        "hqk,qhe->khe", score_grad, split_heads(query_row), preferred_element_type=jnp.float32
    )
    return (
        query_grad.reshape(row_shape).astype(jnp.bfloat16),
        key_grad.reshape(row_shape).astype(jnp.bfloat16),
        value_grad.reshape(row_shape).astype(jnp.bfloat16),
    )


def adam_update(weight, first, second, gradient, factor, rate):
    clipped = gradient * factor
    first_new = BETA_ONE * first + (1.0 - BETA_ONE) * clipped
    second_new = BETA_TWO * second + (1.0 - BETA_TWO) * clipped * clipped
    first_hat = first_new / (1.0 - BETA_ONE**STEP)
    second_hat = second_new / (1.0 - BETA_TWO**STEP)
    weight_new = weight - rate * (first_hat / (jnp.sqrt(second_hat) + ADAM_EPS) + DECAY * weight)
    return (weight_new, first_new, second_new)


F32, BF16 = jnp.float32, jnp.bfloat16
MESH = pl.DeviceIdType.MESH
BLOCKS = 6
CHUNKS = 6
INV_SQRT2 = 0.7071067811865476
INV_SQRT2PI = 0.3989422804014327


def dot_nn(a, b):
    return lax.dot_general(a, b, (((1,), (0,)), ((), ())), preferred_element_type=F32)


def dot_nt(a, b):
    return lax.dot_general(a, b, (((1,), (1,)), ((), ())), preferred_element_type=F32)


def dot_tn(a, b):
    return lax.dot_general(a, b, (((0,), (0,)), ((), ())), preferred_element_type=F32)


def wide(value):
    return value.astype(F32)


class Place:
    def __init__(self):
        dp, fsdp = lax.axis_index("dp"), lax.axis_index("fsdp")
        self.x, self.c, self.z, self.y = dp // 2, dp % 2, fsdp // 2, fsdp % 2

    def dev(self, x=None, c=None, z=None, y=None):
        x = self.x if x is None else x
        c = self.c if c is None else c
        z = self.z if z is None else z
        y = self.y if y is None else y
        return (x * 2 + c, z * 2 + y)

    def far(self, dz):
        return lax.rem(self.z + dz, 4)


def half(x):
    return pl.ds(pl.multiple_of(x * 384, 128), 384)


def remote(src, dst, send, recv, dev):
    return pltpu.make_async_remote_copy(
        src_ref=src, dst_ref=dst, send_sem=send, recv_sem=recv, device_id=dev, device_id_type=MESH
    )


class Gather:
    def __init__(self, at, att, inn, out, sems, alpha):
        self.at, self.att, self.inn, self.out, self.alpha = at, att, inn, out, alpha
        self.zs, self.zr, self.ys, self.yr, self.xs, self.xr, self.cs, self.cr = sems

    def ref(self, i, z, y, x):
        c = self.at.c
        cols = slice(None) if x is None else half(x)
        if i < 2:
            return self.att.at[2 * i + c, z, y, :, cols]
        if i < 4:
            return self.inn.at[2 * (i - 2) + c, z, y, :, cols]
        return self.out.at[z, y, 2 * (i - 4) + c, :, cols]

    def whole(self, i, c):
        if i < 2:
            return self.att.at[2 * i + c]
        if i < 4:
            return self.inn.at[2 * (i - 2) + c]
        return self.out.at[:, :, 2 * (i - 4) + c]

    def zmove(self, i, s, right, sz):
        k = s if right else 3 + s
        z = self.at.z
        dest = jnp.minimum(z + 1, 3) if right else jnp.maximum(z - 1, 0)
        r = self.ref(i, sz, self.at.y, self.at.x if self.alpha[i] == 1 else None)
        return remote(r, r, self.zs.at[i, k], self.zr.at[i, k], self.at.dev(z=dest))

    def ymove(self, i, sz, recv=False):
        y = 1 - self.at.y if recv else self.at.y
        r = self.ref(i, sz, y, self.at.x if self.alpha[i] else None)
        return remote(r, r, self.ys.at[i, sz], self.yr.at[i, sz], self.at.dev(y=1 - self.at.y))

    def xmove(self, i, sz, own, recv=False):
        y = self.at.y if own else 1 - self.at.y
        x = 1 - self.at.x if recv else self.at.x
        k = sz + (0 if own else 4)
        r = self.ref(i, sz, y, x)
        return remote(r, r, self.xs.at[i, k], self.xr.at[i, k], self.at.dev(x=1 - self.at.x))

    def cmove(self, i, recv=False):
        r = self.whole(i, 1 - self.at.c if recv else self.at.c)
        return remote(r, r, self.cs.at[i], self.cr.at[i], self.at.dev(c=1 - self.at.c))

    def zown(self, i):
        z = self.at.z

        @pl.when(z < 3)
        def _():
            self.zmove(i, 0, True, z).start()

        @pl.when(z > 0)
        def _():
            self.zmove(i, 0, False, z).start()

    def yown(self, i):
        self.ymove(i, self.at.z).start()

    def arrive(self, i, s):
        z = self.at.z

        def forward(sz, right, more):
            self.zmove(i, s, right, sz).wait_recv()
            if s < 2:

                @pl.when(more)
                def _():
                    self.zmove(i, s + 1, right, sz).start()

            self.ymove(i, sz).start()
            if self.alpha[i] == 1:
                self.xmove(i, sz, True).start()

        @pl.when(z >= 1 + s)
        def _():
            forward(jnp.maximum(z - 1 - s, 0), True, z < 3)

        @pl.when(z + 1 + s <= 3)
        def _():
            forward(jnp.minimum(z + 1 + s, 3), False, z > 0)

    def across(self, i, s):
        z = self.at.z

        def one(sz):
            self.ymove(i, sz, True).wait_recv()
            if self.alpha[i]:
                self.xmove(i, sz, False).start()

        if s == 0:
            one(z)
            return

        @pl.when(z >= s)
        def _():
            one(jnp.maximum(z - s, 0))

        @pl.when(z + s <= 3)
        def _():
            one(jnp.minimum(z + s, 3))

    def join(self, i):
        if self.alpha[i]:
            for sz in range(4):
                self.xmove(i, sz, False, True).wait_recv()
                if self.alpha[i] == 1:

                    @pl.when(sz != self.at.z)
                    def _():
                        self.xmove(i, sz, True, True).wait_recv()

        self.cmove(i).start()

    def have(self, i):
        self.cmove(i, True).wait_recv()

    def finish(self):
        z = self.at.z
        for i in range(BLOCKS):
            for s in range(3):

                @pl.when((z < 3) & (z - s >= 0))
                def _():
                    self.zmove(i, s, True, jnp.maximum(z - s, 0)).wait_send()

                @pl.when((z > 0) & (z + s <= 3))
                def _():
                    self.zmove(i, s, False, jnp.minimum(z + s, 3)).wait_send()

            for sz in range(4):
                self.ymove(i, sz).wait_send()
                if self.alpha[i]:
                    self.xmove(i, sz, False).wait_send()
                if self.alpha[i] == 1:

                    @pl.when(sz != z)
                    def _():
                        self.xmove(i, sz, True).wait_send()

            self.cmove(i).wait_send()


class Scatter:
    def __init__(self, at, grad, total, bufs, sems, alpha):
        self.at, self.grad, self.total, self.alpha = at, grad, total, alpha
        self.ra1, self.ra2, self.ra3, self.rb1, self.rb2, self.rb3 = bufs
        self.ss, self.rs = sems
        self.slot = [sum(1 for q in alpha[:j] if q == alpha[j]) for j in range(CHUNKS)]

    def cp(self, j, k, src, dst, dev):
        return remote(src, dst, self.ss.at[j, k], self.rs.at[j, k], dev)

    def block(self, j, c):
        return 4 * (j // 2) + 2 * c + j % 2

    def firsts(self, j, dz, own):
        n, at = self.slot[j], self.at
        z = at.far(dz)
        if self.alpha[j]:
            y = at.y if own else 1 - at.y
            return self.cp(
                j, dz + 4 * own, self.grad(j, z, y).at[:, half(1 - at.x)], self.ra1.at[n, z, y], at.dev(x=1 - at.x)
            )
        return self.cp(j, dz, self.grad(j, z, 1 - at.y), self.rb1.at[n, z], at.dev(y=1 - at.y))

    def second(self, j, dz):
        n, at = self.slot[j], self.at
        z = at.far(dz)
        return self.cp(
            j, 8 + dz, self.grad(j, z, 1 - at.y).at[:, half(at.x)], self.ra2.at[n, z], at.dev(y=1 - at.y)
        )

    def third(self, j, dz):
        n, at = self.slot[j], self.at
        z = at.far(dz)
        src = self.grad(j, z, at.y)
        if self.alpha[j]:
            return self.cp(j, 11 + dz, src.at[:, half(at.x)], self.ra3.at[n, dz - 1], at.dev(z=z))
        return self.cp(j, 11 + dz, src, self.rb2.at[n, dz - 1], at.dev(z=z))

    def fourth(self, j, recv=False):
        n, at = self.slot[j], self.at
        if self.alpha[j]:
            r = self.total.at[self.block(j, at.c), :, half(1 - at.x if recv else at.x)]
            return self.cp(j, 15, r, r, at.dev(x=1 - at.x))
        return self.cp(j, 15, self.grad(j, at.z, at.y), self.rb3.at[n], at.dev(x=1 - at.x))

    def fifth(self, j, recv=False):
        r = self.total.at[self.block(j, 1 - self.at.c if recv else self.at.c)]
        return self.cp(j, 16, r, r, self.at.dev(c=1 - self.at.c))

    def s1(self, j):
        for dz in (2, 1, 3, 0):
            self.firsts(j, dz, 0).start()

    def r1(self, j):
        if self.alpha[j]:
            for dz in (2, 1, 3, 0):
                self.firsts(j, dz, 1).start()

    def p(self, j, dz):
        if not self.alpha[j]:
            return
        n, at = self.slot[j], self.at
        z, y, h = at.far(dz), 1 - at.y, half(at.x)
        self.firsts(j, dz, 0).wait_recv()
        r = self.grad(j, z, y)
        r[:, h] = (wide(r[:, h]) + wide(self.ra1[n, z, y])).astype(BF16)
        self.second(j, dz).start()

    def q(self, j, dz):
        n, at = self.slot[j], self.at
        z, y, h = at.far(dz), at.y, half(at.x)
        r = self.grad(j, z, y)
        if self.alpha[j]:
            self.firsts(j, dz, 1).wait_recv()
            self.second(j, dz).wait_recv()
            r[:, h] = (wide(r[:, h]) + wide(self.ra1[n, z, y]) + wide(self.ra2[n, z])).astype(BF16)
        else:
            self.firsts(j, dz, 0).wait_recv()
            r[...] = (wide(r[...]) + wide(self.rb1[n, z])).astype(BF16)
        if dz:
            self.third(j, dz).start()

    def s4(self, j):
        n, at = self.slot[j], self.at
        for dz in (1, 2, 3):
            self.third(j, dz).wait_recv()
        r = self.grad(j, at.z, at.y)
        if self.alpha[j]:
            h = half(at.x)
            total = wide(r[:, h])
            for dz in range(3):
                total = total + wide(self.ra3[n, dz])
            self.total[self.block(j, at.c), :, h] = total.astype(BF16)
        else:
            total = wide(r[...])
            for dz in range(3):
                total = total + wide(self.rb2[n, dz])
            r[...] = total.astype(BF16)
        self.fourth(j).start()

    def s5(self, j):
        n, at = self.slot[j], self.at
        self.fourth(j, True).wait_recv()
        if not self.alpha[j]:
            r = self.grad(j, at.z, at.y)
            self.total[self.block(j, at.c)] = (wide(r[...]) + wide(self.rb3[n])).astype(BF16)
        self.fifth(j).start()

    def s6(self, j):
        self.fifth(j, True).wait_recv()

    def finish(self):
        for j in range(CHUNKS):
            for dz in range(4):
                self.firsts(j, dz, 0).wait_send()
                if self.alpha[j]:
                    self.firsts(j, dz, 1).wait_send()
                    self.second(j, dz).wait_send()
                if dz:
                    self.third(j, dz).wait_send()
            self.fourth(j).wait_send()
            self.fifth(j).wait_send()


def layer_kernel(
    order, alpha_gather, alpha_scatter,
    tok_h, cot_h, seg_row, watt_h, winn_h, wout_h, vec_in,
    act_h, grad_h, total, vec_grad, norm,
    att, inn, out, norm_one, resid, work, pair_in, stack, hidden, outer_grad, shown, turn, turn_two,
    active, slope, probs, mask, vec, dev_one, dev_two,
    sib_in, sib_hidden, sib_active, sib_outer, sib_slope, sib_stack,
    grad_out, ra1, ra2, ra3, rb1, rb2, rb3,
    vec_parts, vec_sib, vec_x, vec_y, vec_z, norm_parts,
    zs, zr, ys, yr, xs, xr, cs, cr, ss, rs, bs, br, vs, vr, ws, wr, ns, nr, ls,
):
    at = Place()
    me = at.z * 2 + at.y
    ag = Gather(at, att, inn, out, (zs, zr, ys, yr, xs, xr, cs, cr), alpha_gather)

    def grad_ref(j, z, y):
        return grad_out.at[j, z, y] if j < 2 else out.at[z, y, j - 2]

    rd = Scatter(at, grad_ref, total, (ra1, ra2, ra3, rb1, rb2, rb3), (ss, rs), alpha_scatter)

    def square(ref, n=768):
        return ref[...].reshape(n, n)

    other = at.dev(c=1 - at.c)

    def to_sibling(k, src, dst):
        return remote(src, dst, bs.at[k], br.at[k], other)

    sib_tokens = to_sibling(0, pair_in.at[0], sib_in.at[0])
    sib_context = to_sibling(1, pair_in.at[1], sib_in.at[1])
    sib_hid = to_sibling(2, hidden, sib_hidden)
    sib_act = to_sibling(3, active.at[:, :, pl.ds(2 * (1 - at.c), 2)], sib_active)
    sib_og = to_sibling(4, outer_grad, sib_outer)
    sib_sl = to_sibling(5, slope.at[:, pl.ds(pl.multiple_of((1 - at.c) * 1536, 128), 1536)], sib_slope)
    sib_first = to_sibling(6, stack.at[1 - at.c], sib_stack.at[0])
    sib_last = to_sibling(7, stack.at[3 - at.c], sib_stack.at[1])

    peers = [(dz, dy) for dz in range(4) for dy in range(2) if (dz, dy) != (0, 0)]

    def peer(dz, dy):
        return at.dev(z=at.far(dz), y=lax.rem(at.y + dy, 2))

    def vec_move(k, recv=False):
        dz, dy = peers[k]
        s = lax.rem(at.z + 4 - dz, 4) * 2 + lax.rem(at.y + dy, 2) if recv else me
        return remote(vec_parts.at[s], vec_parts.at[s], vs.at[k], vr.at[k], peer(dz, dy))

    def norm_move(k, recv=False):
        dz, dy = peers[k]
        s = lax.rem(at.z + 4 - dz, 4) * 2 + lax.rem(at.y + dy, 2) if recv else me
        return remote(norm_parts.at[s], norm_parts.at[s], ns.at[k], nr.at[k], peer(dz, dy))

    loads = []
    for i in range(2):
        k, rows = 2 * i + at.c, pl.ds(96 * i, 96)
        cols, shard_rows = pl.ds(pl.multiple_of(768 * k, 128), 768), pl.ds(pl.multiple_of(96 * k, 96), 96)
        loads.append(pltpu.make_async_copy(watt_h.at[k], norm_one.at[rows], ls.at[3 * i]))
        loads.append(pltpu.make_async_copy(winn_h.at[:, cols], work.at[rows], ls.at[3 * i + 1]))
        loads.append(pltpu.make_async_copy(wout_h.at[shard_rows], resid.at[rows], ls.at[3 * i + 2]))
    load_tokens = pltpu.make_async_copy(tok_h, pair_in.at[0], ls.at[9])
    load_cotangent = pltpu.make_async_copy(cot_h, stack.at[3], ls.at[10])
    store_shown = pltpu.make_async_copy(shown, act_h, ls.at[11])
    store_grad = pltpu.make_async_copy(work, grad_h, ls.at[12])

    def init():
        for cp in loads:
            cp.start()
        load_tokens.start()
        load_cotangent.start()
        barrier = pltpu.get_barrier_semaphore()
        greet = [peer(dz, dy) for dz, dy in peers] + [at.dev(x=1 - at.x), other]
        for d in greet:
            pl.semaphore_signal(barrier, inc=1, device_id=d, device_id_type=MESH)
        for cp in loads:
            cp.wait()
        for i in range(2):
            k = 2 * i + at.c
            rows = pl.ds(96 * i, 96)
            att[k, at.z, at.y] = norm_one[rows, :].astype(BF16)
            inn[k, at.z, at.y] = work[rows, :].astype(BF16)
            out[at.z, at.y, k] = resid[rows, :].astype(BF16)
        vec_parts[me] = jnp.zeros((16, 128), F32)
        vec_parts[me, :12, :96] = vec_in[...]
        vec_grad[...] = jnp.zeros_like(vec_grad)
        pl.semaphore_wait(barrier, len(greet))

    def early():
        for k in range(7):
            vec_move(k).start()
        load_tokens.wait()
        sib_tokens.start()
        ids = jnp.broadcast_to(seg_row[...].astype(F32), (512, 512))
        mask[...] = jnp.where(ids.T == ids, 1.0, 0.0)

    def vectors_here():
        for k in range(7):
            vec_move(k, True).wait_recv()
        full = jnp.zeros((16, 768), F32)
        row = lax.broadcasted_iota(jnp.int32, (128, 768), 0)
        col = lax.broadcasted_iota(jnp.int32, (128, 768), 1)
        for s in range(8):
            pick = jnp.where((col == row + 96 * s) & (row < 96), 1.0, 0.0).astype(BF16)
            full = full + dot_nn(vec_parts[s].astype(BF16), pick)
        vec[...] = full

    def vrow(r):
        return vec[pl.ds(r, 1), :]

    def queries_keys():
        tokens = pair_in[0]
        stack[0] = ((dot_nn(tokens, square(att.at[0])) + vrow(0)) * 0.125).astype(BF16)
        stack[2] = dot_nn(tokens, square(att.at[1])).astype(BF16)

    def values():
        stack[1] = (dot_nn(pair_in[0], square(att.at[2])) + vrow(1)).astype(BF16)

    low = lax.broadcasted_iota(jnp.int32, (512, 128), 1) < 64

    def attend(p):
        ls_ = pl.ds(128 * p, 128)
        queries, keys = stack[0, :, ls_], stack[2, :, ls_]
        values_t = stack[1, :, ls_].T
        for h in range(2):
            mine = jnp.where(low if h == 0 else ~low, keys, jnp.zeros_like(keys))
            scores = jnp.where(mask[...] > 0.5, dot_nt(mine, queries), -1000000000.0)
            peak = jnp.max(scores, axis=0, keepdims=True)
            exponent = jnp.exp(scores - peak)
            scale = 1.0 / jnp.sum(exponent, axis=0, keepdims=True)
            weights = (exponent * scale).astype(BF16)
            probs[2 * p + h] = weights
            turn[pl.ds(128 * p + 64 * h, 64), :] = dot_nn(values_t[64 * h : 64 * h + 64], weights).astype(BF16)

    def norm_stats(value):
        centre = jnp.mean(value, axis=1, keepdims=True)
        centered = value - centre
        spread = jnp.mean(centered * centered, axis=1, keepdims=True)
        scale = lax.rsqrt(spread + EPS_NORM)
        return centered * scale, scale

    def project_out():
        pair_in[1] = turn[...].T
        sib_context.start()
        resid[...] = wide(pair_in[0]) + dot_nn(pair_in[1], square(att.at[3])) + vrow(2)
        for r in range(4):
            rows = pl.ds(128 * r, 128)
            normed, scale = norm_stats(resid[rows, :])
            norm_one[rows, :] = normed
            dev_one[rows, :] = scale
            hidden[rows, :] = (normed * vrow(3) + vrow(4)).astype(BF16)
        sib_hid.start()

    def feed_in(q):
        work[...] = dot_nn(hidden[...], square(inn.at[q])) + vrow(5 + q)
        for r in range(4):
            rows = pl.ds(128 * r, 128)
            value = work[rows, :]
            share = 0.5 * (1.0 + lax.erf(value * INV_SQRT2))
            shown[rows, :] = (value * share).astype(BF16)
            density = jnp.exp(-0.5 * value * value) * INV_SQRT2PI
            slope[rows, 768 * q : 768 * q + 768] = (share + value * density).astype(BF16)
        active[q] = shown[...].T.reshape(2, 4, 96, 512)

    def feed_out(part):
        if part == 4:
            sib_act.start()
            resid[...] = norm_one[...] * vrow(3) + vrow(4) + vrow(9)
        q = 2 * (part - 4)
        for n in range(3):
            cols = slice(256 * n, 256 * n + 256)
            resid[:, cols] += dot_tn(
                active[:, :, q : q + 2].reshape(1536, 512), out[:, :, q : q + 2, :, cols].reshape(1536, 256)
            )

    def end_norm():
        load_cotangent.wait()
        sums = [jnp.zeros((1, 768), F32) for _ in range(3)]
        for r in range(4):
            rows = pl.ds(128 * r, 128)
            normed, scale = norm_stats(resid[rows, :])
            shown[rows, :] = (normed * vrow(10) + vrow(11)).astype(BF16)
            given = wide(stack[3, rows, :])
            scaled = given * vrow(10)
            back = scale * (
                scaled
                - jnp.mean(scaled, axis=1, keepdims=True)
                - normed * jnp.mean(scaled * normed, axis=1, keepdims=True)
            )
            work[rows, :] = back
            low_back = back.astype(BF16)
            outer_grad[rows, :] = low_back
            for k, term in enumerate((wide(low_back), given * normed, given)):
                sums[k] = sums[k] + jnp.sum(term, axis=0, keepdims=True)
        for k in range(3):
            vec_grad[9 + k : 10 + k, :] = sums[k]
        sib_og.start()
        store_shown.start()

    def inner_back(q):
        cols = slice(768 * q, 768 * q + 768)
        resid[...] = dot_nt(outer_grad[...], out[q].reshape(768, 768))
        total_row = jnp.zeros((1, 768), F32)
        for r in range(4):
            rows = pl.ds(128 * r, 128)
            value = (resid[rows, :] * wide(slope[rows, cols])).astype(BF16)
            slope[rows, cols] = value
            total_row = total_row + jnp.sum(wide(value), axis=0, keepdims=True)
        vec_grad[5 + q : 6 + q, :] = total_row
        if q == 3:
            sib_sl.start()

    def put_chunk(j, value):
        value = value.astype(BF16).reshape(4, 2, 96, 768)
        if j < 2:
            grad_out[j] = value
        else:
            out[:, :, j - 2] = value

    def chunk_out(j):
        if j == 0:
            sib_act.wait_recv()
            sib_og.wait_recv()
        mine = active[:, :, pl.ds(2 * at.c + j, 1)].reshape(768, 512)
        theirs = sib_active[:, :, j].reshape(768, 512)
        put_chunk(j, dot_nn(mine, outer_grad[...]) + dot_nn(theirs, sib_outer[...]))

    def chunk_in(j):
        if j == 2:
            sib_hid.wait_recv()
            sib_sl.wait_recv()
        cols = pl.ds(pl.multiple_of(at.c * 1536 + 768 * (j - 2), 128), 768)
        put_chunk(
            j,
            dot_tn(hidden[...], slope[:, cols])
            + dot_tn(sib_hidden[...], sib_slope[:, 768 * (j - 2) : 768 * (j - 1)]),
        )

    def chunk_attention(j):
        if j == 4:
            sib_tokens.wait_recv()
            sib_first.wait_recv()
            value = dot_tn(pair_in[0], stack[at.c]) + dot_tn(sib_in[0], sib_stack[0])
            put_chunk(j, value * jnp.where(at.c == 0, 0.125, 1.0))
        else:
            sib_context.wait_recv()
            sib_last.wait_recv()
            put_chunk(j, dot_tn(pair_in[at.c], stack[2 + at.c]) + dot_tn(sib_in[at.c], sib_stack[1]))

    def hidden_back(q):
        work[...] += dot_nt(slope[:, 768 * q : 768 * q + 768], square(inn.at[q]))

    def middle_norm():
        sums = [jnp.zeros((1, 768), F32) for _ in range(3)]
        for r in range(4):
            rows = pl.ds(128 * r, 128)
            given = work[rows, :]
            normed = norm_one[rows, :]
            scaled = given * vrow(3)
            back = dev_one[rows, :] * (
                scaled
                - jnp.mean(scaled, axis=1, keepdims=True)
                - normed * jnp.mean(scaled * normed, axis=1, keepdims=True)
            )
            work[rows, :] = back
            low_back = back.astype(BF16)
            stack[3, rows, :] = low_back
            for k, term in enumerate((wide(low_back), given * normed, given)):
                sums[k] = sums[k] + jnp.sum(term, axis=0, keepdims=True)
        for k in range(3):
            vec_grad[2 + k : 3 + k, :] = sums[k]

    def context_back():
        store_shown.wait()
        shown[...] = dot_nt(stack[3], square(att.at[3])).astype(BF16)

    def attend_back(p):
        ls_ = pl.ds(128 * p, 128)
        queries, keys, vals, given = stack[0, :, ls_], stack[2, :, ls_], stack[1, :, ls_], shown[:, ls_]
        keys_t = keys.T
        value_grads, key_grads = [], []
        for h in range(2):
            mine = jnp.where(low if h == 0 else ~low, vals, jnp.zeros_like(vals))
            prob_grad = dot_nt(mine, given)
            weights = probs[2 * p + h]
            wide_weights = wide(weights)
            delta = jnp.sum(prob_grad * wide_weights, axis=0, keepdims=True)
            score_grad = (wide_weights * (prob_grad - delta)).astype(BF16)
            value_grads.append(dot_nn(weights, given))
            key_grads.append(dot_nn(score_grad, queries))
            turn[pl.ds(128 * p + 64 * h, 64), :] = dot_nn(keys_t[64 * h : 64 * h + 64], score_grad).astype(BF16)
        stack[1, :, ls_] = jnp.where(low, value_grads[0], value_grads[1]).astype(BF16)
        stack[2, :, ls_] = jnp.where(low, key_grads[0], key_grads[1]).astype(BF16)

    def queries_back():
        stack[0] = turn[...].T
        sib_first.start()
        sib_last.start()
        vec_grad[0:1, :] = 0.125 * jnp.sum(wide(stack[0]), axis=0, keepdims=True)
        vec_grad[1:2, :] = jnp.sum(wide(stack[1]), axis=0, keepdims=True)

    def input_back():
        work[...] += (
            0.125 * dot_nt(stack[0], square(att.at[0]))
            + dot_nt(stack[2], square(att.at[1]))
            + dot_nt(stack[1], square(att.at[2]))
        )
        store_grad.start()

    def vec_sum(k):
        if k == 0:
            return remote(vec_grad, vec_sib, ws.at[0], wr.at[0], other)
        if k == 1:
            return remote(vec_grad, vec_x, ws.at[1], wr.at[1], at.dev(x=1 - at.x))
        if k == 2:
            return remote(vec_grad, vec_y, ws.at[2], wr.at[2], at.dev(y=1 - at.y))
        return remote(vec_z.at[at.z], vec_z.at[at.z], ws.at[k], wr.at[k], at.dev(z=at.far(k - 2)))

    def vec_sum_recv(k):
        s = lax.rem(at.z + 4 - (k - 2), 4)
        return remote(vec_z.at[s], vec_z.at[s], ws.at[k], wr.at[k], at.dev(z=at.far(k - 2)))

    def vec_step(k):
        if k == 0:
            vec_sum(0).start()
        elif k <= 2:
            vec_sum(k - 1).wait()
            vec_grad[...] += (vec_sib if k == 1 else vec_x)[...]
            vec_sum(k).start()
        elif k == 3:
            vec_sum(2).wait()
            vec_z[at.z] = vec_grad[...] + vec_y[...]
            for m in (3, 4, 5):
                vec_sum(m).start()
        else:
            for m in (3, 4, 5):
                vec_sum_recv(m).wait_recv()
                vec_sum(m).wait_send()
            vec_grad[...] = (vec_z[0] + vec_z[1]) + (vec_z[2] + vec_z[3])

    def squares():
        part = jnp.zeros((96, 768), F32)
        for b in range(12):
            value = wide(total[b])
            part = part + value * value
        norm_parts[me] = jnp.full((8, 128), jnp.sum(part), F32)
        for k in range(7):
            norm_move(k).start()
        own = jnp.sum(vec_grad[...] * vec_grad[...])
        for k in range(7):
            norm_move(k, True).wait_recv()
        sums = norm_parts[0]
        for s in range(1, 8):
            sums = sums + norm_parts[s]
        norm[...] = sums + own

    def finish():
        for k in range(7):
            vec_move(k).wait_send()
            norm_move(k).wait_send()
        for cp in (sib_tokens, sib_context, sib_hid, sib_act, sib_og, sib_sl, sib_first, sib_last):
            cp.wait_send()
        store_grad.wait()
        rd.finish()

    run = {
        "init": init, "early": early, "vec": vectors_here, "qk": queries_keys, "v": values, "wo": project_out,
        "ln2": end_norm, "ln1": middle_norm, "dc": context_back, "dq": queries_back,
        "ig": input_back, "sq": squares, "fin": finish, "agf": ag.finish,
    }
    steps = {
        "at": attend, "ab": attend_back, "F": feed_in, "o": feed_out, "D": inner_back, "H": hidden_back, "V": vec_step,
        "G": lambda j: (chunk_out, chunk_in, chunk_attention)[j // 2](j),
        "s1": rd.s1, "r1": rd.r1, "s4": rd.s4, "s5": rd.s5, "s6": rd.s6,
        "zown": ag.zown, "yown": ag.yown, "f": ag.join, "g": ag.have,
    }
    for k in range(4):
        steps[f"p{k}"] = functools.partial(rd.p, dz=k)
        steps[f"q{k}"] = functools.partial(rd.q, dz=k)
        steps[f"a{k}"] = functools.partial(ag.arrive, s=k)
        steps[f"t{k}"] = functools.partial(ag.across, s=k)
    for name, index in order:
        if name in run:
            run[name]()
        else:
            steps[name](index)


def whole_layer(tokens, cotangent, segments, watt, winn, wout, vectors_low, order, alpha_gather, alpha_scatter):
    na = max(1, sum(alpha_scatter))
    nb = max(1, CHUNKS - sum(alpha_scatter))
    vmem, dma = pltpu.VMEM, pltpu.SemaphoreType.DMA
    flat = (512, 768)
    scratch = [
        vmem((4, 4, 2, 96, 768), BF16), vmem((4, 4, 2, 96, 768), BF16), vmem((4, 2, 4, 96, 768), BF16),
        vmem(flat, F32), vmem(flat, F32), vmem(flat, F32),
        vmem((2,) + flat, BF16), vmem((4,) + flat, BF16), vmem(flat, BF16), vmem(flat, BF16), vmem(flat, BF16),
        vmem((768, 512), BF16), vmem((8, 128), BF16),
        vmem((4, 2, 4, 96, 512), BF16), vmem((512, 3072), BF16), vmem((12, 512, 512), BF16),
        vmem((512, 512), F32), vmem((16, 768), F32), vmem((512, 1), F32), vmem((8, 128), F32),
        vmem((2,) + flat, BF16), vmem(flat, BF16), vmem((4, 2, 2, 96, 512), BF16), vmem(flat, BF16),
        vmem((512, 1536), BF16), vmem((2,) + flat, BF16),
        vmem((2, 4, 2, 96, 768), BF16),
        vmem((na, 4, 2, 96, 384), BF16), vmem((na, 4, 96, 384), BF16), vmem((na, 3, 96, 384), BF16),
        vmem((nb, 4, 96, 768), BF16), vmem((nb, 3, 96, 768), BF16), vmem((nb, 96, 768), BF16),
        vmem((8, 16, 128), F32), vmem((16, 768), F32), vmem((16, 768), F32), vmem((16, 768), F32),
        vmem((4, 16, 768), F32), vmem((8, 8, 128), F32),
    ]
    for n in ((BLOCKS, 6), (BLOCKS, 4), (BLOCKS, 8), (BLOCKS,), (CHUNKS, 17), (8,), (7,), (6,), (7,)):
        scratch += [dma(n), dma(n)]
    scratch += [dma((13,))]
    local, far = pl.BlockSpec(memory_space=pltpu.VMEM), pl.BlockSpec(memory_space=pl.ANY)
    return pl.pallas_call(
        functools.partial(layer_kernel, order, alpha_gather, alpha_scatter),
        out_shape=[
            jax.ShapeDtypeStruct(flat, BF16), jax.ShapeDtypeStruct(flat, F32),
            jax.ShapeDtypeStruct((12, 96, 768), BF16), jax.ShapeDtypeStruct((16, 768), F32),
            jax.ShapeDtypeStruct((8, 128), F32),
        ],
        in_specs=[far, far, local, far, far, far, local],
        out_specs=[far, far, local, local, local],
        scratch_shapes=scratch,
        compiler_params=pltpu.CompilerParams(
            collective_id=0, has_side_effects=True, vmem_limit_bytes=63 * 2**20
        ),
        name="layer",
    )(
        tokens, cotangent, segments.reshape(1, 512), watt, winn, wout, vectors_low
    )


def adam_kernel(
    act_h, back_h, total_h, norm_ref, vec_ref,
    att_w, att_m, att_v, inn_w, inn_m, inn_v, out_w, out_m, out_v, vec_w, vec_m, vec_v,
    act_new, back_new, norm_new, att_wn, att_mn, att_vn, inn_wn, inn_mn, inn_vn, out_wn, out_mn, out_vn,
    vec_wn, vec_mn, vec_vn, vec_gn,
    hold, grads, act, back, loads, stores,
):
    parts = []
    for p in range(6):
        k = 2 * (p % 2)
        rows, cols = pl.ds(96 * k, 192), pl.ds(768 * k, 1536)
        if p < 2:
            parts.append((8 + k, [[r.at[pl.ds(k, 2)] for r in (w, n)] for w, n in (
                (att_w, att_wn), (att_m, att_mn), (att_v, att_vn))]))
        elif p < 4:
            parts.append((k, [[r.at[rows] for r in (w, n)] for w, n in (
                (out_w, out_wn), (out_m, out_mn), (out_v, out_vn))]))
        else:
            parts.append((4 + k, [[r.at[:, cols] for r in (w, n)] for w, n in (
                (inn_w, inn_wn), (inn_m, inn_mn), (inn_v, inn_vn))]))

    def slot(p, m):
        if p < 2:
            return hold[0].at[p, m]
        return hold[1].at[p - 2, m] if p < 4 else hold[2].at[p - 4, m]

    def load(p, m):
        return pltpu.make_async_copy(parts[p][1][m][0], slot(p, m), loads.at[p, m])

    def store(p, m):
        return pltpu.make_async_copy(slot(p, m), parts[p][1][m][1], stores.at[p, m])

    load_grads = pltpu.make_async_copy(total_h, grads, loads.at[6, 0])
    moves = [
        (pltpu.make_async_copy(src, mid, loads.at[6, k]), pltpu.make_async_copy(mid, dst, stores.at[6, k]))
        for k, (src, mid, dst) in enumerate(((act_h, act, act_new), (back_h, back, back_new)), 1)
    ]
    load_grads.start()
    for p in range(6):
        for m in range(3):
            load(p, m).start()
        if p == 1:
            for first, _ in moves:
                first.start()
    length = jnp.sqrt(norm_ref[0:1, 0:1])
    factor = CLIP / (length + 1e-06)
    norm_new[...] = length
    shard = vec_w.shape[1]
    own = lax.axis_index("fsdp")
    grad = jnp.zeros(vec_w.shape, F32)
    for s in range(8):
        grad = grad + jnp.where(own == s, vec_ref[:12, shard * s : shard * s + shard], 0.0)
    found = adam_update(vec_w[...], vec_m[...], vec_v[...], grad, factor, RATE_VECTOR)
    for ref, value in zip((vec_wn, vec_mn, vec_vn), found):
        ref[...] = value
    vec_gn[...] = grad * factor
    load_grads.wait()
    for p in range(6):
        for m in range(3):
            load(p, m).wait()
        for k in range(2):
            grad = grads[parts[p][0] + k].astype(F32)
            if p < 2:
                views = [slot(p, m).at[k] for m in range(3)]
            elif p < 4:
                views = [slot(p, m).at[pl.ds(96 * k, 96)] for m in range(3)]
            else:
                views = [slot(p, m).at[:, pl.ds(768 * k, 768)] for m in range(3)]
            found = adam_update(*(v[...] for v in views), grad, factor, RATE_MATRIX)
            for view, value in zip(views, found):
                view[...] = value
        for m in range(3):
            store(p, m).start()
        if p == 2:
            for first, second in moves:
                first.wait()
                second.start()
    for p in range(6):
        for m in range(3):
            store(p, m).wait()
    for _, second in moves:
        second.wait()


def adam_step(activations, input_grad, norm, vec_grad, total, att, inn, out, vec):
    near, far = pl.BlockSpec(memory_space=pltpu.VMEM), pl.BlockSpec(memory_space=pl.ANY)
    like = [jax.ShapeDtypeStruct(a.shape, F32) for a in (*att, *inn, *out, *vec, vec[0])]
    vmem, dma = pltpu.VMEM, pltpu.SemaphoreType.DMA
    hold = (vmem((2, 3, 2, 96, 768), F32), vmem((2, 3, 192, 768), F32), vmem((2, 3, 96, 1536), F32))
    return pl.pallas_call(
        adam_kernel,
        out_shape=[
            jax.ShapeDtypeStruct(activations.shape, BF16), jax.ShapeDtypeStruct(input_grad.shape, F32),
            jax.ShapeDtypeStruct((1, 1), F32), *like,
        ],
        in_specs=[far, far, far, near, near, *[far] * 9, *[near] * 3],
        out_specs=[far, far, near, *[far] * 9, *[near] * 4],
        scratch_shapes=[
            hold, vmem(total.shape, BF16), vmem(activations.shape, BF16), vmem(input_grad.shape, F32),
            dma((7, 3)), dma((7, 3)),
        ],
        compiler_params=pltpu.CompilerParams(vmem_limit_bytes=63 * 2**20),
        name="adam",
    )(activations, input_grad, total, norm, vec_grad, *att, *inn, *out, *vec)


ALPHA_GATHER = (1, 2, 1, 1, 0, 2)
ALPHA_SCATTER = (0, 1, 0, 1, 1, 1)
ORDER = (
    ("init", 0), ("zown", 0), ("yown", 0), ("zown", 1), ("yown", 1), ("yown", 2), ("early", 0), ("t0", 0),
    ("yown", 3), ("a0", 0), ("zown", 2), ("t0", 1), ("a0", 1), ("yown", 4), ("a1", 0), ("zown", 3),
    ("yown", 5), ("a0", 2), ("t1", 0), ("a1", 1), ("t0", 2), ("t1", 1), ("zown", 4), ("a2", 0), ("a0", 3),
    ("t0", 5), ("t2", 0), ("a2", 1), ("t3", 0), ("zown", 5), ("t2", 1), ("a1", 2), ("t1", 2), ("t3", 1),
    ("a0", 4), ("f", 0), ("a1", 3), ("t2", 2), ("a0", 5), ("a2", 2), ("f", 1), ("a1", 4), ("a2", 3),
    ("t0", 3), ("g", 1), ("t1", 3), ("g", 0), ("vec", 0), ("v", 0), ("qk", 0), ("at", 0), ("t3", 2),
    ("a1", 5), ("at", 1), ("at", 2), ("t2", 3), ("a2", 4), ("at", 3), ("t3", 3), ("f", 2), ("t0", 4),
    ("a2", 5), ("t1", 4), ("t1", 5), ("at", 4), ("t2", 4), ("t2", 5), ("at", 5), ("f", 3), ("wo", 0),
    ("t3", 4), ("g", 2), ("f", 4), ("t3", 5), ("F", 0), ("g", 3), ("F", 2), ("F", 1), ("g", 4), ("F", 3),
    ("f", 5), ("o", 4), ("g", 5), ("o", 5), ("ln2", 0), ("D", 1), ("G", 0), ("G", 1), ("s1", 1), ("s1", 0),
    ("D", 0), ("D", 2), ("D", 3), ("H", 0), ("H", 1), ("p2", 0), ("agf", 0), ("r1", 1), ("H", 2), ("H", 3),
    ("r1", 0), ("G", 2), ("G", 3), ("s1", 3), ("q2", 0), ("p1", 0), ("ln1", 0), ("s1", 2), ("dc", 0),
    ("p1", 1), ("ab", 0), ("ab", 1), ("ab", 2), ("p2", 2), ("q1", 0), ("p3", 1), ("r1", 3), ("p3", 0),
    ("ab", 3), ("p3", 2), ("p1", 2), ("q3", 0), ("p0", 2), ("ab", 4), ("r1", 2), ("q2", 2), ("ab", 5),
    ("dq", 0), ("V", 0), ("p1", 3), ("G", 4), ("p3", 3), ("q3", 2), ("V", 1), ("p0", 0), ("G", 5), ("s1", 4),
    ("V", 2), ("q1", 2), ("p2", 1), ("s1", 5), ("p2", 3), ("q1", 1), ("q1", 3), ("p2", 4), ("q2", 1),
    ("q3", 1), ("p0", 1), ("p0", 3), ("q2", 3), ("r1", 4), ("p3", 4), ("ig", 0), ("r1", 5), ("p2", 5),
    ("q3", 3), ("q0", 1), ("p1", 4), ("q0", 3), ("q0", 0), ("p1", 5), ("p3", 5), ("p0", 5), ("q3", 4),
    ("q1", 4), ("q2", 5), ("s4", 3), ("p0", 4), ("q0", 2), ("s4", 0), ("s4", 2), ("q3", 5), ("q1", 5),
    ("q2", 4), ("q0", 5), ("s4", 1), ("s5", 3), ("q0", 4), ("V", 3), ("s4", 5), ("s5", 0), ("s4", 4),
    ("s6", 3), ("s6", 0), ("s5", 1), ("s5", 2), ("s5", 5), ("s6", 1), ("s5", 4), ("V", 4), ("s6", 2),
    ("s6", 5), ("s6", 4), ("sq", 0), ("fin", 0),
)

def plain_body(
    tokens,
    segment_ids,
    cotangent,
    attention_weight,
    attention_first,
    attention_second,
    inner_weight,
    inner_first,
    inner_second,
    outer_weight,
    outer_first,
    outer_second,
    vectors,
    vector_first,
    vector_second,
):
    row_count, seq_length, model_width = tokens.shape
    token_count = row_count * seq_length
    flat_rows = tokens.reshape(token_count, model_width)
    shards = (
        attention_weight.astype(jnp.bfloat16),
        inner_weight.astype(jnp.bfloat16),
        outer_weight.astype(jnp.bfloat16),
        vectors.astype(jnp.bfloat16),
    )
    attention_full, inner_full, outer_full, vector_full = (
        lax.all_gather(shards[0], "fsdp", axis=1, tiled=True),
        lax.all_gather(shards[1], "fsdp", axis=0, tiled=True),
        lax.all_gather(shards[2], "fsdp", axis=0, tiled=True),
        lax.all_gather(shards[3], "fsdp", axis=1, tiled=True),
    )
    vector_rows = vector_full.astype(jnp.float32)
    bias_query = vector_rows[0]
    bias_value = vector_rows[1]
    bias_output = vector_rows[2]
    gain_one = vector_rows[3]
    shift_one = vector_rows[4]
    bias_inner = vector_rows[5:9].reshape(-1)
    bias_outer = vector_rows[9]
    gain_two = vector_rows[10]
    shift_two = vector_rows[11]
    projected = jnp.einsum(
        "td,kde->kte", flat_rows, attention_full[:3], preferred_element_type=jnp.float32
    )
    queries = ((projected[0] + bias_query) * 0.125).astype(jnp.bfloat16)
    key_rows = projected[1].astype(jnp.bfloat16)
    value_rows = (projected[2] + bias_value).astype(jnp.bfloat16)
    row_view = (row_count, seq_length, model_width)
    query_view = queries.reshape(row_view)
    key_view = key_rows.reshape(row_view)
    value_view = value_rows.reshape(row_view)
    context, log_totals = lax.map(attend_row, (query_view, key_view, value_view, segment_ids))
    context_flat = context.reshape(token_count, model_width)
    attention_out = (
        jnp.dot(context_flat, attention_full[3], preferred_element_type=jnp.float32) + bias_output
    )
    sum_one = flat_rows.astype(jnp.float32) + attention_out
    hidden_one, norm_one_back = jax.vjp(layer_norm, sum_one, gain_one, shift_one)
    hidden_low = hidden_one.astype(jnp.bfloat16)
    inner_pre = jnp.dot(hidden_low, inner_full, preferred_element_type=jnp.float32) + bias_inner
    activated, gelu_back = jax.vjp(gelu_exact, inner_pre)
    activated_low = activated.astype(jnp.bfloat16)
    outer_pre = jnp.dot(activated_low, outer_full, preferred_element_type=jnp.float32) + bias_outer
    sum_two = hidden_one + outer_pre
    output, norm_two_back = jax.vjp(layer_norm, sum_two, gain_two, shift_two)
    activations = output.astype(jnp.bfloat16).reshape(row_view)
    attention_back, inner_back, outer_back = (
        lax.all_gather(shards[0], "fsdp", axis=1, tiled=True),
        lax.all_gather(shards[1], "fsdp", axis=0, tiled=True),
        lax.all_gather(shards[2], "fsdp", axis=0, tiled=True),
    )
    output_grad = cotangent.reshape(token_count, model_width).astype(jnp.float32)
    sum_two_grad, gain_two_grad, shift_two_grad = norm_two_back(output_grad)
    outer_grad = sum_two_grad.astype(jnp.bfloat16)
    outer_weight_grad = jnp.einsum(
        "tf,td->fd", activated_low, outer_grad, preferred_element_type=jnp.float32
    )
    bias_outer_grad = jnp.sum(outer_grad.astype(jnp.float32), axis=0)
    activated_grad = jnp.einsum(
        "td,fd->tf", outer_grad, outer_back, preferred_element_type=jnp.float32
    )
    (inner_raw_grad,) = gelu_back(activated_grad)
    inner_grad = inner_raw_grad.astype(jnp.bfloat16)
    inner_weight_grad = jnp.einsum(
        "td,tf->df", hidden_low, inner_grad, preferred_element_type=jnp.float32
    )
    bias_inner_grad = jnp.sum(inner_grad.astype(jnp.float32), axis=0)
    hidden_one_grad = sum_two_grad + jnp.einsum(
        "tf,df->td", inner_grad, inner_back, preferred_element_type=jnp.float32
    )
    sum_one_grad, gain_one_grad, shift_one_grad = norm_one_back(hidden_one_grad)
    attention_grad = sum_one_grad.astype(jnp.bfloat16)
    output_weight_grad = jnp.einsum(
        "td,te->de", context_flat, attention_grad, preferred_element_type=jnp.float32
    )
    bias_output_grad = jnp.sum(attention_grad.astype(jnp.float32), axis=0)
    context_grad = jnp.einsum(
        "te,de->td", attention_grad, attention_back[3], preferred_element_type=jnp.float32
    ).astype(jnp.bfloat16)
    query_grad, key_grad, value_grad = lax.map(
        attend_back,
        (query_view, key_view, value_view, segment_ids, log_totals, context_grad.reshape(row_view)),
    )
    query_grad = query_grad.reshape(token_count, model_width)
    key_grad = key_grad.reshape(token_count, model_width)
    value_grad = value_grad.reshape(token_count, model_width)
    grad_stack = jnp.stack([query_grad, key_grad, value_grad])
    projection_grad = jnp.einsum(
        "td,kte->kde", flat_rows, grad_stack, preferred_element_type=jnp.float32
    )
    projection_grad = projection_grad * jnp.array([0.125, 1.0, 1.0], jnp.float32)[:, None, None]
    attention_weight_grad = jnp.concatenate([projection_grad, output_weight_grad[None]], axis=0)
    bias_query_grad = 0.125 * jnp.sum(query_grad.astype(jnp.float32), axis=0)
    bias_value_grad = jnp.sum(value_grad.astype(jnp.float32), axis=0)
    token_grad = sum_one_grad + 0.125 * jnp.einsum(
        "te,de->td", query_grad, attention_back[0], preferred_element_type=jnp.float32
    )
    token_grad = token_grad + jnp.einsum(
        "kte,kde->td", grad_stack[1:], attention_back[1:3], preferred_element_type=jnp.float32
    )
    input_grad = token_grad.reshape(row_view)
    vector_grad = jnp.concatenate(
        [
            jnp.stack(
                [bias_query_grad, bias_value_grad, bias_output_grad, gain_one_grad, shift_one_grad]
            ),
            bias_inner_grad.reshape(4, model_width),
            jnp.stack([bias_outer_grad, gain_two_grad, shift_two_grad]),
        ],
        axis=0,
    )
    shard_grads = (
        lax.psum_scatter(
            attention_weight_grad.astype(jnp.bfloat16), "fsdp", scatter_dimension=1, tiled=True
        ).astype(jnp.float32),
        lax.psum_scatter(
            inner_weight_grad.astype(jnp.bfloat16), "fsdp", scatter_dimension=0, tiled=True
        ).astype(jnp.float32),
        lax.psum_scatter(
            outer_weight_grad.astype(jnp.bfloat16), "fsdp", scatter_dimension=0, tiled=True
        ).astype(jnp.float32),
        lax.psum_scatter(
            vector_grad.astype(jnp.bfloat16), "fsdp", scatter_dimension=1, tiled=True
        ).astype(jnp.float32),
    )
    summed = (
        lax.psum(shard_grads[0].astype(jnp.bfloat16), "dp").astype(jnp.float32),
        lax.psum(shard_grads[1].astype(jnp.bfloat16), "dp").astype(jnp.float32),
        lax.psum(shard_grads[2].astype(jnp.bfloat16), "dp").astype(jnp.float32),
        lax.psum(shard_grads[3].astype(jnp.bfloat16), "dp").astype(jnp.float32),
    )
    local_squares = (
        jnp.sum(summed[0] * summed[0])
        + jnp.sum(summed[1] * summed[1])
        + jnp.sum(summed[2] * summed[2])
        + jnp.sum(summed[3] * summed[3])
    )
    total_squares = lax.psum(local_squares, "fsdp")
    grad_norm = jnp.sqrt(total_squares)
    factor = CLIP / (grad_norm + 1e-06)
    attention_new, attention_first_new, attention_second_new = adam_update(
        attention_weight, attention_first, attention_second, summed[0], factor, RATE_MATRIX
    )
    inner_new, inner_first_new, inner_second_new = adam_update(
        inner_weight, inner_first, inner_second, summed[1], factor, RATE_MATRIX
    )
    outer_new, outer_first_new, outer_second_new = adam_update(
        outer_weight, outer_first, outer_second, summed[2], factor, RATE_MATRIX
    )
    vectors_new, vector_first_new, vector_second_new = adam_update(
        vectors, vector_first, vector_second, summed[3], factor, RATE_VECTOR
    )
    clipped_vectors = summed[3] * factor
    return (
        activations,
        input_grad,
        grad_norm,
        attention_new,
        attention_first_new,
        attention_second_new,
        inner_new,
        inner_first_new,
        inner_second_new,
        outer_new,
        outer_first_new,
        outer_second_new,
        vectors_new,
        vector_first_new,
        vector_second_new,
        clipped_vectors,
    )


def fused_body(
    tokens,
    segment_ids,
    cotangent,
    attention_weight,
    attention_first,
    attention_second,
    inner_weight,
    inner_first,
    inner_second,
    outer_weight,
    outer_first,
    outer_second,
    vectors,
    vector_first,
    vector_second,
):
    _, seq_length, model_width = tokens.shape
    activations, input_grad, total, vec_grad, norm = whole_layer(
        tokens.reshape(seq_length, model_width),
        cotangent.reshape(seq_length, model_width),
        segment_ids,
        attention_weight,
        inner_weight,
        outer_weight,
        vectors,
        ORDER,
        ALPHA_GATHER,
        ALPHA_SCATTER,
    )
    found = adam_step(
        activations,
        input_grad,
        norm,
        vec_grad,
        total,
        (attention_weight, attention_first, attention_second),
        (inner_weight, inner_first, inner_second),
        (outer_weight, outer_first, outer_second),
        (vectors, vector_first, vector_second),
    )
    return (found[0][None], found[1][None], found[2].reshape(()), *found[3:])


def solution(mesh):
    placed = (
        P(("dp", "fsdp"), None, None),
        P(("dp", "fsdp"), None),
        P(("dp", "fsdp"), None, None),
        P(None, "fsdp", None),
        P(None, "fsdp", None),
        P(None, "fsdp", None),
        P("fsdp", None),
        P("fsdp", None),
        P("fsdp", None),
        P("fsdp", None),
        P("fsdp", None),
        P("fsdp", None),
        P(None, "fsdp"),
        P(None, "fsdp"),
        P(None, "fsdp"),
    )
    fused = mesh.shape["dp"] == 4 and mesh.shape["fsdp"] == 8
    return jax.shard_map(
        fused_body if fused else plain_body,
        mesh=mesh,
        in_specs=placed,
        out_specs=(
            P(("dp", "fsdp"), None, None),
            P(("dp", "fsdp"), None, None),
            P(),
            P(None, "fsdp", None),
            P(None, "fsdp", None),
            P(None, "fsdp", None),
            P("fsdp", None),
            P("fsdp", None),
            P("fsdp", None),
            P("fsdp", None),
            P("fsdp", None),
            P("fsdp", None),
            P(None, "fsdp"),
            P(None, "fsdp"),
            P(None, "fsdp"),
            P(None, "fsdp"),
        ),
        check_vma=False,
    )
```

```python
import functools

import jax
import jax.numpy as jnp
from jax import lax
from jax.experimental import pallas as pl
from jax.experimental.pallas import tpu as pltpu
from jax.sharding import PartitionSpec as P

HEADS = 12
STEP = 10


EPS_NORM = 1e-12
BETA_ONE = 0.9
BETA_TWO = 0.999
ADAM_EPS = 1e-08
DECAY = 0.01
RATE_MATRIX = 0.03
RATE_VECTOR = 0.5
CLIP = 1.0


def layer_norm(resid, gain, shift):
    centre = jnp.mean(resid, axis=-1, keepdims=True)
    centered = resid - centre
    spread = jnp.mean(centered * centered, axis=-1, keepdims=True)
    return centered * lax.rsqrt(spread + EPS_NORM) * gain + shift


def gelu_exact(values):
    return jax.nn.gelu(values, approximate=False)


def split_heads(matrix):
    return matrix.reshape(matrix.shape[0], HEADS, matrix.shape[1] // HEADS)


def row_scores(query_row, key_row, segment_row):
    scores = jnp.einsum(
        "qhe,khe->hqk",
        split_heads(query_row),
        split_heads(key_row),
        preferred_element_type=jnp.float32,
    )
    same_segment = segment_row[:, None] == segment_row[None, :]
    return jnp.where(same_segment[None], scores, -1000000000.0)


def attend_row(pieces):
    query_row, key_row, value_row, segment_row = pieces
    scores = row_scores(query_row, key_row, segment_row)
    row_peak = jnp.max(scores, axis=-1, keepdims=True)
    exponent = jnp.exp(scores - row_peak)
    row_total = jnp.sum(exponent, axis=-1, keepdims=True)
    softmax_rows = exponent / row_total
    mixture = jnp.einsum(
        "hqk,khe->qhe",
        softmax_rows.astype(jnp.bfloat16),
        split_heads(value_row),
        preferred_element_type=jnp.float32,
    )
    return (mixture.reshape(query_row.shape).astype(jnp.bfloat16), row_peak + jnp.log(row_total))


def attend_back(pieces):
    query_row, key_row, value_row, segment_row, log_total, context_grad = pieces
    row_shape = query_row.shape
    scores = row_scores(query_row, key_row, segment_row)
    softmax_rows = jnp.exp(scores - log_total)
    grad_heads = split_heads(context_grad)
    prob_grad = jnp.einsum(
        "qhe,khe->hqk", grad_heads, split_heads(value_row), preferred_element_type=jnp.float32
    )
    value_grad = jnp.einsum(
        "hqk,qhe->khe",
        softmax_rows.astype(jnp.bfloat16),
        grad_heads,
        preferred_element_type=jnp.float32,
    )
    row_delta = jnp.sum(prob_grad * softmax_rows, axis=-1, keepdims=True)
    score_grad = (softmax_rows * (prob_grad - row_delta)).astype(jnp.bfloat16)
    query_grad = jnp.einsum(
        "hqk,khe->qhe", score_grad, split_heads(key_row), preferred_element_type=jnp.float32
    )
    key_grad = jnp.einsum(
        "hqk,qhe->khe", score_grad, split_heads(query_row), preferred_element_type=jnp.float32
    )
    return (
        query_grad.reshape(row_shape).astype(jnp.bfloat16),
        key_grad.reshape(row_shape).astype(jnp.bfloat16),
        value_grad.reshape(row_shape).astype(jnp.bfloat16),
    )


def adam_update(weight, first, second, gradient, factor, rate):
    clipped = gradient * factor
    first_new = BETA_ONE * first + (1.0 - BETA_ONE) * clipped
    second_new = BETA_TWO * second + (1.0 - BETA_TWO) * clipped * clipped
    first_hat = first_new / (1.0 - BETA_ONE**STEP)
    second_hat = second_new / (1.0 - BETA_TWO**STEP)
    weight_new = weight - rate * (first_hat / (jnp.sqrt(second_hat) + ADAM_EPS) + DECAY * weight)
    return (weight_new, first_new, second_new)


F32, BF16 = jnp.float32, jnp.bfloat16
MESH = pl.DeviceIdType.MESH
BLOCKS = 6
CHUNKS = 6
INV_SQRT2 = 0.7071067811865476
INV_SQRT2PI = 0.3989422804014327


def dot_nn(a, b):
    return lax.dot_general(a, b, (((1,), (0,)), ((), ())), preferred_element_type=F32)


def dot_nt(a, b):
    return lax.dot_general(a, b, (((1,), (1,)), ((), ())), preferred_element_type=F32)


def dot_tn(a, b):
    return lax.dot_general(a, b, (((0,), (0,)), ((), ())), preferred_element_type=F32)


def wide(value):
    return value.astype(F32)


class Place:
    def __init__(self):
        dp, fsdp = lax.axis_index("dp"), lax.axis_index("fsdp")
        self.x, self.c, self.z, self.y = dp // 2, dp % 2, fsdp // 2, fsdp % 2

    def dev(self, x=None, c=None, z=None, y=None):
        x = self.x if x is None else x
        c = self.c if c is None else c
        z = self.z if z is None else z
        y = self.y if y is None else y
        return (x * 2 + c, z * 2 + y)

    def far(self, dz):
        return lax.rem(self.z + dz, 4)


def half(x):
    return pl.ds(pl.multiple_of(x * 384, 128), 384)


def remote(src, dst, send, recv, dev):
    return pltpu.make_async_remote_copy(
        src_ref=src, dst_ref=dst, send_sem=send, recv_sem=recv, device_id=dev, device_id_type=MESH
    )


def at_one(index):
    return index.start if isinstance(index, slice) else index


class Gather:
    def __init__(self, at, att, inn, out, sems, alpha):
        self.at, self.att, self.inn, self.out, self.alpha = at, att, inn, out, alpha
        self.zs, self.zr, self.ys, self.yr, self.xs, self.xr, self.cs, self.cr = sems

    def ref(self, i, z, y, x):
        c = self.at.c
        cols = slice(None) if x is None else half(x)
        if i < 2:
            return self.att.at[2 * i + c, z, y, :, cols]
        if i < 4:
            return self.inn.at[2 * (i - 2) + c, z, y, :, cols]
        return self.out.at[z, y, 2 * (i - 4) + c, :, cols]

    def whole(self, i, c):
        if i < 2:
            return self.att.at[2 * i + c]
        if i < 4:
            return self.inn.at[2 * (i - 2) + c]
        return self.out.at[:, :, 2 * (i - 4) + c]

    def zmove(self, i, s, right, sz):
        z = self.at.z
        dest = jnp.minimum(z + 1, 3) if right else jnp.maximum(z - 1, 0)
        r = self.ref(i, sz, self.at.y, self.at.x if self.alpha[i] == 1 else None)
        return remote(r, r, self.zs.at[i, 0 if right else 1], self.zr.at[i, at_one(sz)], self.at.dev(z=dest))

    def ymove(self, i, sz, recv=False):
        y = 1 - self.at.y if recv else self.at.y
        r = self.ref(i, sz, y, self.at.x if self.alpha[i] else None)
        return remote(r, r, self.ys.at[i], self.yr.at[i, at_one(sz)], self.at.dev(y=1 - self.at.y))

    def xmove(self, i, sz, own, recv=False):
        y = self.at.y if own else 1 - self.at.y
        x = 1 - self.at.x if recv else self.at.x
        k = 0 if own else 1
        r = self.ref(i, sz, y, x)
        return remote(r, r, self.xs.at[i, k], self.xr.at[i, k], self.at.dev(x=1 - self.at.x))

    def cmove(self, i, recv=False):
        r = self.whole(i, 1 - self.at.c if recv else self.at.c)
        return remote(r, r, self.cs.at[i], self.cr.at[i], self.at.dev(c=1 - self.at.c))

    def zown(self, i):
        z = self.at.z

        @pl.when(z < 3)
        def _():
            self.zmove(i, 0, True, z).start()

        @pl.when(z > 0)
        def _():
            self.zmove(i, 0, False, z).start()

    def yown(self, i):
        self.ymove(i, self.at.z).start()

    def arrive(self, i, s):
        z = self.at.z

        def forward(sz, right, more):
            self.zmove(i, s, right, sz).wait_recv()
            if s < 2:

                @pl.when(more)
                def _():
                    self.zmove(i, s + 1, right, sz).start()

            self.ymove(i, sz).start()
            if self.alpha[i] == 1:
                self.xmove(i, sz, True).start()

        @pl.when(z >= 1 + s)
        def _():
            forward(jnp.maximum(z - 1 - s, 0), True, z < 3)

        @pl.when(z + 1 + s <= 3)
        def _():
            forward(jnp.minimum(z + 1 + s, 3), False, z > 0)

    def across(self, i, s):
        z = self.at.z

        def one(sz):
            self.ymove(i, sz, True).wait_recv()
            if self.alpha[i]:
                self.xmove(i, sz, False).start()

        if s == 0:
            one(z)
            return

        @pl.when(z >= s)
        def _():
            one(jnp.maximum(z - s, 0))

        @pl.when(z + s <= 3)
        def _():
            one(jnp.minimum(z + s, 3))

    def join(self, i):
        if self.alpha[i]:
            self.xmove(i, slice(0, 4), False, True).wait_recv()
        if self.alpha[i] == 1:
            self.xmove(i, slice(0, 3), True, True).wait_recv()
        self.cmove(i).start()

    def have(self, i):
        self.cmove(i, True).wait_recv()

    def finish(self):
        z = self.at.z
        for i in range(BLOCKS):
            for count in (1, 2, 3):

                @pl.when(z + 1 == count)
                def _():
                    self.zmove(i, 0, True, slice(0, count)).wait_send()

                @pl.when(4 - z == count)
                def _():
                    self.zmove(i, 0, False, slice(0, count)).wait_send()

            self.ymove(i, slice(0, 4)).wait_send()
            if self.alpha[i]:
                self.xmove(i, slice(0, 4), False).wait_send()
            if self.alpha[i] == 1:
                self.xmove(i, slice(0, 3), True).wait_send()
            self.cmove(i).wait_send()


class Scatter:
    def __init__(self, at, grad, total, bufs, sems, alpha):
        self.at, self.grad, self.total, self.alpha = at, grad, total, alpha
        self.ra1, self.ra2, self.ra3, self.rb1, self.rb2, self.rb3 = bufs
        self.ss, self.rs = sems
        self.slot = [sum(1 for q in alpha[:j] if q == alpha[j]) for j in range(CHUNKS)]

    def cp(self, j, kind, k, src, dst, dev):
        return remote(src, dst, self.ss.at[j, kind], self.rs.at[j, k], dev)

    def block(self, j, c):
        return 4 * (j // 2) + 2 * c + j % 2

    def firsts(self, j, dz, own):
        n, at = self.slot[j], self.at
        z = at.far(dz)
        if self.alpha[j]:
            y = at.y if own else 1 - at.y
            return self.cp(
                j, own, dz + 4 * own, self.grad(j, z, y).at[:, half(1 - at.x)], self.ra1.at[n, z, y], at.dev(x=1 - at.x)
            )
        return self.cp(j, 0, dz, self.grad(j, z, 1 - at.y), self.rb1.at[n, z], at.dev(y=1 - at.y))

    def second(self, j, dz):
        n, at = self.slot[j], self.at
        z = at.far(dz)
        return self.cp(
            j, 2, 8 + dz, self.grad(j, z, 1 - at.y).at[:, half(at.x)], self.ra2.at[n, z], at.dev(y=1 - at.y)
        )

    def third(self, j, dz):
        n, at = self.slot[j], self.at
        z = at.far(dz)
        src = self.grad(j, z, at.y)
        if self.alpha[j]:
            return self.cp(j, 3, 12, src.at[:, half(at.x)], self.ra3.at[n, dz - 1], at.dev(z=z))
        return self.cp(j, 3, 12, src, self.rb2.at[n, dz - 1], at.dev(z=z))

    def fourth(self, j, recv=False):
        n, at = self.slot[j], self.at
        if self.alpha[j]:
            r = self.total.at[self.block(j, at.c), :, half(1 - at.x if recv else at.x)]
            return self.cp(j, 4, 13, r, r, at.dev(x=1 - at.x))
        return self.cp(j, 4, 13, self.grad(j, at.z, at.y), self.rb3.at[n], at.dev(x=1 - at.x))

    def fifth(self, j, recv=False):
        r = self.total.at[self.block(j, 1 - self.at.c if recv else self.at.c)]
        return self.cp(j, 5, 14, r, r, self.at.dev(c=1 - self.at.c))

    def s1(self, j):
        if j == 0:
            return
        for dz in (2, 1, 3, 0):
            self.firsts(j, dz, 0).start()

    def r1(self, j):
        if self.alpha[j]:
            for dz in (2, 1, 3, 0):
                self.firsts(j, dz, 1).start()

    def p(self, j, dz):
        if not self.alpha[j]:
            return
        n, at = self.slot[j], self.at
        z, y, h = at.far(dz), 1 - at.y, half(at.x)
        self.firsts(j, dz, 0).wait_recv()
        r = self.grad(j, z, y)
        r[:, h] = (wide(r[:, h]) + wide(self.ra1[n, z, y])).astype(BF16)
        self.second(j, dz).start()

    def q(self, j, dz):
        n, at = self.slot[j], self.at
        z, y, h = at.far(dz), at.y, half(at.x)
        r = self.grad(j, z, y)
        if self.alpha[j]:
            self.firsts(j, dz, 1).wait_recv()
            self.second(j, dz).wait_recv()
            r[:, h] = (wide(r[:, h]) + wide(self.ra1[n, z, y]) + wide(self.ra2[n, z])).astype(BF16)
        else:
            self.firsts(j, dz, 0).wait_recv()
            r[...] = (wide(r[...]) + wide(self.rb1[n, z])).astype(BF16)
        if dz:
            self.third(j, dz).start()

    def s4(self, j):
        n, at = self.slot[j], self.at
        landed = (self.ra3 if self.alpha[j] else self.rb2).at[n]
        remote(landed, landed, self.ss.at[j, 3], self.rs.at[j, 12], at.dev(z=at.far(1))).wait_recv()
        r = self.grad(j, at.z, at.y)
        if self.alpha[j]:
            h = half(at.x)
            total = wide(r[:, h])
            for dz in range(3):
                total = total + wide(self.ra3[n, dz])
            self.total[self.block(j, at.c), :, h] = total.astype(BF16)
        else:
            total = wide(r[...])
            for dz in range(3):
                total = total + wide(self.rb2[n, dz])
            r[...] = total.astype(BF16)
        self.fourth(j).start()

    def s5(self, j):
        n, at = self.slot[j], self.at
        self.fourth(j, True).wait_recv()
        if not self.alpha[j]:
            r = self.grad(j, at.z, at.y)
            self.total[self.block(j, at.c)] = (wide(r[...]) + wide(self.rb3[n])).astype(BF16)
        self.fifth(j).start()

    def s6(self, j):
        self.fifth(j, True).wait_recv()

    def finish(self):
        at = self.at
        for j in range(CHUNKS):
            n = self.slot[j]
            first = (self.ra2 if self.alpha[j] else self.rb1).at[n]
            last = (self.ra3 if self.alpha[j] else self.rb2).at[n]
            sent = [(0, first)]
            if self.alpha[j]:
                sent += [(1, first), (2, first)]
            for kind, like in sent + [(3, last)]:
                remote(like, like, self.ss.at[j, kind], self.rs.at[j, 0], at.dev(x=1 - at.x)).wait_send()
            self.fourth(j).wait_send()
            self.fifth(j).wait_send()


def layer_kernel(
    order, alpha_gather, alpha_scatter,
    tok_h, cot_h, seg_h, watt_h, winn_h, wout_h, vec_h,
    act_h, grad_h, total_h, vec_grad, norm,
    att, inn, out, norm_one, resid, work, pair_in, stack, hidden, outer_grad, shown, turn, turn_two,
    active, slope, probs, mask, vec, dev_one, dev_two,
    sib_in, sib_hidden, sib_active, sib_outer, sib_slope, sib_stack,
    grad_out, ra1, ra2, ra3, rb1, rb2, rb3,
    vec_parts, vec_sib, vec_x, vec_y, vec_z, norm_parts, mate_parts, total, seg_row, vec_in,
    zs, zr, ys, yr, xs, xr, cs, cr, ss, rs, bs, br, vs, vr, ws, wr, ns, nr, ls,
):
    at = Place()
    me = at.z * 2 + at.y
    ag = Gather(at, att, inn, out, (zs, zr, ys, yr, xs, xr, cs, cr), alpha_gather)

    def grad_ref(j, z, y):
        return grad_out.at[j, z, y] if j < 2 else out.at[z, y, j - 2]

    rd = Scatter(at, grad_ref, total, (ra1, ra2, ra3, rb1, rb2, rb3), (ss, rs), alpha_scatter)

    def square(ref, n=768):
        return ref[...].reshape(n, n)

    other = at.dev(c=1 - at.c)

    def to_sibling(k, src, dst):
        return remote(src, dst, bs.at[k], br.at[k], other)

    sib_tokens = to_sibling(0, pair_in.at[0], sib_in.at[0])
    sib_context = to_sibling(1, pair_in.at[1], sib_in.at[1])
    sib_hid = to_sibling(2, hidden, sib_hidden)
    sib_act = to_sibling(3, active.at[:, :, pl.ds(2 * (1 - at.c), 2)], sib_active)
    sib_og = [
        to_sibling(k, outer_grad.at[pl.ds(128 * r, 128)], sib_outer.at[pl.ds(128 * r, 128)])
        for r, k in enumerate((4, 8, 9, 10))
    ]
    sib_sl = to_sibling(5, slope.at[:, pl.ds(pl.multiple_of((1 - at.c) * 1536, 128), 1536)], sib_slope)
    sib_first = to_sibling(6, stack.at[1 - at.c], sib_stack.at[0])
    sib_last = to_sibling(7, stack.at[3 - at.c], sib_stack.at[1])

    peers = [(dz, dy) for dz in range(4) for dy in range(2) if (dz, dy) != (0, 0)]

    def peer(dz, dy):
        return at.dev(z=at.far(dz), y=lax.rem(at.y + dy, 2))

    def vec_move(k):
        dz, dy = peers[k]
        return remote(vec_parts.at[me], vec_parts.at[me], vs.at[0], vr.at[0], peer(dz, dy))

    def norm_move(k):
        return remote(norm_parts.at[me], norm_parts.at[me], ns.at[0], nr.at[0], peer(*peers[k]))

    mates = [at.dev(x=1 - at.x), at.dev(x=1 - at.x, c=1 - at.c), other]
    rank = at.x * 2 + at.c

    def mate_move(k):
        return remote(mate_parts.at[rank], mate_parts.at[rank], ns.at[1], nr.at[1], mates[k])

    def all_of(ref, count, send, recv):
        view = ref.at[pl.ds(0, count)]
        return remote(view, view, send, recv, other)

    loads = []
    for i in range(2):
        k, rows = 2 * i + at.c, pl.ds(96 * i, 96)
        cols, shard_rows = pl.ds(pl.multiple_of(768 * k, 128), 768), pl.ds(pl.multiple_of(96 * k, 96), 96)
        loads.append(pltpu.make_async_copy(watt_h.at[k], norm_one.at[rows], ls.at[3 * i]))
        loads.append(pltpu.make_async_copy(winn_h.at[:, cols], work.at[rows], ls.at[3 * i + 1]))
        loads.append(pltpu.make_async_copy(wout_h.at[shard_rows], resid.at[rows], ls.at[3 * i + 2]))
    load_tokens = pltpu.make_async_copy(tok_h, pair_in.at[0], ls.at[9])
    load_ids = pltpu.make_async_copy(seg_h, seg_row, ls.at[7])
    load_vectors = pltpu.make_async_copy(vec_h, vec_in, ls.at[8])
    load_cotangent = pltpu.make_async_copy(cot_h, stack.at[3], ls.at[10])
    store_shown = pltpu.make_async_copy(shown, act_h, ls.at[11])
    store_grad = pltpu.make_async_copy(work, grad_h, ls.at[12])

    def init():
        barrier = pltpu.get_barrier_semaphore()
        greet = [peer(dz, dy) for dz, dy in peers] + mates
        for d in greet:
            pl.semaphore_signal(barrier, inc=1, device_id=d, device_id_type=MESH)
        for k in (0, 3, 1, 4, 2, 5):
            loads[k].start()
        load_vectors.start()
        load_ids.start()
        load_tokens.start()
        load_cotangent.start()
        for i in range(2):
            loads[3 * i].wait()
            att[2 * i + at.c, at.z, at.y] = norm_one[pl.ds(96 * i, 96), :].astype(BF16)
        pl.semaphore_wait(barrier, len(greet))

    def cast_rest():
        for i in range(2):
            k, rows = 2 * i + at.c, pl.ds(96 * i, 96)
            loads[3 * i + 1].wait()
            inn[k, at.z, at.y] = work[rows, :].astype(BF16)
            loads[3 * i + 2].wait()
            out[at.z, at.y, k] = resid[rows, :].astype(BF16)
        vec_grad[...] = jnp.zeros_like(vec_grad)

    def early():
        load_vectors.wait()
        load_ids.wait()
        vec_parts[me] = jnp.zeros((16, 128), F32)
        vec_parts[me, :12, :96] = vec_in[...]
        for k in range(7):
            vec_move(k).start()
        load_tokens.wait()
        sib_tokens.start()
        ids = jnp.broadcast_to(seg_row[...].astype(F32), (512, 512))
        mask[...] = jnp.where(ids.T == ids, 1.0, 0.0)

    def vectors_here():
        all_of(vec_parts, 7, vs.at[0], vr.at[0]).wait_recv()
        full = jnp.zeros((16, 768), F32)
        row = lax.broadcasted_iota(jnp.int32, (128, 768), 0)
        col = lax.broadcasted_iota(jnp.int32, (128, 768), 1)
        for s in range(8):
            pick = jnp.where((col == row + 96 * s) & (row < 96), 1.0, 0.0).astype(BF16)
            full = full + dot_nn(vec_parts[s].astype(BF16), pick)
        vec[...] = full

    def vrow(r):
        return vec[pl.ds(r, 1), :]

    def queries_keys():
        tokens = pair_in[0]
        stack[0] = ((dot_nn(tokens, square(att.at[0])) + vrow(0)) * 0.125).astype(BF16)
        stack[2] = dot_nn(tokens, square(att.at[1])).astype(BF16)

    def values():
        stack[1] = (dot_nn(pair_in[0], square(att.at[2])) + vrow(1)).astype(BF16)

    low = lax.broadcasted_iota(jnp.int32, (512, 128), 1) < 64

    def attend(p):
        ls_ = pl.ds(128 * p, 128)
        queries, keys = stack[0, :, ls_], stack[2, :, ls_]
        values_t = stack[1, :, ls_].T
        for h in range(2):
            mine = jnp.where(low if h == 0 else ~low, keys, jnp.zeros_like(keys))
            scores = jnp.where(mask[...] > 0.5, dot_nt(mine, queries), -1000000000.0)
            peak = jnp.max(scores, axis=0, keepdims=True)
            exponent = jnp.exp(scores - peak)
            scale = 1.0 / jnp.sum(exponent, axis=0, keepdims=True)
            weights = (exponent * scale).astype(BF16)
            probs[2 * p + h] = weights
            turn[pl.ds(128 * p + 64 * h, 64), :] = dot_nn(values_t[64 * h : 64 * h + 64], weights).astype(BF16)

    def norm_stats(value):
        centre = jnp.mean(value, axis=1, keepdims=True)
        centered = value - centre
        spread = jnp.mean(centered * centered, axis=1, keepdims=True)
        scale = lax.rsqrt(spread + EPS_NORM)
        return centered * scale, scale

    def project_out():
        pair_in[1] = turn[...].T
        sib_context.start()
        resid[...] = wide(pair_in[0]) + dot_nn(pair_in[1], square(att.at[3])) + vrow(2)
        for r in range(4):
            rows = pl.ds(128 * r, 128)
            normed, scale = norm_stats(resid[rows, :])
            norm_one[rows, :] = normed
            dev_one[rows, :] = scale
            hidden[rows, :] = (normed * vrow(3) + vrow(4)).astype(BF16)
        sib_hid.start()

    def feed_in(q):
        work[...] = dot_nn(hidden[...], square(inn.at[q])) + vrow(5 + q)
        for r in range(4):
            rows = pl.ds(128 * r, 128)
            value = work[rows, :]
            share = 0.5 * (1.0 + lax.erf(value * INV_SQRT2))
            shown[rows, :] = (value * share).astype(BF16)
            density = jnp.exp(-0.5 * value * value) * INV_SQRT2PI
            slope[rows, 768 * q : 768 * q + 768] = (share + value * density).astype(BF16)
        active[q] = shown[...].T.reshape(2, 4, 96, 512)

    def feed_out(part):
        if part == 4:
            sib_act.start()
            resid[...] = norm_one[...] * vrow(3) + vrow(4) + vrow(9)
        q = 2 * (part - 4)
        for n in range(3):
            cols = slice(256 * n, 256 * n + 256)
            resid[:, cols] += dot_tn(
                active[:, :, q : q + 2].reshape(1536, 512), out[:, :, q : q + 2, :, cols].reshape(1536, 256)
            )

    def end_norm():
        load_cotangent.wait()
        sums = [jnp.zeros((1, 768), F32) for _ in range(3)]
        for r in range(4):
            rows = pl.ds(128 * r, 128)
            normed, scale = norm_stats(resid[rows, :])
            shown[rows, :] = (normed * vrow(10) + vrow(11)).astype(BF16)
            given = wide(stack[3, rows, :])
            scaled = given * vrow(10)
            back = scale * (
                scaled
                - jnp.mean(scaled, axis=1, keepdims=True)
                - normed * jnp.mean(scaled * normed, axis=1, keepdims=True)
            )
            work[rows, :] = back
            low_back = back.astype(BF16)
            outer_grad[rows, :] = low_back
            sib_og[r].start()
            for k, term in enumerate((wide(low_back), given * normed, given)):
                sums[k] = sums[k] + jnp.sum(term, axis=0, keepdims=True)
        for k in range(3):
            vec_grad[9 + k : 10 + k, :] = sums[k]
        store_shown.start()

    def inner_back(q):
        cols = slice(768 * q, 768 * q + 768)
        resid[...] = dot_nt(outer_grad[...], out[q].reshape(768, 768))
        total_row = jnp.zeros((1, 768), F32)
        for r in range(4):
            rows = pl.ds(128 * r, 128)
            value = (resid[rows, :] * wide(slope[rows, cols])).astype(BF16)
            slope[rows, cols] = value
            total_row = total_row + jnp.sum(wide(value), axis=0, keepdims=True)
        vec_grad[5 + q : 6 + q, :] = total_row
        if q == 3:
            sib_sl.start()

    def put_chunk(j, value):
        value = value.astype(BF16).reshape(4, 2, 96, 768)
        if j < 2:
            grad_out[j] = value
        else:
            out[:, :, j - 2] = value

    def chunk_out(j):
        if j == 0:
            sib_act.wait_recv()
            for cp in sib_og:
                cp.wait_recv()
            for dz in (2, 1, 3, 0):
                z = at.far(dz)
                mine = active[z, :, pl.ds(2 * at.c, 1)].reshape(192, 512)
                theirs = sib_active[z, :, 0].reshape(192, 512)
                value = dot_nn(mine, outer_grad[...]) + dot_nn(theirs, sib_outer[...])
                grad_out[0, z] = value.astype(BF16).reshape(2, 96, 768)
                rd.firsts(0, dz, 0).start()
            return
        mine = active[:, :, pl.ds(2 * at.c + j, 1)].reshape(768, 512)
        theirs = sib_active[:, :, j].reshape(768, 512)
        put_chunk(j, dot_nn(mine, outer_grad[...]) + dot_nn(theirs, sib_outer[...]))

    def chunk_in(j):
        if j == 2:
            sib_hid.wait_recv()
            sib_sl.wait_recv()
        cols = pl.ds(pl.multiple_of(at.c * 1536 + 768 * (j - 2), 128), 768)
        put_chunk(
            j,
            dot_tn(hidden[...], slope[:, cols])
            + dot_tn(sib_hidden[...], sib_slope[:, 768 * (j - 2) : 768 * (j - 1)]),
        )

    def chunk_attention(j):
        if j == 4:
            sib_tokens.wait_recv()
            sib_first.wait_recv()
            value = dot_tn(pair_in[0], stack[at.c]) + dot_tn(sib_in[0], sib_stack[0])
            put_chunk(j, value * jnp.where(at.c == 0, 0.125, 1.0))
        else:
            sib_context.wait_recv()
            sib_last.wait_recv()
            put_chunk(j, dot_tn(pair_in[at.c], stack[2 + at.c]) + dot_tn(sib_in[at.c], sib_stack[1]))

    def hidden_back(q):
        work[...] += dot_nt(slope[:, 768 * q : 768 * q + 768], square(inn.at[q]))

    def middle_norm():
        sums = [jnp.zeros((1, 768), F32) for _ in range(3)]
        for r in range(4):
            rows = pl.ds(128 * r, 128)
            given = work[rows, :]
            normed = norm_one[rows, :]
            scaled = given * vrow(3)
            back = dev_one[rows, :] * (
                scaled
                - jnp.mean(scaled, axis=1, keepdims=True)
                - normed * jnp.mean(scaled * normed, axis=1, keepdims=True)
            )
            work[rows, :] = back
            low_back = back.astype(BF16)
            stack[3, rows, :] = low_back
            for k, term in enumerate((wide(low_back), given * normed, given)):
                sums[k] = sums[k] + jnp.sum(term, axis=0, keepdims=True)
        for k in range(3):
            vec_grad[2 + k : 3 + k, :] = sums[k]

    def context_back():
        store_shown.wait()
        shown[...] = dot_nt(stack[3], square(att.at[3])).astype(BF16)

    def attend_back(p):
        ls_ = pl.ds(128 * p, 128)
        queries, keys, vals, given = stack[0, :, ls_], stack[2, :, ls_], stack[1, :, ls_], shown[:, ls_]
        keys_t = keys.T
        value_grads, key_grads = [], []
        for h in range(2):
            mine = jnp.where(low if h == 0 else ~low, vals, jnp.zeros_like(vals))
            prob_grad = dot_nt(mine, given)
            weights = probs[2 * p + h]
            wide_weights = wide(weights)
            delta = jnp.sum(prob_grad * wide_weights, axis=0, keepdims=True)
            score_grad = (wide_weights * (prob_grad - delta)).astype(BF16)
            value_grads.append(dot_nn(weights, given))
            key_grads.append(dot_nn(score_grad, queries))
            turn[pl.ds(128 * p + 64 * h, 64), :] = dot_nn(keys_t[64 * h : 64 * h + 64], score_grad).astype(BF16)
        stack[1, :, ls_] = jnp.where(low, value_grads[0], value_grads[1]).astype(BF16)
        stack[2, :, ls_] = jnp.where(low, key_grads[0], key_grads[1]).astype(BF16)

    def queries_back():
        stack[0] = turn[...].T
        sib_first.start()
        sib_last.start()
        vec_grad[0:1, :] = 0.125 * jnp.sum(wide(stack[0]), axis=0, keepdims=True)
        vec_grad[1:2, :] = jnp.sum(wide(stack[1]), axis=0, keepdims=True)

    def input_back():
        work[...] += (
            0.125 * dot_nt(stack[0], square(att.at[0]))
            + dot_nt(stack[2], square(att.at[1]))
            + dot_nt(stack[1], square(att.at[2]))
        )
        store_grad.start()

    def vec_sum(k):
        if k == 0:
            return remote(vec_grad, vec_sib, ws.at[0], wr.at[0], other)
        if k == 1:
            return remote(vec_grad, vec_x, ws.at[1], wr.at[1], at.dev(x=1 - at.x))
        if k == 2:
            return remote(vec_grad, vec_y, ws.at[2], wr.at[2], at.dev(y=1 - at.y))
        return remote(vec_z.at[at.z], vec_z.at[at.z], ws.at[3], wr.at[3], at.dev(z=at.far(k - 2)))

    def vec_step(k):
        if k == 0:
            vec_sum(0).start()
        elif k <= 2:
            vec_sum(k - 1).wait()
            vec_grad[...] += (vec_sib if k == 1 else vec_x)[...]
            vec_sum(k).start()
        elif k == 3:
            vec_sum(2).wait()
            vec_z[at.z] = vec_grad[...] + vec_y[...]
            for m in (3, 4, 5):
                vec_sum(m).start()
        else:
            all_of(vec_z, 3, ws.at[3], wr.at[3]).wait()
            vec_grad[...] = (vec_z[0] + vec_z[1]) + (vec_z[2] + vec_z[3])

    def norm_step(k):
        if k == 0:
            part = jnp.zeros((96, 384), F32)
            for j in range(CHUNKS):
                value = wide(total[rd.block(j, at.c), :, half(at.x)])
                part = part + value * value
            mate_parts[rank] = jnp.full((8, 128), jnp.sum(part), F32)
            for m in range(3):
                mate_move(m).start()
        elif k == 1:
            all_of(mate_parts, 3, ns.at[1], nr.at[1]).wait_recv()
            norm_parts[me] = (mate_parts[0] + mate_parts[1]) + (mate_parts[2] + mate_parts[3])
            for m in range(7):
                norm_move(m).start()
        else:
            own = jnp.sum(vec_grad[...] * vec_grad[...])
            all_of(norm_parts, 7, ns.at[0], nr.at[0]).wait_recv()
            sums = norm_parts[0]
            for s in range(1, 8):
                sums = sums + norm_parts[s]
            norm[...] = sums + own

    def chunk_done(j):
        rd.s6(j)
        for c in range(2):
            b = rd.block(j, c)
            pltpu.make_async_copy(total.at[b], total_h.at[b], ls.at[6]).start()

    def finish():
        all_of(vec_parts, 7, vs.at[0], vr.at[0]).wait_send()
        all_of(norm_parts, 7, ns.at[0], nr.at[0]).wait_send()
        all_of(mate_parts, 3, ns.at[1], nr.at[1]).wait_send()
        for cp in (sib_tokens, sib_context, sib_hid, sib_act, *sib_og, sib_sl, sib_first, sib_last):
            cp.wait_send()
        pltpu.make_async_copy(total, total_h, ls.at[6]).wait()
        store_grad.wait()
        rd.finish()

    run = {
        "init": init, "early": early, "vec": vectors_here, "qk": queries_keys, "v": values, "wo": project_out,
        "ln2": end_norm, "ln1": middle_norm, "dc": context_back, "dq": queries_back,
        "ig": input_back, "init2": cast_rest, "fin": finish, "agf": ag.finish,
    }
    steps = {
        "at": attend, "ab": attend_back, "F": feed_in, "o": feed_out, "D": inner_back, "H": hidden_back, "V": vec_step,
        "G": lambda j: (chunk_out, chunk_in, chunk_attention)[j // 2](j),
        "s1": rd.s1, "r1": rd.r1, "s4": rd.s4, "s5": rd.s5, "s6": chunk_done, "N": norm_step,
        "zown": ag.zown, "yown": ag.yown, "f": ag.join, "g": ag.have,
    }
    for k in range(4):
        steps[f"p{k}"] = functools.partial(rd.p, dz=k)
        steps[f"q{k}"] = functools.partial(rd.q, dz=k)
        steps[f"a{k}"] = functools.partial(ag.arrive, s=k)
        steps[f"t{k}"] = functools.partial(ag.across, s=k)
    for name, index in order:
        if name in run:
            run[name]()
        else:
            steps[name](index)


def whole_layer(tokens, cotangent, segments, watt, winn, wout, vectors_low, order, alpha_gather, alpha_scatter):
    na = max(1, sum(alpha_scatter))
    nb = max(1, CHUNKS - sum(alpha_scatter))
    vmem, dma = pltpu.VMEM, pltpu.SemaphoreType.DMA
    flat = (512, 768)
    scratch = [
        vmem((4, 4, 2, 96, 768), BF16), vmem((4, 4, 2, 96, 768), BF16), vmem((4, 2, 4, 96, 768), BF16),
        vmem(flat, F32), vmem(flat, F32), vmem(flat, F32),
        vmem((2,) + flat, BF16), vmem((4,) + flat, BF16), vmem(flat, BF16), vmem(flat, BF16), vmem(flat, BF16),
        vmem((768, 512), BF16), vmem((8, 128), BF16),
        vmem((4, 2, 4, 96, 512), BF16), vmem((512, 3072), BF16), vmem((12, 512, 512), BF16),
        vmem((512, 512), F32), vmem((16, 768), F32), vmem((512, 1), F32), vmem((8, 128), F32),
        vmem((2,) + flat, BF16), vmem(flat, BF16), vmem((4, 2, 2, 96, 512), BF16), vmem(flat, BF16),
        vmem((512, 1536), BF16), vmem((2,) + flat, BF16),
        vmem((2, 4, 2, 96, 768), BF16),
        vmem((na, 4, 2, 96, 384), BF16), vmem((na, 4, 96, 384), BF16), vmem((na, 3, 96, 384), BF16),
        vmem((nb, 4, 96, 768), BF16), vmem((nb, 3, 96, 768), BF16), vmem((nb, 96, 768), BF16),
        vmem((8, 16, 128), F32), vmem((16, 768), F32), vmem((16, 768), F32), vmem((16, 768), F32),
        vmem((4, 16, 768), F32), vmem((8, 8, 128), F32), vmem((4, 8, 128), F32), vmem((12, 96, 768), BF16),
        vmem((1, 512), jnp.int32), vmem((12, 96), F32),
    ]
    for n in (
        (BLOCKS, 2), (BLOCKS, 4), (BLOCKS,), (BLOCKS, 4), (BLOCKS, 2), (BLOCKS, 2), (BLOCKS,), (BLOCKS,),
        (CHUNKS, 6), (CHUNKS, 15), (11,), (11,), (1,), (1,), (4,), (4,), (2,), (2,), (13,),
    ):
        scratch.append(dma(n))
    local, far = pl.BlockSpec(memory_space=pltpu.VMEM), pl.BlockSpec(memory_space=pl.ANY)
    return pl.pallas_call(
        functools.partial(layer_kernel, order, alpha_gather, alpha_scatter),
        out_shape=[
            jax.ShapeDtypeStruct(flat, BF16), jax.ShapeDtypeStruct(flat, F32),
            jax.ShapeDtypeStruct((12, 96, 768), BF16), jax.ShapeDtypeStruct((16, 768), F32),
            jax.ShapeDtypeStruct((8, 128), F32),
        ],
        in_specs=[far] * 7,
        out_specs=[far, far, far, local, local],
        scratch_shapes=scratch,
        compiler_params=pltpu.CompilerParams(
            collective_id=0, has_side_effects=True, vmem_limit_bytes=63 * 2**20
        ),
        name="layer",
    )(
        tokens, cotangent, segments.reshape(1, 512), watt, winn, wout, vectors_low
    )


def adam_kernel(
    act_h, back_h, total_h, norm_ref, vec_ref,
    att_w, att_m, att_v, inn_w, inn_m, inn_v, out_w, out_m, out_v, vec_w, vec_m, vec_v,
    act_new, back_new, norm_new, att_wn, att_mn, att_vn, inn_wn, inn_mn, inn_vn, out_wn, out_mn, out_vn,
    vec_wn, vec_mn, vec_vn, vec_gn,
    hold, grads, act, back, loads, stores,
):
    parts = []
    for p in range(6):
        k = 2 * (p % 2)
        rows, cols = pl.ds(96 * k, 192), pl.ds(768 * k, 1536)
        if p < 2:
            parts.append((8 + k, [[r.at[pl.ds(k, 2)] for r in (w, n)] for w, n in (
                (att_w, att_wn), (att_m, att_mn), (att_v, att_vn))]))
        elif p < 4:
            parts.append((k, [[r.at[rows] for r in (w, n)] for w, n in (
                (out_w, out_wn), (out_m, out_mn), (out_v, out_vn))]))
        else:
            parts.append((4 + k, [[r.at[:, cols] for r in (w, n)] for w, n in (
                (inn_w, inn_wn), (inn_m, inn_mn), (inn_v, inn_vn))]))

    def slot(p, m):
        if p < 2:
            return hold[0].at[p, m]
        return hold[1].at[p - 2, m] if p < 4 else hold[2].at[p - 4, m]

    def load(p, m):
        return pltpu.make_async_copy(parts[p][1][m][0], slot(p, m), loads.at[p, m])

    def store(p, m):
        return pltpu.make_async_copy(slot(p, m), parts[p][1][m][1], stores.at[p, m])

    load_grads = pltpu.make_async_copy(total_h, grads, loads.at[6, 0])
    moves = [
        (pltpu.make_async_copy(src, mid, loads.at[6, k]), pltpu.make_async_copy(mid, dst, stores.at[6, k]))
        for k, (src, mid, dst) in enumerate(((act_h, act, act_new), (back_h, back, back_new)), 1)
    ]
    load_grads.start()
    for p in range(6):
        for m in range(3):
            load(p, m).start()
        if p == 1:
            for first, _ in moves:
                first.start()
    length = jnp.sqrt(norm_ref[0:1, 0:1])
    factor = CLIP / (length + 1e-06)
    norm_new[...] = length
    shard = vec_w.shape[1]
    own = lax.axis_index("fsdp")
    grad = jnp.zeros(vec_w.shape, F32)
    for s in range(8):
        grad = grad + jnp.where(own == s, vec_ref[:12, shard * s : shard * s + shard], 0.0)
    found = adam_update(vec_w[...], vec_m[...], vec_v[...], grad, factor, RATE_VECTOR)
    for ref, value in zip((vec_wn, vec_mn, vec_vn), found):
        ref[...] = value
    vec_gn[...] = grad * factor
    load_grads.wait()
    for p in range(6):
        for m in range(3):
            load(p, m).wait()
        for k in range(2):
            grad = grads[parts[p][0] + k].astype(F32)
            if p < 2:
                views = [slot(p, m).at[k] for m in range(3)]
            elif p < 4:
                views = [slot(p, m).at[pl.ds(96 * k, 96)] for m in range(3)]
            else:
                views = [slot(p, m).at[:, pl.ds(768 * k, 768)] for m in range(3)]
            found = adam_update(*(v[...] for v in views), grad, factor, RATE_MATRIX)
            for view, value in zip(views, found):
                view[...] = value
        for m in range(3):
            store(p, m).start()
        if p == 2:
            for first, second in moves:
                first.wait()
                second.start()
    for p in range(6):
        for m in range(3):
            store(p, m).wait()
    for _, second in moves:
        second.wait()


def adam_step(activations, input_grad, norm, vec_grad, total, att, inn, out, vec):
    near, far = pl.BlockSpec(memory_space=pltpu.VMEM), pl.BlockSpec(memory_space=pl.ANY)
    like = [jax.ShapeDtypeStruct(a.shape, F32) for a in (*att, *inn, *out, *vec, vec[0])]
    vmem, dma = pltpu.VMEM, pltpu.SemaphoreType.DMA
    hold = (vmem((2, 3, 2, 96, 768), F32), vmem((2, 3, 192, 768), F32), vmem((2, 3, 96, 1536), F32))
    return pl.pallas_call(
        adam_kernel,
        out_shape=[
            jax.ShapeDtypeStruct(activations.shape, BF16), jax.ShapeDtypeStruct(input_grad.shape, F32),
            jax.ShapeDtypeStruct((1, 1), F32), *like,
        ],
        in_specs=[far, far, far, near, near, *[far] * 9, *[near] * 3],
        out_specs=[far, far, near, *[far] * 9, *[near] * 4],
        scratch_shapes=[
            hold, vmem(total.shape, BF16), vmem(activations.shape, BF16), vmem(input_grad.shape, F32),
            dma((7, 3)), dma((7, 3)),
        ],
        compiler_params=pltpu.CompilerParams(vmem_limit_bytes=63 * 2**20),
        name="adam",
    )(activations, input_grad, total, norm, vec_grad, *att, *inn, *out, *vec)


ALPHA_GATHER = (1, 1, 0, 1, 1, 0)
ALPHA_SCATTER = (0, 1, 0, 1, 1, 1)
ORDER = (
    ("init", 0), ("yown", 0), ("zown", 0), ("yown", 1), ("init2", 0), ("yown", 2), ("zown", 1), ("early", 0),
    ("t0", 0), ("a0", 0), ("a0", 1), ("zown", 2), ("t0", 1), ("a1", 0), ("zown", 3), ("yown", 3), ("t1", 0),
    ("a1", 1), ("a0", 2), ("t1", 1), ("t2", 0), ("zown", 4), ("t2", 1), ("a2", 0), ("a2", 1), ("yown", 4),
    ("a0", 3), ("t3", 0), ("yown", 5), ("t3", 1), ("t0", 3), ("zown", 5), ("a1", 3), ("a1", 2), ("f", 0),
    ("f", 1), ("g", 0), ("a0", 4), ("a2", 3), ("vec", 0), ("qk", 0), ("t1", 3), ("g", 1), ("t0", 2), ("v", 0),
    ("a1", 4), ("at", 0), ("t1", 2), ("at", 1), ("t2", 3), ("a2", 2), ("a0", 5), ("t2", 2), ("at", 2),
    ("t3", 3), ("a2", 4), ("at", 3), ("t3", 2), ("t0", 4), ("f", 2), ("a1", 5), ("at", 4), ("t1", 4),
    ("f", 3), ("t0", 5), ("at", 5), ("t2", 4), ("wo", 0), ("t3", 4), ("g", 2), ("g", 3), ("a2", 5), ("F", 2),
    ("F", 3), ("f", 4), ("t1", 5), ("F", 0), ("t2", 5), ("t3", 5), ("f", 5), ("g", 4), ("F", 1), ("g", 5),
    ("o", 4), ("o", 5), ("ln2", 0), ("agf", 0), ("D", 1), ("G", 0), ("s1", 0), ("G", 1), ("p2", 0), ("s1", 1),
    ("r1", 1), ("D", 0), ("D", 2), ("D", 3), ("p3", 0), ("p1", 0), ("r1", 0), ("H", 0), ("q2", 0), ("H", 1),
    ("H", 2), ("G", 2), ("G", 3), ("s1", 2), ("r1", 2), ("p1", 2), ("H", 3), ("ln1", 0), ("p2", 2), ("q3", 0),
    ("dc", 0), ("p2", 1), ("p3", 2), ("s1", 3), ("ab", 0), ("p0", 0), ("ab", 1), ("r1", 3), ("ab", 2),
    ("ab", 3), ("q2", 2), ("ab", 4), ("ab", 5), ("dq", 0), ("q1", 0), ("p1", 3), ("p3", 1), ("q0", 0),
    ("G", 4), ("s1", 4), ("p1", 1), ("p3", 3), ("q2", 1), ("p0", 2), ("q3", 2), ("V", 0), ("q1", 2),
    ("p0", 3), ("G", 5), ("q1", 3), ("p2", 3), ("p1", 4), ("s1", 5), ("ig", 0), ("V", 1), ("p0", 1),
    ("q3", 3), ("r1", 4), ("q3", 1), ("q1", 1), ("q0", 3), ("r1", 5), ("p3", 4), ("q2", 3), ("p2", 4),
    ("q0", 1), ("p2", 5), ("p1", 5), ("V", 2), ("s4", 0), ("q1", 4), ("p0", 4), ("q2", 4), ("q0", 4),
    ("q2", 5), ("q0", 2), ("p3", 5), ("s4", 2), ("s4", 3), ("q1", 5), ("p0", 5), ("q3", 5), ("q3", 4),
    ("q0", 5), ("s4", 1), ("V", 3), ("s4", 5), ("s5", 0), ("s5", 2), ("s4", 4), ("s5", 3), ("N", 0), ("V", 4),
    ("s5", 1), ("s5", 5), ("N", 1), ("s6", 3), ("s6", 0), ("s6", 1), ("s5", 4), ("s6", 4), ("s6", 2),
    ("N", 2), ("s6", 5), ("fin", 0),
)

def plain_body(
    tokens,
    segment_ids,
    cotangent,
    attention_weight,
    attention_first,
    attention_second,
    inner_weight,
    inner_first,
    inner_second,
    outer_weight,
    outer_first,
    outer_second,
    vectors,
    vector_first,
    vector_second,
):
    row_count, seq_length, model_width = tokens.shape
    token_count = row_count * seq_length
    flat_rows = tokens.reshape(token_count, model_width)
    shards = (
        attention_weight.astype(jnp.bfloat16),
        inner_weight.astype(jnp.bfloat16),
        outer_weight.astype(jnp.bfloat16),
        vectors.astype(jnp.bfloat16),
    )
    attention_full, inner_full, outer_full, vector_full = (
        lax.all_gather(shards[0], "fsdp", axis=1, tiled=True),
        lax.all_gather(shards[1], "fsdp", axis=0, tiled=True),
        lax.all_gather(shards[2], "fsdp", axis=0, tiled=True),
        lax.all_gather(shards[3], "fsdp", axis=1, tiled=True),
    )
    vector_rows = vector_full.astype(jnp.float32)
    bias_query = vector_rows[0]
    bias_value = vector_rows[1]
    bias_output = vector_rows[2]
    gain_one = vector_rows[3]
    shift_one = vector_rows[4]
    bias_inner = vector_rows[5:9].reshape(-1)
    bias_outer = vector_rows[9]
    gain_two = vector_rows[10]
    shift_two = vector_rows[11]
    projected = jnp.einsum(
        "td,kde->kte", flat_rows, attention_full[:3], preferred_element_type=jnp.float32
    )
    queries = ((projected[0] + bias_query) * 0.125).astype(jnp.bfloat16)
    key_rows = projected[1].astype(jnp.bfloat16)
    value_rows = (projected[2] + bias_value).astype(jnp.bfloat16)
    row_view = (row_count, seq_length, model_width)
    query_view = queries.reshape(row_view)
    key_view = key_rows.reshape(row_view)
    value_view = value_rows.reshape(row_view)
    context, log_totals = lax.map(attend_row, (query_view, key_view, value_view, segment_ids))
    context_flat = context.reshape(token_count, model_width)
    attention_out = (
        jnp.dot(context_flat, attention_full[3], preferred_element_type=jnp.float32) + bias_output
    )
    sum_one = flat_rows.astype(jnp.float32) + attention_out
    hidden_one, norm_one_back = jax.vjp(layer_norm, sum_one, gain_one, shift_one)
    hidden_low = hidden_one.astype(jnp.bfloat16)
    inner_pre = jnp.dot(hidden_low, inner_full, preferred_element_type=jnp.float32) + bias_inner
    activated, gelu_back = jax.vjp(gelu_exact, inner_pre)
    activated_low = activated.astype(jnp.bfloat16)
    outer_pre = jnp.dot(activated_low, outer_full, preferred_element_type=jnp.float32) + bias_outer
    sum_two = hidden_one + outer_pre
    output, norm_two_back = jax.vjp(layer_norm, sum_two, gain_two, shift_two)
    activations = output.astype(jnp.bfloat16).reshape(row_view)
    attention_back, inner_back, outer_back = (
        lax.all_gather(shards[0], "fsdp", axis=1, tiled=True),
        lax.all_gather(shards[1], "fsdp", axis=0, tiled=True),
        lax.all_gather(shards[2], "fsdp", axis=0, tiled=True),
    )
    output_grad = cotangent.reshape(token_count, model_width).astype(jnp.float32)
    sum_two_grad, gain_two_grad, shift_two_grad = norm_two_back(output_grad)
    outer_grad = sum_two_grad.astype(jnp.bfloat16)
    outer_weight_grad = jnp.einsum(
        "tf,td->fd", activated_low, outer_grad, preferred_element_type=jnp.float32
    )
    bias_outer_grad = jnp.sum(outer_grad.astype(jnp.float32), axis=0)
    activated_grad = jnp.einsum(
        "td,fd->tf", outer_grad, outer_back, preferred_element_type=jnp.float32
    )
    (inner_raw_grad,) = gelu_back(activated_grad)
    inner_grad = inner_raw_grad.astype(jnp.bfloat16)
    inner_weight_grad = jnp.einsum(
        "td,tf->df", hidden_low, inner_grad, preferred_element_type=jnp.float32
    )
    bias_inner_grad = jnp.sum(inner_grad.astype(jnp.float32), axis=0)
    hidden_one_grad = sum_two_grad + jnp.einsum(
        "tf,df->td", inner_grad, inner_back, preferred_element_type=jnp.float32
    )
    sum_one_grad, gain_one_grad, shift_one_grad = norm_one_back(hidden_one_grad)
    attention_grad = sum_one_grad.astype(jnp.bfloat16)
    output_weight_grad = jnp.einsum(
        "td,te->de", context_flat, attention_grad, preferred_element_type=jnp.float32
    )
    bias_output_grad = jnp.sum(attention_grad.astype(jnp.float32), axis=0)
    context_grad = jnp.einsum(
        "te,de->td", attention_grad, attention_back[3], preferred_element_type=jnp.float32
    ).astype(jnp.bfloat16)
    query_grad, key_grad, value_grad = lax.map(
        attend_back,
        (query_view, key_view, value_view, segment_ids, log_totals, context_grad.reshape(row_view)),
    )
    query_grad = query_grad.reshape(token_count, model_width)
    key_grad = key_grad.reshape(token_count, model_width)
    value_grad = value_grad.reshape(token_count, model_width)
    grad_stack = jnp.stack([query_grad, key_grad, value_grad])
    projection_grad = jnp.einsum(
        "td,kte->kde", flat_rows, grad_stack, preferred_element_type=jnp.float32
    )
    projection_grad = projection_grad * jnp.array([0.125, 1.0, 1.0], jnp.float32)[:, None, None]
    attention_weight_grad = jnp.concatenate([projection_grad, output_weight_grad[None]], axis=0)
    bias_query_grad = 0.125 * jnp.sum(query_grad.astype(jnp.float32), axis=0)
    bias_value_grad = jnp.sum(value_grad.astype(jnp.float32), axis=0)
    token_grad = sum_one_grad + 0.125 * jnp.einsum(
        "te,de->td", query_grad, attention_back[0], preferred_element_type=jnp.float32
    )
    token_grad = token_grad + jnp.einsum(
        "kte,kde->td", grad_stack[1:], attention_back[1:3], preferred_element_type=jnp.float32
    )
    input_grad = token_grad.reshape(row_view)
    vector_grad = jnp.concatenate(
        [
            jnp.stack(
                [bias_query_grad, bias_value_grad, bias_output_grad, gain_one_grad, shift_one_grad]
            ),
            bias_inner_grad.reshape(4, model_width),
            jnp.stack([bias_outer_grad, gain_two_grad, shift_two_grad]),
        ],
        axis=0,
    )
    shard_grads = (
        lax.psum_scatter(
            attention_weight_grad.astype(jnp.bfloat16), "fsdp", scatter_dimension=1, tiled=True
        ).astype(jnp.float32),
        lax.psum_scatter(
            inner_weight_grad.astype(jnp.bfloat16), "fsdp", scatter_dimension=0, tiled=True
        ).astype(jnp.float32),
        lax.psum_scatter(
            outer_weight_grad.astype(jnp.bfloat16), "fsdp", scatter_dimension=0, tiled=True
        ).astype(jnp.float32),
        lax.psum_scatter(
            vector_grad.astype(jnp.bfloat16), "fsdp", scatter_dimension=1, tiled=True
        ).astype(jnp.float32),
    )
    summed = (
        lax.psum(shard_grads[0].astype(jnp.bfloat16), "dp").astype(jnp.float32),
        lax.psum(shard_grads[1].astype(jnp.bfloat16), "dp").astype(jnp.float32),
        lax.psum(shard_grads[2].astype(jnp.bfloat16), "dp").astype(jnp.float32),
        lax.psum(shard_grads[3].astype(jnp.bfloat16), "dp").astype(jnp.float32),
    )
    local_squares = (
        jnp.sum(summed[0] * summed[0])
        + jnp.sum(summed[1] * summed[1])
        + jnp.sum(summed[2] * summed[2])
        + jnp.sum(summed[3] * summed[3])
    )
    total_squares = lax.psum(local_squares, "fsdp")
    grad_norm = jnp.sqrt(total_squares)
    factor = CLIP / (grad_norm + 1e-06)
    attention_new, attention_first_new, attention_second_new = adam_update(
        attention_weight, attention_first, attention_second, summed[0], factor, RATE_MATRIX
    )
    inner_new, inner_first_new, inner_second_new = adam_update(
        inner_weight, inner_first, inner_second, summed[1], factor, RATE_MATRIX
    )
    outer_new, outer_first_new, outer_second_new = adam_update(
        outer_weight, outer_first, outer_second, summed[2], factor, RATE_MATRIX
    )
    vectors_new, vector_first_new, vector_second_new = adam_update(
        vectors, vector_first, vector_second, summed[3], factor, RATE_VECTOR
    )
    clipped_vectors = summed[3] * factor
    return (
        activations,
        input_grad,
        grad_norm,
        attention_new,
        attention_first_new,
        attention_second_new,
        inner_new,
        inner_first_new,
        inner_second_new,
        outer_new,
        outer_first_new,
        outer_second_new,
        vectors_new,
        vector_first_new,
        vector_second_new,
        clipped_vectors,
    )


def fused_body(
    tokens,
    segment_ids,
    cotangent,
    attention_weight,
    attention_first,
    attention_second,
    inner_weight,
    inner_first,
    inner_second,
    outer_weight,
    outer_first,
    outer_second,
    vectors,
    vector_first,
    vector_second,
):
    _, seq_length, model_width = tokens.shape
    activations, input_grad, total, vec_grad, norm = whole_layer(
        tokens.reshape(seq_length, model_width),
        cotangent.reshape(seq_length, model_width),
        segment_ids,
        attention_weight,
        inner_weight,
        outer_weight,
        vectors,
        ORDER,
        ALPHA_GATHER,
        ALPHA_SCATTER,
    )
    found = adam_step(
        activations,
        input_grad,
        norm,
        vec_grad,
        total,
        (attention_weight, attention_first, attention_second),
        (inner_weight, inner_first, inner_second),
        (outer_weight, outer_first, outer_second),
        (vectors, vector_first, vector_second),
    )
    return (found[0][None], found[1][None], found[2].reshape(()), *found[3:])


def solution(mesh):
    placed = (
        P(("dp", "fsdp"), None, None),
        P(("dp", "fsdp"), None),
        P(("dp", "fsdp"), None, None),
        P(None, "fsdp", None),
        P(None, "fsdp", None),
        P(None, "fsdp", None),
        P("fsdp", None),
        P("fsdp", None),
        P("fsdp", None),
        P("fsdp", None),
        P("fsdp", None),
        P("fsdp", None),
        P(None, "fsdp"),
        P(None, "fsdp"),
        P(None, "fsdp"),
    )
    fused = mesh.shape["dp"] == 4 and mesh.shape["fsdp"] == 8
    return jax.shard_map(
        fused_body if fused else plain_body,
        mesh=mesh,
        in_specs=placed,
        out_specs=(
            P(("dp", "fsdp"), None, None),
            P(("dp", "fsdp"), None, None),
            P(),
            P(None, "fsdp", None),
            P(None, "fsdp", None),
            P(None, "fsdp", None),
            P("fsdp", None),
            P("fsdp", None),
            P("fsdp", None),
            P("fsdp", None),
            P("fsdp", None),
            P("fsdp", None),
            P(None, "fsdp"),
            P(None, "fsdp"),
            P(None, "fsdp"),
            P(None, "fsdp"),
        ),
        check_vma=False,
    )
```

```python
import functools

import jax
import jax.numpy as jnp
from jax import lax
from jax.experimental import pallas as pl
from jax.experimental.pallas import tpu as pltpu
from jax.sharding import PartitionSpec as P

HEADS = 12
STEP = 10


EPS_NORM = 1e-12
BETA_ONE = 0.9
BETA_TWO = 0.999
ADAM_EPS = 1e-08
DECAY = 0.01
RATE_MATRIX = 0.03
RATE_VECTOR = 0.5
CLIP = 1.0


def layer_norm(resid, gain, shift):
    centre = jnp.mean(resid, axis=-1, keepdims=True)
    centered = resid - centre
    spread = jnp.mean(centered * centered, axis=-1, keepdims=True)
    return centered * lax.rsqrt(spread + EPS_NORM) * gain + shift


def gelu_exact(values):
    return jax.nn.gelu(values, approximate=False)


def split_heads(matrix):
    return matrix.reshape(matrix.shape[0], HEADS, matrix.shape[1] // HEADS)


def row_scores(query_row, key_row, segment_row):
    scores = jnp.einsum(
        "qhe,khe->hqk",
        split_heads(query_row),
        split_heads(key_row),
        preferred_element_type=jnp.float32,
    )
    same_segment = segment_row[:, None] == segment_row[None, :]
    return jnp.where(same_segment[None], scores, -1000000000.0)


def attend_row(pieces):
    query_row, key_row, value_row, segment_row = pieces
    scores = row_scores(query_row, key_row, segment_row)
    row_peak = jnp.max(scores, axis=-1, keepdims=True)
    exponent = jnp.exp(scores - row_peak)
    row_total = jnp.sum(exponent, axis=-1, keepdims=True)
    softmax_rows = exponent / row_total
    mixture = jnp.einsum(
        "hqk,khe->qhe",
        softmax_rows.astype(jnp.bfloat16),
        split_heads(value_row),
        preferred_element_type=jnp.float32,
    )
    return (mixture.reshape(query_row.shape).astype(jnp.bfloat16), row_peak + jnp.log(row_total))


def attend_back(pieces):
    query_row, key_row, value_row, segment_row, log_total, context_grad = pieces
    row_shape = query_row.shape
    scores = row_scores(query_row, key_row, segment_row)
    softmax_rows = jnp.exp(scores - log_total)
    grad_heads = split_heads(context_grad)
    prob_grad = jnp.einsum(
        "qhe,khe->hqk", grad_heads, split_heads(value_row), preferred_element_type=jnp.float32
    )
    value_grad = jnp.einsum(
        "hqk,qhe->khe",
        softmax_rows.astype(jnp.bfloat16),
        grad_heads,
        preferred_element_type=jnp.float32,
    )
    row_delta = jnp.sum(prob_grad * softmax_rows, axis=-1, keepdims=True)
    score_grad = (softmax_rows * (prob_grad - row_delta)).astype(jnp.bfloat16)
    query_grad = jnp.einsum(
        "hqk,khe->qhe", score_grad, split_heads(key_row), preferred_element_type=jnp.float32
    )
    key_grad = jnp.einsum(
        "hqk,qhe->khe", score_grad, split_heads(query_row), preferred_element_type=jnp.float32
    )
    return (
        query_grad.reshape(row_shape).astype(jnp.bfloat16),
        key_grad.reshape(row_shape).astype(jnp.bfloat16),
        value_grad.reshape(row_shape).astype(jnp.bfloat16),
    )


def adam_update(weight, first, second, gradient, factor, rate):
    clipped = gradient * factor
    first_new = BETA_ONE * first + (1.0 - BETA_ONE) * clipped
    second_new = BETA_TWO * second + (1.0 - BETA_TWO) * clipped * clipped
    first_hat = first_new / (1.0 - BETA_ONE**STEP)
    second_hat = second_new / (1.0 - BETA_TWO**STEP)
    weight_new = weight - rate * (first_hat / (jnp.sqrt(second_hat) + ADAM_EPS) + DECAY * weight)
    return (weight_new, first_new, second_new)


F32, BF16 = jnp.float32, jnp.bfloat16
MESH = pl.DeviceIdType.MESH
BLOCKS = 6
CHUNKS = 6
INV_SQRT2 = 0.7071067811865476
INV_SQRT2PI = 0.3989422804014327


def dot_nn(a, b):
    return lax.dot_general(a, b, (((1,), (0,)), ((), ())), preferred_element_type=F32)


def dot_nt(a, b):
    return lax.dot_general(a, b, (((1,), (1,)), ((), ())), preferred_element_type=F32)


def dot_tn(a, b):
    return lax.dot_general(a, b, (((0,), (0,)), ((), ())), preferred_element_type=F32)


def wide(value):
    return value.astype(F32)


class Place:
    def __init__(self):
        dp, fsdp = lax.axis_index("dp"), lax.axis_index("fsdp")
        self.x, self.c, self.z, self.y = dp // 2, dp % 2, fsdp // 2, fsdp % 2

    def dev(self, x=None, c=None, z=None, y=None):
        x = self.x if x is None else x
        c = self.c if c is None else c
        z = self.z if z is None else z
        y = self.y if y is None else y
        return (x * 2 + c, z * 2 + y)

    def far(self, dz):
        return lax.rem(self.z + dz, 4)


def half(x):
    return pl.ds(pl.multiple_of(x * 384, 128), 384)


def remote(src, dst, send, recv, dev):
    return pltpu.make_async_remote_copy(
        src_ref=src, dst_ref=dst, send_sem=send, recv_sem=recv, device_id=dev, device_id_type=MESH
    )


def at_one(index):
    return index.start if isinstance(index, slice) else index


class Gather:
    def __init__(self, at, att, inn, out, sems, alpha):
        self.at, self.att, self.inn, self.out, self.alpha = at, att, inn, out, alpha
        self.zs, self.zr, self.ys, self.yr, self.xs, self.xr, self.cs, self.cr = sems

    def ref(self, i, z, y, x):
        c = self.at.c
        cols = slice(None) if x is None else half(x)
        if i < 2:
            return self.att.at[2 * i + c, z, y, :, cols]
        if i < 4:
            return self.inn.at[2 * (i - 2) + c, z, y, :, cols]
        return self.out.at[z, y, 2 * (i - 4) + c, :, cols]

    def whole(self, i, c):
        if i < 2:
            return self.att.at[2 * i + c]
        if i < 4:
            return self.inn.at[2 * (i - 2) + c]
        return self.out.at[:, :, 2 * (i - 4) + c]

    def zmove(self, i, s, right, sz):
        z = self.at.z
        dest = jnp.minimum(z + 1, 3) if right else jnp.maximum(z - 1, 0)
        r = self.ref(i, sz, self.at.y, self.at.x if self.alpha[i] == 1 else None)
        return remote(r, r, self.zs.at[i, 0 if right else 1], self.zr.at[i, at_one(sz)], self.at.dev(z=dest))

    def ymove(self, i, sz, recv=False):
        y = 1 - self.at.y if recv else self.at.y
        r = self.ref(i, sz, y, self.at.x if self.alpha[i] else None)
        return remote(r, r, self.ys.at[i], self.yr.at[i, at_one(sz)], self.at.dev(y=1 - self.at.y))

    def xmove(self, i, sz, own, recv=False):
        y = self.at.y if own else 1 - self.at.y
        x = 1 - self.at.x if recv else self.at.x
        k = 0 if own else 1
        r = self.ref(i, sz, y, x)
        return remote(r, r, self.xs.at[i, k], self.xr.at[i, k], self.at.dev(x=1 - self.at.x))

    def cmove(self, i, recv=False):
        r = self.whole(i, 1 - self.at.c if recv else self.at.c)
        return remote(r, r, self.cs.at[i], self.cr.at[i], self.at.dev(c=1 - self.at.c))

    def zown(self, i):
        z = self.at.z

        @pl.when(z < 3)
        def _():
            self.zmove(i, 0, True, z).start()

        @pl.when(z > 0)
        def _():
            self.zmove(i, 0, False, z).start()

    def yown(self, i):
        self.ymove(i, self.at.z).start()

    def arrive(self, i, s):
        z = self.at.z

        def forward(sz, right, more):
            self.zmove(i, s, right, sz).wait_recv()
            if s < 2:

                @pl.when(more)
                def _():
                    self.zmove(i, s + 1, right, sz).start()

            self.ymove(i, sz).start()
            if self.alpha[i] == 1:
                self.xmove(i, sz, True).start()

        @pl.when(z >= 1 + s)
        def _():
            forward(jnp.maximum(z - 1 - s, 0), True, z < 3)

        @pl.when(z + 1 + s <= 3)
        def _():
            forward(jnp.minimum(z + 1 + s, 3), False, z > 0)

    def across(self, i, s):
        z = self.at.z

        def one(sz):
            self.ymove(i, sz, True).wait_recv()
            if self.alpha[i]:
                self.xmove(i, sz, False).start()

        if s == 0:
            one(z)
            return

        @pl.when(z >= s)
        def _():
            one(jnp.maximum(z - s, 0))

        @pl.when(z + s <= 3)
        def _():
            one(jnp.minimum(z + s, 3))

    def join(self, i):
        if self.alpha[i]:
            self.xmove(i, slice(0, 4), False, True).wait_recv()
        if self.alpha[i] == 1:
            self.xmove(i, slice(0, 3), True, True).wait_recv()
        self.cmove(i).start()

    def have(self, i):
        self.cmove(i, True).wait_recv()

    def finish(self):
        z = self.at.z
        for i in range(BLOCKS):
            for count in (1, 2, 3):

                @pl.when(z + 1 == count)
                def _():
                    self.zmove(i, 0, True, slice(0, count)).wait_send()

                @pl.when(4 - z == count)
                def _():
                    self.zmove(i, 0, False, slice(0, count)).wait_send()

            self.ymove(i, slice(0, 4)).wait_send()
            if self.alpha[i]:
                self.xmove(i, slice(0, 4), False).wait_send()
            if self.alpha[i] == 1:
                self.xmove(i, slice(0, 3), True).wait_send()
            self.cmove(i).wait_send()


class Scatter:
    def __init__(self, at, grad, total, bufs, sems, alpha):
        self.at, self.grad, self.total, self.alpha = at, grad, total, alpha
        self.ra1, self.ra2, self.ra3, self.rb1, self.rb2, self.rb3 = bufs
        self.ss, self.rs = sems
        self.slot = [sum(1 for q in alpha[:j] if q == alpha[j]) for j in range(CHUNKS)]

    def cp(self, j, kind, k, src, dst, dev):
        return remote(src, dst, self.ss.at[j, kind], self.rs.at[j, k], dev)

    def block(self, j, c):
        return 4 * (j // 2) + 2 * c + j % 2

    def firsts(self, j, dz, own):
        n, at = self.slot[j], self.at
        z = at.far(dz)
        if self.alpha[j]:
            y = at.y if own else 1 - at.y
            return self.cp(
                j, own, dz + 4 * own, self.grad(j, z, y).at[:, half(1 - at.x)], self.ra1.at[n, z, y], at.dev(x=1 - at.x)
            )
        return self.cp(j, 0, dz, self.grad(j, z, 1 - at.y), self.rb1.at[n, z], at.dev(y=1 - at.y))

    def second(self, j, dz):
        n, at = self.slot[j], self.at
        z = at.far(dz)
        return self.cp(
            j, 2, 8 + dz, self.grad(j, z, 1 - at.y).at[:, half(at.x)], self.ra2.at[n, z], at.dev(y=1 - at.y)
        )

    def third(self, j, dz):
        n, at = self.slot[j], self.at
        z = at.far(dz)
        src = self.grad(j, z, at.y)
        if self.alpha[j]:
            return self.cp(j, 3, 12, src.at[:, half(at.x)], self.ra3.at[n, dz - 1], at.dev(z=z))
        return self.cp(j, 3, 12, src, self.rb2.at[n, dz - 1], at.dev(z=z))

    def fourth(self, j, recv=False):
        n, at = self.slot[j], self.at
        if self.alpha[j]:
            r = self.total.at[self.block(j, at.c), :, half(1 - at.x if recv else at.x)]
            return self.cp(j, 4, 13, r, r, at.dev(x=1 - at.x))
        return self.cp(j, 4, 13, self.grad(j, at.z, at.y), self.rb3.at[n], at.dev(x=1 - at.x))

    def fifth(self, j, recv=False):
        r = self.total.at[self.block(j, 1 - self.at.c if recv else self.at.c)]
        return self.cp(j, 5, 14, r, r, self.at.dev(c=1 - self.at.c))

    def s1(self, j):
        if j == 0:
            return
        for dz in (2, 1, 3, 0):
            self.firsts(j, dz, 0).start()

    def r1(self, j):
        if self.alpha[j]:
            for dz in (2, 1, 3, 0):
                self.firsts(j, dz, 1).start()

    def p(self, j, dz):
        if not self.alpha[j]:
            return
        n, at = self.slot[j], self.at
        z, y, h = at.far(dz), 1 - at.y, half(at.x)
        self.firsts(j, dz, 0).wait_recv()
        r = self.grad(j, z, y)
        r[:, h] = (wide(r[:, h]) + wide(self.ra1[n, z, y])).astype(BF16)
        self.second(j, dz).start()

    def q(self, j, dz):
        n, at = self.slot[j], self.at
        z, y, h = at.far(dz), at.y, half(at.x)
        r = self.grad(j, z, y)
        if self.alpha[j]:
            self.firsts(j, dz, 1).wait_recv()
            self.second(j, dz).wait_recv()
            r[:, h] = (wide(r[:, h]) + wide(self.ra1[n, z, y]) + wide(self.ra2[n, z])).astype(BF16)
        else:
            self.firsts(j, dz, 0).wait_recv()
            r[...] = (wide(r[...]) + wide(self.rb1[n, z])).astype(BF16)
        if dz:
            self.third(j, dz).start()

    def s4(self, j):
        n, at = self.slot[j], self.at
        landed = (self.ra3 if self.alpha[j] else self.rb2).at[n]
        remote(landed, landed, self.ss.at[j, 3], self.rs.at[j, 12], at.dev(z=at.far(1))).wait_recv()
        r = self.grad(j, at.z, at.y)
        if self.alpha[j]:
            h = half(at.x)
            total = wide(r[:, h])
            for dz in range(3):
                total = total + wide(self.ra3[n, dz])
            self.total[self.block(j, at.c), :, h] = total.astype(BF16)
        else:
            total = wide(r[...])
            for dz in range(3):
                total = total + wide(self.rb2[n, dz])
            r[...] = total.astype(BF16)
        self.fourth(j).start()

    def s5(self, j):
        n, at = self.slot[j], self.at
        self.fourth(j, True).wait_recv()
        if not self.alpha[j]:
            r = self.grad(j, at.z, at.y)
            self.total[self.block(j, at.c)] = (wide(r[...]) + wide(self.rb3[n])).astype(BF16)
        self.fifth(j).start()

    def s6(self, j):
        self.fifth(j, True).wait_recv()

    def finish(self):
        at = self.at
        for j in range(CHUNKS):
            n = self.slot[j]
            first = (self.ra2 if self.alpha[j] else self.rb1).at[n]
            last = (self.ra3 if self.alpha[j] else self.rb2).at[n]
            sent = [(0, first)]
            if self.alpha[j]:
                sent += [(1, first), (2, first)]
            for kind, like in sent + [(3, last)]:
                remote(like, like, self.ss.at[j, kind], self.rs.at[j, 0], at.dev(x=1 - at.x)).wait_send()
            self.fourth(j).wait_send()
            self.fifth(j).wait_send()


def layer_kernel(
    order, alpha_gather, alpha_scatter,
    tok_h, cot_h, seg_h, watt_h, winn_h, wout_h, vec_h,
    act_h, grad_h, total_h, vec_grad, norm,
    att, inn, out, norm_one, resid, work, pair_in, stack, hidden, outer_grad, shown, turn, turn_two,
    active, slope, probs, mask, vec, dev_one, dev_two,
    sib_in, sib_hidden, sib_active, sib_outer, sib_slope, sib_stack,
    grad_out, ra1, ra2, ra3, rb1, rb2, rb3,
    vec_parts, vec_sib, vec_x, vec_y, vec_z, norm_parts, mate_parts, total, seg_row, vec_in,
    zs, zr, ys, yr, xs, xr, cs, cr, ss, rs, bs, br, vs, vr, ws, wr, ns, nr, ls,
):
    at = Place()
    me = at.z * 2 + at.y
    ag = Gather(at, att, inn, out, (zs, zr, ys, yr, xs, xr, cs, cr), alpha_gather)

    def grad_ref(j, z, y):
        return grad_out.at[j, z, y] if j < 2 else out.at[z, y, j - 2]

    rd = Scatter(at, grad_ref, total, (ra1, ra2, ra3, rb1, rb2, rb3), (ss, rs), alpha_scatter)

    def square(ref, n=768):
        return ref[...].reshape(n, n)

    other = at.dev(c=1 - at.c)

    def to_sibling(k, src, dst):
        return remote(src, dst, bs.at[k], br.at[k], other)

    sib_tokens = to_sibling(0, pair_in.at[0], sib_in.at[0])
    sib_context = to_sibling(1, pair_in.at[1], sib_in.at[1])
    sib_hid = to_sibling(2, hidden, sib_hidden)
    sib_act = to_sibling(3, active.at[:, :, pl.ds(2 * (1 - at.c), 2)], sib_active)
    sib_og = [
        to_sibling(k, outer_grad.at[pl.ds(128 * r, 128)], sib_outer.at[pl.ds(128 * r, 128)])
        for r, k in enumerate((4, 8, 9, 10))
    ]
    sib_sl = to_sibling(5, slope.at[:, pl.ds(pl.multiple_of((1 - at.c) * 1536, 128), 1536)], sib_slope)
    sib_first = to_sibling(6, stack.at[1 - at.c], sib_stack.at[0])
    sib_last = to_sibling(7, stack.at[3 - at.c], sib_stack.at[1])

    peers = [(dz, dy) for dz in range(4) for dy in range(2) if (dz, dy) != (0, 0)]

    def peer(dz, dy):
        return at.dev(z=at.far(dz), y=lax.rem(at.y + dy, 2))

    def vec_move(k):
        dz, dy = peers[k]
        return remote(vec_parts.at[me], vec_parts.at[me], vs.at[0], vr.at[0], peer(dz, dy))

    def norm_move(k):
        return remote(norm_parts.at[me], norm_parts.at[me], ns.at[0], nr.at[0], peer(*peers[k]))

    mates = [at.dev(x=1 - at.x), at.dev(x=1 - at.x, c=1 - at.c), other]
    rank = at.x * 2 + at.c

    def mate_move(k):
        return remote(mate_parts.at[rank], mate_parts.at[rank], ns.at[1], nr.at[1], mates[k])

    def all_of(ref, count, send, recv):
        view = ref.at[pl.ds(0, count)]
        return remote(view, view, send, recv, other)

    loads = []
    for i in range(2):
        k, rows = 2 * i + at.c, pl.ds(96 * i, 96)
        cols, shard_rows = pl.ds(pl.multiple_of(768 * k, 128), 768), pl.ds(pl.multiple_of(96 * k, 96), 96)
        loads.append(pltpu.make_async_copy(watt_h.at[k], norm_one.at[rows], ls.at[3 * i]))
        loads.append(pltpu.make_async_copy(winn_h.at[:, cols], work.at[rows], ls.at[3 * i + 1]))
        loads.append(pltpu.make_async_copy(wout_h.at[shard_rows], resid.at[rows], ls.at[3 * i + 2]))
    load_tokens = pltpu.make_async_copy(tok_h, pair_in.at[0], ls.at[9])
    load_ids = pltpu.make_async_copy(seg_h, seg_row, ls.at[7])
    load_vectors = pltpu.make_async_copy(vec_h, vec_in, ls.at[8])
    load_cotangent = pltpu.make_async_copy(cot_h, stack.at[3], ls.at[10])
    store_shown = pltpu.make_async_copy(shown, act_h, ls.at[11])
    store_grad = pltpu.make_async_copy(work, grad_h, ls.at[12])

    def init():
        barrier = pltpu.get_barrier_semaphore()
        greet = [peer(dz, dy) for dz, dy in peers] + mates
        for d in greet:
            pl.semaphore_signal(barrier, inc=1, device_id=d, device_id_type=MESH)
        for k in (0, 3, 1, 4, 2, 5):
            loads[k].start()
        load_vectors.start()
        load_ids.start()
        load_tokens.start()
        load_cotangent.start()
        for i in range(2):
            loads[3 * i].wait()
            att[2 * i + at.c, at.z, at.y] = norm_one[pl.ds(96 * i, 96), :].astype(BF16)
        pl.semaphore_wait(barrier, len(greet))

    def cast_rest():
        for i in range(2):
            k, rows = 2 * i + at.c, pl.ds(96 * i, 96)
            loads[3 * i + 1].wait()
            inn[k, at.z, at.y] = work[rows, :].astype(BF16)
            loads[3 * i + 2].wait()
            out[at.z, at.y, k] = resid[rows, :].astype(BF16)
        vec_grad[...] = jnp.zeros_like(vec_grad)

    def early():
        load_vectors.wait()
        load_ids.wait()
        vec_parts[me] = jnp.zeros((16, 128), F32)
        vec_parts[me, :12, :96] = vec_in[...]
        for k in range(7):
            vec_move(k).start()
        load_tokens.wait()
        sib_tokens.start()
        ids = jnp.broadcast_to(seg_row[...].astype(F32), (512, 512))
        mask[...] = jnp.where(ids.T == ids, 1.0, 0.0)

    def vectors_here():
        all_of(vec_parts, 7, vs.at[0], vr.at[0]).wait_recv()
        full = jnp.zeros((16, 768), F32)
        row = lax.broadcasted_iota(jnp.int32, (128, 768), 0)
        col = lax.broadcasted_iota(jnp.int32, (128, 768), 1)
        for s in range(8):
            pick = jnp.where((col == row + 96 * s) & (row < 96), 1.0, 0.0).astype(BF16)
            full = full + dot_nn(vec_parts[s].astype(BF16), pick)
        vec[...] = full

    def vrow(r):
        return vec[pl.ds(r, 1), :]

    def queries_keys():
        tokens = pair_in[0]
        stack[0] = ((dot_nn(tokens, square(att.at[0])) + vrow(0)) * 0.125).astype(BF16)
        stack[2] = dot_nn(tokens, square(att.at[1])).astype(BF16)

    def values():
        stack[1] = (dot_nn(pair_in[0], square(att.at[2])) + vrow(1)).astype(BF16)

    low = lax.broadcasted_iota(jnp.int32, (512, 128), 1) < 64

    def attend(p):
        ls_ = pl.ds(128 * p, 128)
        queries, keys = stack[0, :, ls_], stack[2, :, ls_]
        values_t = stack[1, :, ls_].T
        for h in range(2):
            mine = jnp.where(low if h == 0 else ~low, keys, jnp.zeros_like(keys))
            scores = jnp.where(mask[...] > 0.5, dot_nt(mine, queries), -1000000000.0)
            peak = jnp.max(scores, axis=0, keepdims=True)
            exponent = jnp.exp(scores - peak)
            scale = 1.0 / jnp.sum(exponent, axis=0, keepdims=True)
            weights = (exponent * scale).astype(BF16)
            probs[2 * p + h] = weights
            turn[pl.ds(128 * p + 64 * h, 64), :] = dot_nn(values_t[64 * h : 64 * h + 64], weights).astype(BF16)

    def norm_stats(value):
        centre = jnp.mean(value, axis=1, keepdims=True)
        centered = value - centre
        spread = jnp.mean(centered * centered, axis=1, keepdims=True)
        scale = lax.rsqrt(spread + EPS_NORM)
        return centered * scale, scale

    def project_out():
        pair_in[1] = turn[...].T
        sib_context.start()
        resid[...] = wide(pair_in[0]) + dot_nn(pair_in[1], square(att.at[3])) + vrow(2)
        for r in range(4):
            rows = pl.ds(128 * r, 128)
            normed, scale = norm_stats(resid[rows, :])
            norm_one[rows, :] = normed
            dev_one[rows, :] = scale
            hidden[rows, :] = (normed * vrow(3) + vrow(4)).astype(BF16)
        sib_hid.start()

    def feed_in(q):
        work[...] = dot_nn(hidden[...], square(inn.at[q])) + vrow(5 + q)
        for r in range(4):
            rows = pl.ds(128 * r, 128)
            value = work[rows, :]
            share = 0.5 * (1.0 + lax.erf(value * INV_SQRT2))
            shown[rows, :] = (value * share).astype(BF16)
            density = jnp.exp(-0.5 * value * value) * INV_SQRT2PI
            slope[rows, 768 * q : 768 * q + 768] = (share + value * density).astype(BF16)
        active[q] = shown[...].T.reshape(2, 4, 96, 512)

    def feed_out(part):
        if part == 4:
            sib_act.start()
            resid[...] = norm_one[...] * vrow(3) + vrow(4) + vrow(9)
        q = 2 * (part - 4)
        for n in range(3):
            cols = slice(256 * n, 256 * n + 256)
            resid[:, cols] += dot_tn(
                active[:, :, q : q + 2].reshape(1536, 512), out[:, :, q : q + 2, :, cols].reshape(1536, 256)
            )

    def end_norm():
        load_cotangent.wait()
        sums = [jnp.zeros((1, 768), F32) for _ in range(3)]
        for r in range(4):
            rows = pl.ds(128 * r, 128)
            normed, scale = norm_stats(resid[rows, :])
            shown[rows, :] = (normed * vrow(10) + vrow(11)).astype(BF16)
            given = wide(stack[3, rows, :])
            scaled = given * vrow(10)
            back = scale * (
                scaled
                - jnp.mean(scaled, axis=1, keepdims=True)
                - normed * jnp.mean(scaled * normed, axis=1, keepdims=True)
            )
            work[rows, :] = back
            low_back = back.astype(BF16)
            outer_grad[rows, :] = low_back
            sib_og[r].start()
            for k, term in enumerate((wide(low_back), given * normed, given)):
                sums[k] = sums[k] + jnp.sum(term, axis=0, keepdims=True)
        for k in range(3):
            vec_grad[9 + k : 10 + k, :] = sums[k]
        store_shown.start()

    def inner_back(q):
        cols = slice(768 * q, 768 * q + 768)
        resid[...] = dot_nt(outer_grad[...], out[q].reshape(768, 768))
        total_row = jnp.zeros((1, 768), F32)
        for r in range(4):
            rows = pl.ds(128 * r, 128)
            value = (resid[rows, :] * wide(slope[rows, cols])).astype(BF16)
            slope[rows, cols] = value
            total_row = total_row + jnp.sum(wide(value), axis=0, keepdims=True)
        vec_grad[5 + q : 6 + q, :] = total_row
        if q == 3:
            sib_sl.start()

    def put_chunk(j, value):
        value = value.astype(BF16).reshape(4, 2, 96, 768)
        if j < 2:
            grad_out[j] = value
        else:
            out[:, :, j - 2] = value

    def chunk_out(j):
        if j == 0:
            sib_act.wait_recv()
            for cp in sib_og:
                cp.wait_recv()
            for dz in (2, 1, 3, 0):
                z = at.far(dz)
                mine = active[z, :, pl.ds(2 * at.c, 1)].reshape(192, 512)
                theirs = sib_active[z, :, 0].reshape(192, 512)
                value = dot_nn(mine, outer_grad[...]) + dot_nn(theirs, sib_outer[...])
                grad_out[0, z] = value.astype(BF16).reshape(2, 96, 768)
                rd.firsts(0, dz, 0).start()
            return
        mine = active[:, :, pl.ds(2 * at.c + j, 1)].reshape(768, 512)
        theirs = sib_active[:, :, j].reshape(768, 512)
        put_chunk(j, dot_nn(mine, outer_grad[...]) + dot_nn(theirs, sib_outer[...]))

    def chunk_in(j):
        if j == 2:
            sib_hid.wait_recv()
            sib_sl.wait_recv()
        cols = pl.ds(pl.multiple_of(at.c * 1536 + 768 * (j - 2), 128), 768)
        put_chunk(
            j,
            dot_tn(hidden[...], slope[:, cols])
            + dot_tn(sib_hidden[...], sib_slope[:, 768 * (j - 2) : 768 * (j - 1)]),
        )

    def chunk_attention(j):
        if j == 4:
            sib_tokens.wait_recv()
            sib_first.wait_recv()
            value = dot_tn(pair_in[0], stack[at.c]) + dot_tn(sib_in[0], sib_stack[0])
            put_chunk(j, value * jnp.where(at.c == 0, 0.125, 1.0))
        else:
            sib_context.wait_recv()
            sib_last.wait_recv()
            put_chunk(j, dot_tn(pair_in[at.c], stack[2 + at.c]) + dot_tn(sib_in[at.c], sib_stack[1]))

    def hidden_back(q):
        work[...] += dot_nt(slope[:, 768 * q : 768 * q + 768], square(inn.at[q]))

    def middle_norm():
        sums = [jnp.zeros((1, 768), F32) for _ in range(3)]
        for r in range(4):
            rows = pl.ds(128 * r, 128)
            given = work[rows, :]
            normed = norm_one[rows, :]
            scaled = given * vrow(3)
            back = dev_one[rows, :] * (
                scaled
                - jnp.mean(scaled, axis=1, keepdims=True)
                - normed * jnp.mean(scaled * normed, axis=1, keepdims=True)
            )
            work[rows, :] = back
            low_back = back.astype(BF16)
            stack[3, rows, :] = low_back
            for k, term in enumerate((wide(low_back), given * normed, given)):
                sums[k] = sums[k] + jnp.sum(term, axis=0, keepdims=True)
        for k in range(3):
            vec_grad[2 + k : 3 + k, :] = sums[k]

    def context_back():
        store_shown.wait()
        shown[...] = dot_nt(stack[3], square(att.at[3])).astype(BF16)

    def attend_back(p):
        ls_ = pl.ds(128 * p, 128)
        queries, keys, vals, given = stack[0, :, ls_], stack[2, :, ls_], stack[1, :, ls_], shown[:, ls_]
        keys_t = keys.T
        value_grads, key_grads = [], []
        for h in range(2):
            mine = jnp.where(low if h == 0 else ~low, vals, jnp.zeros_like(vals))
            prob_grad = dot_nt(mine, given)
            weights = probs[2 * p + h]
            wide_weights = wide(weights)
            delta = jnp.sum(prob_grad * wide_weights, axis=0, keepdims=True)
            score_grad = (wide_weights * (prob_grad - delta)).astype(BF16)
            value_grads.append(dot_nn(weights, given))
            key_grads.append(dot_nn(score_grad, queries))
            turn[pl.ds(128 * p + 64 * h, 64), :] = dot_nn(keys_t[64 * h : 64 * h + 64], score_grad).astype(BF16)
        stack[1, :, ls_] = jnp.where(low, value_grads[0], value_grads[1]).astype(BF16)
        stack[2, :, ls_] = jnp.where(low, key_grads[0], key_grads[1]).astype(BF16)

    def queries_back():
        stack[0] = turn[...].T
        sib_first.start()
        sib_last.start()
        vec_grad[0:1, :] = 0.125 * jnp.sum(wide(stack[0]), axis=0, keepdims=True)
        vec_grad[1:2, :] = jnp.sum(wide(stack[1]), axis=0, keepdims=True)

    def input_back():
        work[...] += (
            0.125 * dot_nt(stack[0], square(att.at[0]))
            + dot_nt(stack[2], square(att.at[1]))
            + dot_nt(stack[1], square(att.at[2]))
        )
        store_grad.start()

    def vec_sum(k):
        if k == 0:
            return remote(vec_grad, vec_sib, ws.at[0], wr.at[0], other)
        if k == 1:
            return remote(vec_grad, vec_x, ws.at[1], wr.at[1], at.dev(x=1 - at.x))
        if k == 2:
            return remote(vec_grad, vec_y, ws.at[2], wr.at[2], at.dev(y=1 - at.y))
        return remote(vec_z.at[at.z], vec_z.at[at.z], ws.at[3], wr.at[3], at.dev(z=at.far(k - 2)))

    def vec_step(k):
        if k == 0:
            vec_sum(0).start()
        elif k <= 2:
            vec_sum(k - 1).wait()
            vec_grad[...] += (vec_sib if k == 1 else vec_x)[...]
            vec_sum(k).start()
        elif k == 3:
            vec_sum(2).wait()
            vec_z[at.z] = vec_grad[...] + vec_y[...]
            for m in (3, 4, 5):
                vec_sum(m).start()
        else:
            all_of(vec_z, 3, ws.at[3], wr.at[3]).wait()
            vec_grad[...] = (vec_z[0] + vec_z[1]) + (vec_z[2] + vec_z[3])

    def norm_step(k):
        if k == 0:
            part = jnp.zeros((96, 384), F32)
            for j in range(CHUNKS):
                value = wide(total[rd.block(j, at.c), :, half(at.x)])
                part = part + value * value
            mate_parts[rank] = jnp.full((8, 128), jnp.sum(part), F32)
            for m in range(3):
                mate_move(m).start()
        elif k == 1:
            all_of(mate_parts, 3, ns.at[1], nr.at[1]).wait_recv()
            norm_parts[me] = (mate_parts[0] + mate_parts[1]) + (mate_parts[2] + mate_parts[3])
            for m in range(7):
                norm_move(m).start()
        else:
            own = jnp.sum(vec_grad[...] * vec_grad[...])
            all_of(norm_parts, 7, ns.at[0], nr.at[0]).wait_recv()
            sums = norm_parts[0]
            for s in range(1, 8):
                sums = sums + norm_parts[s]
            norm[...] = sums + own

    def chunk_done(j):
        rd.s6(j)
        for c in range(2):
            b = rd.block(j, c)
            pltpu.make_async_copy(total.at[b], total_h.at[b], ls.at[6]).start()

    def finish():
        all_of(vec_parts, 7, vs.at[0], vr.at[0]).wait_send()
        all_of(norm_parts, 7, ns.at[0], nr.at[0]).wait_send()
        all_of(mate_parts, 3, ns.at[1], nr.at[1]).wait_send()
        for cp in (sib_tokens, sib_context, sib_hid, sib_act, *sib_og, sib_sl, sib_first, sib_last):
            cp.wait_send()
        pltpu.make_async_copy(total, total_h, ls.at[6]).wait()
        store_grad.wait()
        rd.finish()

    run = {
        "init": init, "early": early, "vec": vectors_here, "qk": queries_keys, "v": values, "wo": project_out,
        "ln2": end_norm, "ln1": middle_norm, "dc": context_back, "dq": queries_back,
        "ig": input_back, "init2": cast_rest, "fin": finish, "agf": ag.finish,
    }
    steps = {
        "at": attend, "ab": attend_back, "F": feed_in, "o": feed_out, "D": inner_back, "H": hidden_back, "V": vec_step,
        "G": lambda j: (chunk_out, chunk_in, chunk_attention)[j // 2](j),
        "s1": rd.s1, "r1": rd.r1, "s4": rd.s4, "s5": rd.s5, "s6": chunk_done, "N": norm_step,
        "zown": ag.zown, "yown": ag.yown, "f": ag.join, "g": ag.have,
    }
    for k in range(4):
        steps[f"p{k}"] = functools.partial(rd.p, dz=k)
        steps[f"q{k}"] = functools.partial(rd.q, dz=k)
        steps[f"a{k}"] = functools.partial(ag.arrive, s=k)
        steps[f"t{k}"] = functools.partial(ag.across, s=k)
    for name, index in order:
        if name in run:
            run[name]()
        else:
            steps[name](index)


def whole_layer(tokens, cotangent, segments, watt, winn, wout, vectors_low, order, alpha_gather, alpha_scatter):
    na = max(1, sum(alpha_scatter))
    nb = max(1, CHUNKS - sum(alpha_scatter))
    vmem, dma = pltpu.VMEM, pltpu.SemaphoreType.DMA
    flat = (512, 768)
    scratch = [
        vmem((4, 4, 2, 96, 768), BF16), vmem((4, 4, 2, 96, 768), BF16), vmem((4, 2, 4, 96, 768), BF16),
        vmem(flat, F32), vmem(flat, F32), vmem(flat, F32),
        vmem((2,) + flat, BF16), vmem((4,) + flat, BF16), vmem(flat, BF16), vmem(flat, BF16), vmem(flat, BF16),
        vmem((768, 512), BF16), vmem((8, 128), BF16),
        vmem((4, 2, 4, 96, 512), BF16), vmem((512, 3072), BF16), vmem((12, 512, 512), BF16),
        vmem((512, 512), F32), vmem((16, 768), F32), vmem((512, 1), F32), vmem((8, 128), F32),
        vmem((2,) + flat, BF16), vmem(flat, BF16), vmem((4, 2, 2, 96, 512), BF16), vmem(flat, BF16),
        vmem((512, 1536), BF16), vmem((2,) + flat, BF16),
        vmem((2, 4, 2, 96, 768), BF16),
        vmem((na, 4, 2, 96, 384), BF16), vmem((na, 4, 96, 384), BF16), vmem((na, 3, 96, 384), BF16),
        vmem((nb, 4, 96, 768), BF16), vmem((nb, 3, 96, 768), BF16), vmem((nb, 96, 768), BF16),
        vmem((8, 16, 128), F32), vmem((16, 768), F32), vmem((16, 768), F32), vmem((16, 768), F32),
        vmem((4, 16, 768), F32), vmem((8, 8, 128), F32), vmem((4, 8, 128), F32), vmem((12, 96, 768), BF16),
        vmem((1, 512), jnp.int32), vmem((12, 96), F32),
    ]
    for n in (
        (BLOCKS, 2), (BLOCKS, 4), (BLOCKS,), (BLOCKS, 4), (BLOCKS, 2), (BLOCKS, 2), (BLOCKS,), (BLOCKS,),
        (CHUNKS, 6), (CHUNKS, 15), (11,), (11,), (1,), (1,), (4,), (4,), (2,), (2,), (13,),
    ):
        scratch.append(dma(n))
    local, far = pl.BlockSpec(memory_space=pltpu.VMEM), pl.BlockSpec(memory_space=pl.ANY)
    return pl.pallas_call(
        functools.partial(layer_kernel, order, alpha_gather, alpha_scatter),
        out_shape=[
            jax.ShapeDtypeStruct(flat, BF16), jax.ShapeDtypeStruct(flat, F32),
            jax.ShapeDtypeStruct((12, 96, 768), BF16), jax.ShapeDtypeStruct((16, 768), F32),
            jax.ShapeDtypeStruct((8, 128), F32),
        ],
        in_specs=[far] * 7,
        out_specs=[far, far, far, local, local],
        scratch_shapes=scratch,
        compiler_params=pltpu.CompilerParams(
            collective_id=0, has_side_effects=True, vmem_limit_bytes=63 * 2**20
        ),
        name="layer",
    )(
        tokens, cotangent, segments.reshape(1, 512), watt, winn, wout, vectors_low
    )


def adam_kernel(
    act_h, back_h, total_h, norm_ref, vec_ref,
    att_w, att_m, att_v, inn_w, inn_m, inn_v, out_w, out_m, out_v, vec_w, vec_m, vec_v,
    act_new, back_new, norm_new, att_wn, att_mn, att_vn, inn_wn, inn_mn, inn_vn, out_wn, out_mn, out_vn,
    vec_wn, vec_mn, vec_vn, vec_gn,
    hold, grads, act, back, loads, stores,
):
    parts = []
    for p in range(6):
        k = 2 * (p % 2)
        rows, cols = pl.ds(96 * k, 192), pl.ds(768 * k, 1536)
        if p < 2:
            parts.append((8 + k, [[r.at[pl.ds(k, 2)] for r in (w, n)] for w, n in (
                (att_w, att_wn), (att_m, att_mn), (att_v, att_vn))]))
        elif p < 4:
            parts.append((k, [[r.at[rows] for r in (w, n)] for w, n in (
                (out_w, out_wn), (out_m, out_mn), (out_v, out_vn))]))
        else:
            parts.append((4 + k, [[r.at[:, cols] for r in (w, n)] for w, n in (
                (inn_w, inn_wn), (inn_m, inn_mn), (inn_v, inn_vn))]))

    def slot(p, m):
        if p < 2:
            return hold[0].at[p, m]
        return hold[1].at[p - 2, m] if p < 4 else hold[2].at[p - 4, m]

    def load(p, m):
        return pltpu.make_async_copy(parts[p][1][m][0], slot(p, m), loads.at[p, m])

    def store(p, m):
        return pltpu.make_async_copy(slot(p, m), parts[p][1][m][1], stores.at[p, m])

    load_grads = [
        pltpu.make_async_copy(total_h.at[pl.ds(first, 4)], grads.at[pl.ds(first, 4)], loads.at[7, k])
        for k, first in enumerate((8, 0, 4))
    ]
    moves = [
        (pltpu.make_async_copy(src, mid, loads.at[6, k]), pltpu.make_async_copy(mid, dst, stores.at[6, k]))
        for k, (src, mid, dst) in enumerate(((act_h, act, act_new), (back_h, back, back_new)), 1)
    ]
    for p in range(6):
        if p % 2 == 0:
            load_grads[p // 2].start()
        for m in range(3):
            load(p, m).start()
        if p == 1:
            for first, _ in moves:
                first.start()
    length = jnp.sqrt(norm_ref[0:1, 0:1])
    factor = CLIP / (length + 1e-06)
    norm_new[...] = length
    shard = vec_w.shape[1]
    own = lax.axis_index("fsdp")
    grad = jnp.zeros(vec_w.shape, F32)
    for s in range(8):
        grad = grad + jnp.where(own == s, vec_ref[:12, shard * s : shard * s + shard], 0.0)
    found = adam_update(vec_w[...], vec_m[...], vec_v[...], grad, factor, RATE_VECTOR)
    for ref, value in zip((vec_wn, vec_mn, vec_vn), found):
        ref[...] = value
    vec_gn[...] = grad * factor
    for p in range(6):
        if p % 2 == 0:
            load_grads[p // 2].wait()
        for m in range(3):
            load(p, m).wait()
        for k in range(2):
            grad = grads[parts[p][0] + k].astype(F32)
            if p < 2:
                views = [slot(p, m).at[k] for m in range(3)]
            elif p < 4:
                views = [slot(p, m).at[pl.ds(96 * k, 96)] for m in range(3)]
            else:
                views = [slot(p, m).at[:, pl.ds(768 * k, 768)] for m in range(3)]
            found = adam_update(*(v[...] for v in views), grad, factor, RATE_MATRIX)
            for view, value in zip(views, found):
                view[...] = value
        for m in range(3):
            store(p, m).start()
        if p == 2:
            for first, second in moves:
                first.wait()
                second.start()
    for p in range(6):
        for m in range(3):
            store(p, m).wait()
    for _, second in moves:
        second.wait()


def adam_step(activations, input_grad, norm, vec_grad, total, att, inn, out, vec):
    near, far = pl.BlockSpec(memory_space=pltpu.VMEM), pl.BlockSpec(memory_space=pl.ANY)
    like = [jax.ShapeDtypeStruct(a.shape, F32) for a in (*att, *inn, *out, *vec, vec[0])]
    vmem, dma = pltpu.VMEM, pltpu.SemaphoreType.DMA
    hold = (vmem((2, 3, 2, 96, 768), F32), vmem((2, 3, 192, 768), F32), vmem((2, 3, 96, 1536), F32))
    return pl.pallas_call(
        adam_kernel,
        out_shape=[
            jax.ShapeDtypeStruct(activations.shape, BF16), jax.ShapeDtypeStruct(input_grad.shape, F32),
            jax.ShapeDtypeStruct((1, 1), F32), *like,
        ],
        in_specs=[far, far, far, near, near, *[far] * 9, *[near] * 3],
        out_specs=[far, far, near, *[far] * 9, *[near] * 4],
        scratch_shapes=[
            hold, vmem(total.shape, BF16), vmem(activations.shape, BF16), vmem(input_grad.shape, F32),
            dma((8, 3)), dma((7, 3)),
        ],
        compiler_params=pltpu.CompilerParams(vmem_limit_bytes=63 * 2**20),
        name="adam",
    )(activations, input_grad, total, norm, vec_grad, *att, *inn, *out, *vec)


ALPHA_GATHER = (1, 1, 0, 1, 1, 0)
ALPHA_SCATTER = (0, 1, 0, 1, 1, 1)
ORDER = (
    ("init", 0), ("yown", 0), ("zown", 0), ("yown", 1), ("init2", 0), ("yown", 2), ("zown", 1), ("early", 0),
    ("t0", 0), ("a0", 0), ("a0", 1), ("zown", 2), ("t0", 1), ("a1", 0), ("zown", 3), ("yown", 3), ("t1", 0),
    ("a1", 1), ("a0", 2), ("t1", 1), ("t2", 0), ("zown", 4), ("t2", 1), ("a2", 0), ("a2", 1), ("yown", 4),
    ("a0", 3), ("t3", 0), ("yown", 5), ("t3", 1), ("t0", 3), ("zown", 5), ("a1", 3), ("a1", 2), ("f", 0),
    ("f", 1), ("g", 0), ("a0", 4), ("a2", 3), ("vec", 0), ("qk", 0), ("t1", 3), ("g", 1), ("t0", 2), ("v", 0),
    ("a1", 4), ("at", 0), ("t1", 2), ("at", 1), ("t2", 3), ("a2", 2), ("a0", 5), ("t2", 2), ("at", 2),
    ("t3", 3), ("a2", 4), ("at", 3), ("t3", 2), ("t0", 4), ("f", 2), ("a1", 5), ("at", 4), ("t1", 4),
    ("f", 3), ("t0", 5), ("at", 5), ("t2", 4), ("wo", 0), ("t3", 4), ("g", 2), ("g", 3), ("a2", 5), ("F", 2),
    ("F", 3), ("f", 4), ("t1", 5), ("F", 0), ("t2", 5), ("t3", 5), ("f", 5), ("g", 4), ("F", 1), ("o", 4),
    ("g", 5), ("o", 5), ("ln2", 0), ("D", 1), ("G", 0), ("s1", 0), ("G", 1), ("p2", 0), ("s1", 1), ("r1", 1),
    ("D", 0), ("D", 2), ("D", 3), ("p3", 0), ("p1", 0), ("r1", 0), ("H", 0), ("q2", 0), ("H", 1), ("H", 2),
    ("agf", 0), ("G", 2), ("G", 3), ("s1", 2), ("r1", 2), ("p1", 2), ("H", 3), ("ln1", 0), ("p2", 2),
    ("q3", 0), ("dc", 0), ("p2", 1), ("p3", 2), ("s1", 3), ("ab", 0), ("p0", 0), ("ab", 1), ("r1", 3),
    ("ab", 2), ("ab", 3), ("q2", 2), ("ab", 4), ("ab", 5), ("dq", 0), ("q1", 0), ("p1", 3), ("p3", 1),
    ("q0", 0), ("G", 4), ("s1", 4), ("p1", 1), ("p3", 3), ("q2", 1), ("p0", 2), ("q3", 2), ("V", 0),
    ("q1", 2), ("p0", 3), ("G", 5), ("q1", 3), ("p2", 3), ("p1", 4), ("s1", 5), ("ig", 0), ("V", 1),
    ("p0", 1), ("q3", 3), ("r1", 4), ("q3", 1), ("q1", 1), ("q0", 3), ("r1", 5), ("p3", 4), ("q2", 3),
    ("p2", 4), ("q0", 1), ("p2", 5), ("p1", 5), ("V", 2), ("s4", 0), ("q1", 4), ("p0", 4), ("q2", 4),
    ("q0", 4), ("q2", 5), ("q0", 2), ("p3", 5), ("s4", 2), ("s4", 3), ("q1", 5), ("p0", 5), ("q3", 5),
    ("q3", 4), ("q0", 5), ("s4", 1), ("V", 3), ("s4", 5), ("s5", 0), ("s5", 2), ("s4", 4), ("s5", 3),
    ("N", 0), ("V", 4), ("s5", 1), ("s5", 5), ("N", 1), ("s6", 3), ("s6", 0), ("s6", 1), ("s5", 4), ("s6", 4),
    ("s6", 2), ("N", 2), ("s6", 5), ("fin", 0),
)

def plain_body(
    tokens,
    segment_ids,
    cotangent,
    attention_weight,
    attention_first,
    attention_second,
    inner_weight,
    inner_first,
    inner_second,
    outer_weight,
    outer_first,
    outer_second,
    vectors,
    vector_first,
    vector_second,
):
    row_count, seq_length, model_width = tokens.shape
    token_count = row_count * seq_length
    flat_rows = tokens.reshape(token_count, model_width)
    shards = (
        attention_weight.astype(jnp.bfloat16),
        inner_weight.astype(jnp.bfloat16),
        outer_weight.astype(jnp.bfloat16),
        vectors.astype(jnp.bfloat16),
    )
    attention_full, inner_full, outer_full, vector_full = (
        lax.all_gather(shards[0], "fsdp", axis=1, tiled=True),
        lax.all_gather(shards[1], "fsdp", axis=0, tiled=True),
        lax.all_gather(shards[2], "fsdp", axis=0, tiled=True),
        lax.all_gather(shards[3], "fsdp", axis=1, tiled=True),
    )
    vector_rows = vector_full.astype(jnp.float32)
    bias_query = vector_rows[0]
    bias_value = vector_rows[1]
    bias_output = vector_rows[2]
    gain_one = vector_rows[3]
    shift_one = vector_rows[4]
    bias_inner = vector_rows[5:9].reshape(-1)
    bias_outer = vector_rows[9]
    gain_two = vector_rows[10]
    shift_two = vector_rows[11]
    projected = jnp.einsum(
        "td,kde->kte", flat_rows, attention_full[:3], preferred_element_type=jnp.float32
    )
    queries = ((projected[0] + bias_query) * 0.125).astype(jnp.bfloat16)
    key_rows = projected[1].astype(jnp.bfloat16)
    value_rows = (projected[2] + bias_value).astype(jnp.bfloat16)
    row_view = (row_count, seq_length, model_width)
    query_view = queries.reshape(row_view)
    key_view = key_rows.reshape(row_view)
    value_view = value_rows.reshape(row_view)
    context, log_totals = lax.map(attend_row, (query_view, key_view, value_view, segment_ids))
    context_flat = context.reshape(token_count, model_width)
    attention_out = (
        jnp.dot(context_flat, attention_full[3], preferred_element_type=jnp.float32) + bias_output
    )
    sum_one = flat_rows.astype(jnp.float32) + attention_out
    hidden_one, norm_one_back = jax.vjp(layer_norm, sum_one, gain_one, shift_one)
    hidden_low = hidden_one.astype(jnp.bfloat16)
    inner_pre = jnp.dot(hidden_low, inner_full, preferred_element_type=jnp.float32) + bias_inner
    activated, gelu_back = jax.vjp(gelu_exact, inner_pre)
    activated_low = activated.astype(jnp.bfloat16)
    outer_pre = jnp.dot(activated_low, outer_full, preferred_element_type=jnp.float32) + bias_outer
    sum_two = hidden_one + outer_pre
    output, norm_two_back = jax.vjp(layer_norm, sum_two, gain_two, shift_two)
    activations = output.astype(jnp.bfloat16).reshape(row_view)
    attention_back, inner_back, outer_back = (
        lax.all_gather(shards[0], "fsdp", axis=1, tiled=True),
        lax.all_gather(shards[1], "fsdp", axis=0, tiled=True),
        lax.all_gather(shards[2], "fsdp", axis=0, tiled=True),
    )
    output_grad = cotangent.reshape(token_count, model_width).astype(jnp.float32)
    sum_two_grad, gain_two_grad, shift_two_grad = norm_two_back(output_grad)
    outer_grad = sum_two_grad.astype(jnp.bfloat16)
    outer_weight_grad = jnp.einsum(
        "tf,td->fd", activated_low, outer_grad, preferred_element_type=jnp.float32
    )
    bias_outer_grad = jnp.sum(outer_grad.astype(jnp.float32), axis=0)
    activated_grad = jnp.einsum(
        "td,fd->tf", outer_grad, outer_back, preferred_element_type=jnp.float32
    )
    (inner_raw_grad,) = gelu_back(activated_grad)
    inner_grad = inner_raw_grad.astype(jnp.bfloat16)
    inner_weight_grad = jnp.einsum(
        "td,tf->df", hidden_low, inner_grad, preferred_element_type=jnp.float32
    )
    bias_inner_grad = jnp.sum(inner_grad.astype(jnp.float32), axis=0)
    hidden_one_grad = sum_two_grad + jnp.einsum(
        "tf,df->td", inner_grad, inner_back, preferred_element_type=jnp.float32
    )
    sum_one_grad, gain_one_grad, shift_one_grad = norm_one_back(hidden_one_grad)
    attention_grad = sum_one_grad.astype(jnp.bfloat16)
    output_weight_grad = jnp.einsum(
        "td,te->de", context_flat, attention_grad, preferred_element_type=jnp.float32
    )
    bias_output_grad = jnp.sum(attention_grad.astype(jnp.float32), axis=0)
    context_grad = jnp.einsum(
        "te,de->td", attention_grad, attention_back[3], preferred_element_type=jnp.float32
    ).astype(jnp.bfloat16)
    query_grad, key_grad, value_grad = lax.map(
        attend_back,
        (query_view, key_view, value_view, segment_ids, log_totals, context_grad.reshape(row_view)),
    )
    query_grad = query_grad.reshape(token_count, model_width)
    key_grad = key_grad.reshape(token_count, model_width)
    value_grad = value_grad.reshape(token_count, model_width)
    grad_stack = jnp.stack([query_grad, key_grad, value_grad])
    projection_grad = jnp.einsum(
        "td,kte->kde", flat_rows, grad_stack, preferred_element_type=jnp.float32
    )
    projection_grad = projection_grad * jnp.array([0.125, 1.0, 1.0], jnp.float32)[:, None, None]
    attention_weight_grad = jnp.concatenate([projection_grad, output_weight_grad[None]], axis=0)
    bias_query_grad = 0.125 * jnp.sum(query_grad.astype(jnp.float32), axis=0)
    bias_value_grad = jnp.sum(value_grad.astype(jnp.float32), axis=0)
    token_grad = sum_one_grad + 0.125 * jnp.einsum(
        "te,de->td", query_grad, attention_back[0], preferred_element_type=jnp.float32
    )
    token_grad = token_grad + jnp.einsum(
        "kte,kde->td", grad_stack[1:], attention_back[1:3], preferred_element_type=jnp.float32
    )
    input_grad = token_grad.reshape(row_view)
    vector_grad = jnp.concatenate(
        [
            jnp.stack(
                [bias_query_grad, bias_value_grad, bias_output_grad, gain_one_grad, shift_one_grad]
            ),
            bias_inner_grad.reshape(4, model_width),
            jnp.stack([bias_outer_grad, gain_two_grad, shift_two_grad]),
        ],
        axis=0,
    )
    shard_grads = (
        lax.psum_scatter(
            attention_weight_grad.astype(jnp.bfloat16), "fsdp", scatter_dimension=1, tiled=True
        ).astype(jnp.float32),
        lax.psum_scatter(
            inner_weight_grad.astype(jnp.bfloat16), "fsdp", scatter_dimension=0, tiled=True
        ).astype(jnp.float32),
        lax.psum_scatter(
            outer_weight_grad.astype(jnp.bfloat16), "fsdp", scatter_dimension=0, tiled=True
        ).astype(jnp.float32),
        lax.psum_scatter(
            vector_grad.astype(jnp.bfloat16), "fsdp", scatter_dimension=1, tiled=True
        ).astype(jnp.float32),
    )
    summed = (
        lax.psum(shard_grads[0].astype(jnp.bfloat16), "dp").astype(jnp.float32),
        lax.psum(shard_grads[1].astype(jnp.bfloat16), "dp").astype(jnp.float32),
        lax.psum(shard_grads[2].astype(jnp.bfloat16), "dp").astype(jnp.float32),
        lax.psum(shard_grads[3].astype(jnp.bfloat16), "dp").astype(jnp.float32),
    )
    local_squares = (
        jnp.sum(summed[0] * summed[0])
        + jnp.sum(summed[1] * summed[1])
        + jnp.sum(summed[2] * summed[2])
        + jnp.sum(summed[3] * summed[3])
    )
    total_squares = lax.psum(local_squares, "fsdp")
    grad_norm = jnp.sqrt(total_squares)
    factor = CLIP / (grad_norm + 1e-06)
    attention_new, attention_first_new, attention_second_new = adam_update(
        attention_weight, attention_first, attention_second, summed[0], factor, RATE_MATRIX
    )
    inner_new, inner_first_new, inner_second_new = adam_update(
        inner_weight, inner_first, inner_second, summed[1], factor, RATE_MATRIX
    )
    outer_new, outer_first_new, outer_second_new = adam_update(
        outer_weight, outer_first, outer_second, summed[2], factor, RATE_MATRIX
    )
    vectors_new, vector_first_new, vector_second_new = adam_update(
        vectors, vector_first, vector_second, summed[3], factor, RATE_VECTOR
    )
    clipped_vectors = summed[3] * factor
    return (
        activations,
        input_grad,
        grad_norm,
        attention_new,
        attention_first_new,
        attention_second_new,
        inner_new,
        inner_first_new,
        inner_second_new,
        outer_new,
        outer_first_new,
        outer_second_new,
        vectors_new,
        vector_first_new,
        vector_second_new,
        clipped_vectors,
    )


def fused_body(
    tokens,
    segment_ids,
    cotangent,
    attention_weight,
    attention_first,
    attention_second,
    inner_weight,
    inner_first,
    inner_second,
    outer_weight,
    outer_first,
    outer_second,
    vectors,
    vector_first,
    vector_second,
):
    _, seq_length, model_width = tokens.shape
    activations, input_grad, total, vec_grad, norm = whole_layer(
        tokens.reshape(seq_length, model_width),
        cotangent.reshape(seq_length, model_width),
        segment_ids,
        attention_weight,
        inner_weight,
        outer_weight,
        vectors,
        ORDER,
        ALPHA_GATHER,
        ALPHA_SCATTER,
    )
    found = adam_step(
        activations,
        input_grad,
        norm,
        vec_grad,
        total,
        (attention_weight, attention_first, attention_second),
        (inner_weight, inner_first, inner_second),
        (outer_weight, outer_first, outer_second),
        (vectors, vector_first, vector_second),
    )
    return (found[0][None], found[1][None], found[2].reshape(()), *found[3:])


def solution(mesh):
    placed = (
        P(("dp", "fsdp"), None, None),
        P(("dp", "fsdp"), None),
        P(("dp", "fsdp"), None, None),
        P(None, "fsdp", None),
        P(None, "fsdp", None),
        P(None, "fsdp", None),
        P("fsdp", None),
        P("fsdp", None),
        P("fsdp", None),
        P("fsdp", None),
        P("fsdp", None),
        P("fsdp", None),
        P(None, "fsdp"),
        P(None, "fsdp"),
        P(None, "fsdp"),
    )
    fused = mesh.shape["dp"] == 4 and mesh.shape["fsdp"] == 8
    return jax.shard_map(
        fused_body if fused else plain_body,
        mesh=mesh,
        in_specs=placed,
        out_specs=(
            P(("dp", "fsdp"), None, None),
            P(("dp", "fsdp"), None, None),
            P(),
            P(None, "fsdp", None),
            P(None, "fsdp", None),
            P(None, "fsdp", None),
            P("fsdp", None),
            P("fsdp", None),
            P("fsdp", None),
            P("fsdp", None),
            P("fsdp", None),
            P("fsdp", None),
            P(None, "fsdp"),
            P(None, "fsdp"),
            P(None, "fsdp"),
            P(None, "fsdp"),
        ),
        check_vma=False,
    )
```
